32 devices in a mesh: seq: 8 (over y, x, core), head: 4 (over z).
Axes of the slice: x: 2, y: 2, z: 4, core: 2. Of those that a mesh axis runs over, the one named last changes fastest.
Arguments:
- hidden: bfloat16 [2, 8192, 768], P(None, ('seq', 'head')), may hold values from -6 to 6
- out_grad: bfloat16 [2, 8192, 768], P(None, ('seq', 'head')), may hold values from -6 to 6
- norm_gain: float32 [768], replicated, may hold values from 0.1 to 1.9
- input_projection_weight: bfloat16 [768, 3352], P(('seq', 'head')), may hold values from -0.21875 to 0.21875
- conv_weight: float32 [4, 1792], replicated, may hold values from -3 to 3
- conv_bias: float32 [1792], replicated, may hold values from -3 to 3
- step_bias: float32 [24], replicated, may hold values from -3 to 0
- decay_log: float32 [24], replicated
- skip_weight: float32 [24], replicated, may hold values from 0.5 to 1.5
- gate_gain: float32 [1536], replicated, may hold values from 0.1 to 1.9
- output_projection_weight: bfloat16 [768, 1536], P(('seq', 'head')), may hold values from -0.15625 to 0.15625
Outputs:
- mixed: bfloat16 [2, 8192, 768], P(None, ('seq', 'head'))
- hidden_grad: float32 [2, 8192, 768], P(None, ('seq', 'head'))
- norm_gain_grad: float32 [768], replicated
- in_weight_grad: float32 [768, 3352], P(('seq', 'head'))
- conv_weight_grad: float32 [4, 1792], replicated
- conv_bias_grad: float32 [1792], replicated
- step_bias_grad: float32 [24], replicated
- decay_log_grad: float32 [24], replicated
- skip_weight_grad: float32 [24], replicated
- gate_gain_grad: float32 [1536], replicated
- out_weight_grad: float32 [768, 1536], P(('seq', 'head'))
The draws below stay inside these ranges and needn't reach their ends.
All inputs are finite; a program needn't handle non-finite values.
Results may differ from the reference program's by a relative error of at most 0.014.
The reference program's roundings to bfloat16 on the way count: a program that leaves them out, or rounds other values in their place, can miss the bound.
Values may be sent and summed in bfloat16 or wider, within the bound.
No kernel may reach another device: no remote copies, remote signals or barrier semaphores. Data moves between devices by JAX's collectives and lax.ppermute only.
A program may use at most 192 MiB of HBM per device.

```python
import math
from functools import partial
import jax
import jax.numpy as jnp
from jax import lax

D = 768
H = 24
P_SIZE = 64
N = 128
KERNEL = 4
CH = 256
DI = 1536
PROJ = 3352
CONV = 1792
SEQS = 2
LENGTH = 8192
N_HEAD = 4


def draw_decay_log(key, part):
    key = jax.random.fold_in(key, 11)
    pick_key, fast_key, slow_key = jax.random.split(key, 3)
    fast_share = 0.5
    fast_heads = jax.random.uniform(pick_key, (H,), jnp.float32) < fast_share
    fast_rate = jnp.exp(jax.random.uniform(fast_key, (H,), jnp.float32, math.log(0.03), math.log(0.2)))
    slow_rate = jnp.exp(jax.random.uniform(slow_key, (H,), jnp.float32, math.log(0.3), math.log(3.0))) / LENGTH
    return jnp.log(jnp.where(fast_heads, fast_rate, slow_rate)).astype(jnp.float32)


def shard_levels(rng, dims, pieces, smallest, top_value):
    gain = 1.0
    for axis_at, parts in pieces:
        draws = jax.random.uniform(jax.random.fold_in(jax.random.fold_in(rng, 6), axis_at), (parts,), jnp.float32, smallest / len(pieces), top_value / len(pieces))
        gain = gain * jnp.repeat(jnp.exp(draws), dims[axis_at] // parts).reshape((-1,) + (1,) * (len(dims) - 1 - axis_at))
    return gain


def scatter_about(key, extent, width, bound, cuts=(), dtype=jnp.bfloat16):
    drawn = width * jax.random.normal(key, extent, jnp.float32)
    if cuts:
        drawn = drawn * shard_levels(key, extent, cuts, -0.22, 0.18)
    return jnp.clip(drawn, -bound, bound).astype(dtype)


def setup_inputs(seed: int = 0) -> dict:
    streams_of = jax.random.split(jax.random.key(seed), 12)
    hidden = scatter_about(streams_of[0], (SEQS, LENGTH, D), 1.0, 6.0, ((1, 32),))
    out_grad = scatter_about(streams_of[1], (SEQS, LENGTH, D), 1.0, 6.0, ((1, 32),))
    norm_gain = jnp.clip(1.0 + 0.18 * jax.random.normal(streams_of[2], (D,), jnp.float32), 0.1, 1.9)
    input_projection_weight = scatter_about(streams_of[3], (D, PROJ), D ** -0.5, 0.21875, ((0, 32),))
    conv_weight = scatter_about(streams_of[4], (KERNEL, CONV), KERNEL ** -0.5, 3.0, (), jnp.float32)
    conv_bias = scatter_about(streams_of[5], (CONV,), 0.5, 3.0, (), jnp.float32)
    step_bias = jnp.clip(jax.random.uniform(streams_of[6], (H,), jnp.float32, -3.0, 0.0), -3.0, 0.0)
    decay_log = draw_decay_log(jax.random.fold_in(streams_of[11], 71), 0)
    skip_weight = jnp.clip(jax.random.uniform(streams_of[8], (H,), jnp.float32, 0.5, 1.5), 0.5, 1.5)
    gate_gain = jnp.clip(1.0 + 0.18 * jax.random.normal(streams_of[9], (DI,), jnp.float32), 0.1, 1.9)
    output_projection_weight = scatter_about(streams_of[10], (D, DI), DI ** -0.5, 0.15625, ((0, 32),))
    return dict(hidden=hidden, out_grad=out_grad, norm_gain=norm_gain, input_projection_weight=input_projection_weight, conv_weight=conv_weight, conv_bias=conv_bias, step_bias=step_bias, decay_log=decay_log, skip_weight=skip_weight, gate_gain=gate_gain, output_projection_weight=output_projection_weight)


FULL_ACCURACY = lax.Precision.HIGHEST
EPSILON = 1e-05

@jax.custom_vjp
def low(v):
    return lax.optimization_barrier(v.astype(jnp.bfloat16)).astype(jnp.float32)

@jax.custom_vjp
def lowered_backward_result(v):
    return v

def low_keep(v):
    return (low(v), None)

def low_pass(kept, grad):
    return (grad,)

def back_keep(v):
    return (v, None)

def back_low(kept, grad):
    return (low(grad),)
low.defvjp(low_keep, low_pass)
lowered_backward_result.defvjp(back_keep, back_low)

def causal_conv(values, kernel, offset):
    positions = values.shape[-2]
    padding = [(0, 0)] * (values.ndim - 2) + [(KERNEL - 1, 0), (0, 0)]
    padded = jnp.pad(values, padding)
    summed = offset + jnp.zeros_like(values)
    for kernel_tap in range(KERNEL):
        summed = summed + kernel[kernel_tap] * lax.slice_in_dim(padded, kernel_tap, kernel_tap + positions, axis=values.ndim - 2)
    return summed

def block_step(decay_rate, carry_state, block_in):
    inputs, step_sizes, keys_in, queries_in = block_in
    cumulative = jnp.cumsum(step_sizes * decay_rate, axis=1)
    final_cum = cumulative[:, -1]
    scores = jnp.einsum('gstn,gsun->stug', queries_in, keys_in, precision=FULL_ACCURACY)
    spread = cumulative[:, :, None] - cumulative[:, None, :]
    lower_mask = jnp.arange(CH)[:, None] >= jnp.arange(CH)[None, :]
    decay_mask = jnp.where(lower_mask[None, :, :, None, None], jnp.exp(jnp.minimum(spread, 0.0)), 0.0)
    mixing = low(scores[..., None] * decay_mask * step_sizes[:, None])
    within = jnp.einsum('stugj,sugjp->stgjp', mixing, inputs, precision=FULL_ACCURACY)
    weights = jnp.exp(final_cum[:, None] - cumulative) * step_sizes
    weighted = low(inputs * weights[..., None])
    local_state = jnp.einsum('sqgjp,gsqn->sgjpn', weighted, keys_in, precision=FULL_ACCURACY)
    carried = jnp.einsum('gstn,sgjpn->stgjp', queries_in, carry_state, precision=FULL_ACCURACY) * jnp.exp(cumulative)[..., None]
    new_state = jnp.exp(final_cum)[..., None, None] * carry_state + local_state
    return (new_state, within + carried)

def layer(hidden, norm_gain, input_projection_weight, conv_weight, conv_bias, step_bias, decay_log, skip_weight, gate_gain, output_projection_weight):
    groups = N_HEAD
    per_group = H // groups
    scale_one = lax.rsqrt(lax.optimization_barrier(jnp.mean(hidden * hidden, axis=-1, keepdims=True)) + EPSILON)
    normalized_rows = low(hidden * scale_one * norm_gain)
    projected_features = lowered_backward_result(jnp.einsum('qob,bf->qof', normalized_rows, input_projection_weight, precision=FULL_ACCURACY))
    gate_in = projected_features[..., :DI]
    remainder = low(projected_features[..., DI:])
    x_pre = lowered_backward_result(remainder[..., :DI])
    bc_pre = remainder[..., DI:DI + 2 * N]
    step_raw = lowered_backward_result(remainder[..., DI + 2 * N:])
    bc_groups = lowered_backward_result(jnp.broadcast_to(bc_pre[None], (groups,) + bc_pre.shape))
    x_conv = low(jax.nn.silu(causal_conv(x_pre, conv_weight[:, :DI], conv_bias[:DI])))
    bc_conv = low(jax.nn.silu(causal_conv(bc_groups, conv_weight[:, DI:], conv_bias[DI:])))
    step_sizes = jax.nn.softplus(step_raw + step_bias)
    decay_rate = (-jnp.exp(decay_log)).reshape(groups, per_group)
    block_total = LENGTH // CH
    inputs = x_conv.reshape(SEQS, block_total, CH, groups, per_group, P_SIZE)
    step_blocks = step_sizes.reshape(SEQS, block_total, CH, groups, per_group)
    key_blocks = bc_conv[..., :N].reshape(groups, SEQS, block_total, CH, N)
    query_blocks = bc_conv[..., N:].reshape(groups, SEQS, block_total, CH, N)
    blocks = (jnp.moveaxis(inputs, 1, 0), jnp.moveaxis(step_blocks, 1, 0), jnp.moveaxis(key_blocks, 2, 0), jnp.moveaxis(query_blocks, 2, 0))
    initial = jnp.zeros((SEQS, groups, per_group, P_SIZE, N), jnp.float32)
    final_state, outputs = lax.scan(jax.checkpoint(partial(block_step, decay_rate)), initial, blocks)
    mixed_heads = jnp.moveaxis(outputs, 0, 1).reshape(SEQS, LENGTH, groups, per_group, P_SIZE)
    mixed_heads = mixed_heads + skip_weight.reshape(groups, per_group)[..., None] * x_conv.reshape(SEQS, LENGTH, groups, per_group, P_SIZE)
    mixed_heads = low(lowered_backward_result(mixed_heads.reshape(SEQS, LENGTH, DI)))
    gated_values = mixed_heads * jax.nn.silu(gate_in)
    scale_two = lax.rsqrt(lax.optimization_barrier(jnp.mean(gated_values * gated_values, axis=-1, keepdims=True)) + EPSILON)
    mixer_input_rows = low(gated_values * scale_two * gate_gain)
    branch_output = jnp.einsum('eyz,rz->eyr', mixer_input_rows, output_projection_weight, precision=FULL_ACCURACY)
    return hidden + branch_output

def reference(hidden, out_grad, norm_gain, input_projection_weight, conv_weight, conv_bias, step_bias, decay_log, skip_weight, gate_gain, output_projection_weight):
    result, pull_back = jax.vjp(layer, hidden.astype(jnp.float32), norm_gain, input_projection_weight.astype(jnp.float32), conv_weight, conv_bias, step_bias, decay_log, skip_weight, gate_gain, output_projection_weight.astype(jnp.float32))
    gradients = pull_back(out_grad.astype(jnp.float32))
    return (result.astype(jnp.bfloat16), gradients[0], gradients[1], gradients[2], gradients[3], gradients[4], gradients[5], gradients[6], gradients[7], gradients[8], gradients[9])
```

```python
import jax
import jax.numpy as jnp
from jax import lax
from jax.experimental import pallas as pl
from jax.experimental.pallas import tpu as pltpu
from jax.sharding import PartitionSpec as P

D = 768
H = 24
P_SIZE = 64
N = 128
KERNEL = 4
CH = 256
DI = H * P_SIZE
CONV = DI + 2 * N
STEP_AT = CONV
WIDE = CONV + 128
STATE = DI + 128
HALO = 16
EPSILON = 1e-05
BF = jnp.bfloat16
F32 = jnp.float32
BOTH = ("seq", "head")
PARAMS = pltpu.CompilerParams(vmem_limit_bytes=56 * 1024 * 1024)


def dot(a, b, contract=(1, 0)):
    return lax.dot_general(
        a, b, (((contract[0],), (contract[1],)), ((), ())), preferred_element_type=F32
    )


def halves(v):
    high = v.astype(BF)
    return high, (v - high.astype(F32)).astype(BF)


def head_map(rows, period=None):
    row = lax.broadcasted_iota(jnp.int32, (rows, DI), 0)
    col = lax.broadcasted_iota(jnp.int32, (rows, DI), 1)
    if period is not None:
        row = jnp.bitwise_and(row, period - 1)
    return (row == jnp.right_shift(col, 6)).astype(F32).astype(BF)


def spread_heads(v, heads):
    high, low = halves(v)
    return dot(high, heads) + dot(low, heads)


def sum_heads(v, heads):
    high, low = halves(v)
    return dot(high, heads, (1, 1)) + dot(low, heads, (1, 1))


def sigmoid(v):
    return 1.0 / (1.0 + jnp.exp(-v))


def softplus(v):
    return jnp.maximum(v, 0.0) + jnp.log1p(jnp.exp(-jnp.abs(v)))


def triangle(flip):
    row = lax.broadcasted_iota(jnp.int32, (CH, CH), 0)
    col = lax.broadcasted_iota(jnp.int32, (CH, CH), 1)
    return row <= col if flip else row >= col


def last_lanes(last):
    high = last.astype(BF).astype(F32)
    rest = last - high
    mid = rest.astype(BF).astype(F32)
    low = rest - mid
    return high + pltpu.roll(mid, 32, 1) + pltpu.roll(low, 64, 1)


def before_scan(
    hid, halo, gain, weight, taps, offset, bias, rate,
    normed_out, normed_halo_out, ext_out, pre_out, conv_out, cum_out, cumt_out,
    step_out, arg_out, state_out, ext32,
):
    def norm(v):
        v = v.astype(F32)
        scale = lax.rsqrt(jnp.mean(v * v, axis=-1, keepdims=True) + EPSILON)
        return (v * scale * gain[...]).astype(BF)

    rows = norm(hid[0])
    rows_halo = norm(halo[0])
    normed_out[0] = rows
    normed_halo_out[0] = rows_halo
    projected = dot(rows, weight[...])
    projected_halo = dot(rows_halo, weight[:, :CONV])
    low = projected[:, :CONV].astype(BF)
    low_halo = projected_halo.astype(BF)
    ext_out[0, :HALO] = low_halo
    ext_out[0, HALO:] = low
    ext32[:HALO] = low_halo.astype(F32)
    ext32[HALO:] = low.astype(F32)
    for at in range(0, CONV, 128):
        cols = slice(at, at + 128)
        pre = offset[:, cols] + taps[0:1, cols] * ext32[HALO - 3 : HALO - 3 + CH, cols]
        for k in range(1, KERNEL):
            pre = pre + taps[k : k + 1, cols] * ext32[HALO - 3 + k : HALO - 3 + k + CH, cols]
        pre_out[0, :, cols] = pre
        conv_out[0, :, cols] = (pre * sigmoid(pre)).astype(BF)
    arg = projected[:, STEP_AT:].astype(BF).astype(F32) + bias[...]
    step = softplus(arg)
    cum = jnp.dot(
        triangle(False).astype(F32),
        step * rate[...],
        precision=lax.Precision.HIGHEST,
        preferred_element_type=F32,
    )
    arg_out[0] = arg
    step_out[0] = step
    cum_out[0] = cum
    cumt_out[0] = jnp.transpose(cum)[:32]
    last = cum[CH - 1 : CH]
    heads = head_map(128)
    w = spread_heads(jnp.exp(last - cum) * step, heads)
    weighted = (conv_out[0, :, :DI].astype(F32) * w).astype(BF)
    keys = conv_out[0, :, DI : DI + N]
    state_out[0, :, :DI] = dot(keys, weighted, (0, 0)).astype(BF)
    state_out[0, :, DI:] = jnp.broadcast_to(last_lanes(last), (N, 128)).astype(BF)


def within_block(conv, cum, cumt, stept, y_out):
    keys = conv[0, :, DI : DI + N]
    queries = conv[0, :, DI + N :]
    scores = jnp.where(triangle(False), dot(queries, keys, (1, 1)), 0.0)
    half = CH // 2
    lane = lax.broadcasted_iota(jnp.int32, (half, 128), 1) < P_SIZE
    for pair in range(H // 2):
        cols = slice(pair * 128, pair * 128 + 128)
        for top, width in ((0, half), (half, CH)):
            x = conv[0, :width, cols]
            parts = []
            for h in (2 * pair, 2 * pair + 1):
                spread = cum[0, top : top + half, h : h + 1] - cumt[0, h : h + 1, :width]
                decay = jnp.exp(jnp.minimum(spread, 0.0))
                mixing = scores[top : top + half, :width] * decay * stept[0, h : h + 1, :width]
                parts.append(dot(mixing.astype(BF), x))
            y_out[0, top : top + half, cols] = jnp.where(lane, parts[0], parts[1])


def state_scan(reverse, blocks, rows, parts_in, out, decay):
    heads = head_map(128, 32)
    lane = lax.broadcasted_iota(jnp.int32, (blocks * rows, 128), 1)
    last = parts_in[:, :, DI:].reshape(blocks * rows, 128)
    last = jnp.where(lane < 96, last.astype(F32), 0.0).astype(BF)
    decay[...] = jnp.exp(dot(last, heads)).reshape(blocks, rows, DI)
    carry = jnp.zeros((rows, DI), F32)
    for k in range(blocks - 1, -1, -1) if reverse else range(blocks):
        out[k] = carry.astype(BF)
        carry = decay[k] * carry + parts_in[k, :, :DI].astype(F32)


def around_norm(
    within, conv, cum, start, gate, dmi, gain, skip,
    mixed_in_out, d_gate_out, d_y_out, dot_y_out, state_out, sums_out,
):
    heads = head_map(128)
    x = conv[0, :, :DI].astype(F32)
    queries = conv[0, :, DI + N :]
    cum_here = cum[0]
    e_cum = spread_heads(jnp.exp(cum_here), heads)
    y_scan = within[0] + dot(queries, start[0]) * e_cum
    y = (y_scan + skip[...] * x).astype(BF).astype(F32)
    gate_here = gate[0]
    sig = sigmoid(gate_here)
    act = gate_here * sig
    gated = y * act
    scale = lax.rsqrt(jnp.mean(gated * gated, axis=-1, keepdims=True) + EPSILON)
    unit = gated * scale
    mixed_in_out[0] = (unit * gain[...]).astype(BF)
    d_mixed_in = dmi[0]
    gain_part = jnp.sum(d_mixed_in * unit, axis=0, keepdims=True)
    d_unit = d_mixed_in * gain[...]
    d_gated = scale * (d_unit - unit * jnp.mean(d_unit * unit, axis=-1, keepdims=True))
    d_y_low = (d_gated * act).astype(BF)
    d_y_out[0] = d_y_low
    d_gate_out[0] = (d_gated * y * (sig * (1.0 + gate_here * (1.0 - sig)))).astype(BF)
    d_y = d_y_low.astype(F32)
    dot_y_out[0] = sum_heads(d_y * y_scan, heads)
    skip_part = jnp.sum(d_y * x, axis=0, keepdims=True)
    sums_out[0] = jnp.concatenate([gain_part, skip_part, jnp.zeros((6, DI), F32)], axis=0)
    scaled = (d_y * e_cum).astype(BF)
    state_out[0, :, :DI] = dot(queries, scaled, (0, 0)).astype(BF)
    state_out[0, :, DI:] = jnp.broadcast_to(last_lanes(cum_here[CH - 1 : CH]), (N, 128)).astype(BF)


def within_block_back(
    conv, cum, cumt, step, d_y, start, dx_out, d_keys_out, d_queries_out, scores_grad
):
    keys = conv[0, :, DI : DI + N]
    queries = conv[0, :, DI + N :]
    scores = jnp.where(triangle(True), dot(keys, queries, (1, 1)), 0.0)
    scores_grad[...] = jnp.zeros_like(scores_grad)
    half = CH // 2
    lane = lax.broadcasted_iota(jnp.int32, (half, 128), 1) < P_SIZE
    for pair in range(H // 2):
        cols = slice(pair * 128, pair * 128 + 128)
        for top, left in ((0, 0), (half, half)):
            x = conv[0, top : top + half, cols].astype(F32)
            dy = d_y[0, left:, cols]
            parts = []
            for side, h in enumerate((2 * pair, 2 * pair + 1)):
                spread = cumt[0, h : h + 1, left:] - cum[0, top : top + half, h : h + 1]
                decay = jnp.exp(jnp.minimum(spread, 0.0)) * step[0, top : top + half, h : h + 1]
                mixing = (scores[top : top + half, left:] * decay).astype(BF)
                parts.append(dot(mixing, dy))
                x_one = jnp.where(lane if side == 0 else ~lane, x, 0.0).astype(BF)
                d_mixing = dot(x_one, dy, (1, 1))
                scores_grad[top : top + half, left:] += d_mixing * decay
            dx_out[0, top : top + half, cols] = jnp.where(lane, parts[0], parts[1])
    d_scores = jnp.where(triangle(True), scores_grad[...], 0.0)
    high, low = halves(d_scores)
    d_keys_out[0] = dot(high, queries) + dot(low, queries)
    heads = head_map(128)
    scaled = (d_y[0].astype(F32) * spread_heads(jnp.exp(cum[0]), heads)).astype(BF)
    d_queries_out[0] = (
        dot(high, keys, (0, 0)) + dot(low, keys, (0, 0)) + dot(scaled, start[0], (1, 1))
    )


def after_scan(
    conv, pre, ext, cum, step, arg, d_y, dx_within, d_keys_in, d_queries, dot_y, start, after,
    skip, rate, taps,
    d_proj_out, d_halo_out, conv_sums_out, head_sums_out, d_pre, ext32,
):
    heads = head_map(128)
    x = conv[0, :, :DI].astype(F32)
    keys = conv[0, :, DI : DI + N]
    cum_here = cum[0]
    step_here = step[0]
    last = cum_here[CH - 1 : CH]
    w = spread_heads(jnp.exp(last - cum_here) * step_here, heads)
    weighted = (x * w).astype(BF)
    dx_state = dot(keys, after[0]) * w
    d_keys = d_keys_in[0] + dot(weighted, after[0], (1, 1))
    sum_within = sum_heads(x * dx_within[0], heads)
    sum_state = sum_heads(x * dx_state, heads)
    passing = jnp.sum(start[0].astype(F32) * after[0].astype(F32), axis=0, keepdims=True)
    passing = sum_heads(jnp.broadcast_to(passing, (8, DI)), heads)[0:1]
    d_last = jnp.sum(sum_state, axis=0, keepdims=True) + jnp.exp(last) * passing
    row = lax.broadcasted_iota(jnp.int32, (CH, 128), 0)
    d_cum = dot_y[0] - sum_within - sum_state + jnp.where(row == CH - 1, d_last, 0.0)
    later = jnp.dot(
        triangle(True).astype(F32),
        d_cum,
        precision=lax.Precision.HIGHEST,
        preferred_element_type=F32,
    )
    arg_here = arg[0]
    sig = sigmoid(arg_here)
    ratio = jnp.where(step_here > 1e-30, sig / jnp.maximum(step_here, 1e-30), 1.0)
    d_arg = (sum_within + sum_state) * ratio + rate[...] * later * sig
    bias_part = jnp.sum(d_arg, axis=0, keepdims=True)
    decay_part = rate[...] * jnp.sum(step_here * later, axis=0, keepdims=True)
    head_sums_out[0] = jnp.concatenate([bias_part, decay_part, jnp.zeros((6, 128), F32)], axis=0)

    dx = dx_within[0] + dx_state + skip[...] * d_y[0].astype(F32)
    ext32[...] = ext[0].astype(F32)
    d_pre[:HALO] = jnp.zeros((HALO, CONV), F32)
    d_pre[HALO + CH :] = jnp.zeros((8, CONV), F32)
    for at in range(0, CONV, 128):
        cols = slice(at, at + 128)
        v = pre[0, :, cols]
        s = sigmoid(v)
        slope = s * (1.0 + v * (1.0 - s))
        if at < DI:
            d_out = dx[:, cols]
        else:
            d_out = d_keys if at == DI else d_queries[0]
        d_here = d_out * slope
        d_pre[HALO : HALO + CH, cols] = d_here
        sums = [
            jnp.sum(
                d_here * ext32[HALO - 3 + k : HALO - 3 + k + CH, cols], axis=0, keepdims=True
            )
            for k in range(KERNEL)
        ]
        sums.append(jnp.sum(d_here, axis=0, keepdims=True))
        sums.append(jnp.zeros((3, 128), F32))
        conv_sums_out[0, :, cols] = jnp.concatenate(sums, axis=0)
        d_in = taps[0:1, cols] * d_pre[3 : 3 + HALO + CH, cols]
        for k in range(1, KERNEL):
            d_in = d_in + taps[k : k + 1, cols] * d_pre[3 - k : 3 - k + HALO + CH, cols]
        d_halo_out[0, :, cols] = d_in[:HALO].astype(BF)
        d_proj_out[0, :, cols] = d_in[HALO:].astype(BF)
    d_halo_out[0, :, STEP_AT:] = jnp.zeros((HALO, 128), BF)
    d_proj_out[0, :, STEP_AT:] = d_arg.astype(BF)


def per_sequence(body, ins, outs, scratch=(), name=None):
    seqs = next(v.shape[0] for v in ins if v.ndim == 3)

    def spec(shape):
        if len(shape) == 2:
            return pl.BlockSpec(shape, lambda s: (0, 0))
        return pl.BlockSpec((1,) + tuple(shape[1:]), lambda s: (s, 0, 0))

    return pl.pallas_call(
        body,
        grid=(seqs,),
        in_specs=[spec(v.shape) for v in ins],
        out_specs=[spec(shape) for shape, _ in outs],
        out_shape=[jax.ShapeDtypeStruct(shape, kind) for shape, kind in outs],
        scratch_shapes=list(scratch),
        compiler_params=PARAMS,
        name=name,
    )(*ins)


def scan_states(parts, groups, blocks, reverse):
    seqs = parts.shape[0]
    rows = seqs * N // blocks
    sent = lax.all_to_all(
        parts.reshape(seqs * N, STATE), BOTH, split_axis=0, concat_axis=0, tiled=True,
        axis_index_groups=groups,
    ).reshape(blocks, rows, STATE)
    if rows % 8 == 0:
        out = pl.pallas_call(
            lambda *refs: state_scan(reverse, blocks, rows, *refs),
            out_shape=jax.ShapeDtypeStruct((blocks, rows, DI), BF),
            scratch_shapes=[pltpu.VMEM((blocks, rows, DI), F32)],
            compiler_params=PARAMS,
            name="state_scan",
        )(sent)
    else:
        last = sent[:, :, DI:].astype(F32)
        last = last[..., :H] + last[..., 32 : 32 + H] + last[..., 64 : 64 + H]
        decay = jnp.repeat(jnp.exp(last), P_SIZE, axis=-1)

        def move(carry, at):
            return at[0] * carry + at[1], carry.astype(BF)

        _, out = lax.scan(
            move,
            jnp.zeros((rows, DI), F32),
            (decay, sent[:, :, :DI].astype(F32)),
            reverse=reverse,
        )
    back = lax.all_to_all(
        out.reshape(seqs * N, DI), BOTH, split_axis=0, concat_axis=0, tiled=True,
        axis_index_groups=groups,
    )
    return back.reshape(seqs, N, DI)


def pad_lanes(v, width):
    return jnp.pad(v, [(0, 0)] * (v.ndim - 1) + [(0, width - v.shape[-1])])


def gather_rows(v):
    return lax.all_gather(lax.all_gather(v, "head", axis=0, tiled=True), "seq", axis=0, tiled=True)


def scatter_rows(v):
    part = lax.psum_scatter(v, "seq", scatter_dimension=0, tiled=True)
    part = lax.psum_scatter(part, "head", scatter_dimension=0, tiled=True)
    return lax.optimization_barrier(part).astype(F32)


def on_device(
    hidden,
    out_grad,
    norm_gain,
    input_projection_weight,
    conv_weight,
    conv_bias,
    step_bias,
    decay_log,
    skip_weight,
    gate_gain,
    output_projection_weight,
):
    devices = lax.axis_size("seq") * lax.axis_size("head")
    given_rows = hidden.shape[1]
    near = CH // given_rows
    if near > 1:
        near_groups = [
            [i + j for j in range(near)] for i in range(0, lax.axis_size("head"), near)
        ]

        def to_blocks(v):
            return lax.all_to_all(
                v, "head", split_axis=0, concat_axis=1, tiled=True, axis_index_groups=near_groups
            )

        def from_blocks(v):
            return lax.all_to_all(
                v, "head", split_axis=1, concat_axis=0, tiled=True, axis_index_groups=near_groups
            )

        hidden, out_grad = to_blocks(hidden), to_blocks(out_grad)
    blocks = devices // near
    scan_groups = None
    if near > 1:
        scan_groups = [[d for d in range(devices) if d % near == r] for r in range(near)]
    seqs = hidden.shape[0]
    tokens = seqs * CH
    onward = [(i, i + near) for i in range(devices - near)]
    backward = [(i + near, i) for i in range(devices - near)]

    halo = lax.ppermute(hidden[:, CH - HALO :], BOTH, onward)
    w_gate = gather_rows(input_projection_weight[:, :DI])
    w_scan = gather_rows(pad_lanes(input_projection_weight[:, DI:], WIDE))
    w_out = gather_rows(output_projection_weight)

    gain_one = norm_gain[None]
    gain_two = gate_gain[None]
    taps = jnp.pad(conv_weight, ((0, 4), (0, 0)))
    offset = conv_bias[None]
    bias = pad_lanes(step_bias[None], 128)
    rate = pad_lanes(-jnp.exp(decay_log)[None], 128)
    skip = jnp.repeat(skip_weight, P_SIZE)[None]

    (normed, normed_halo, ext, pre, conv, cum, cumt, step, arg, parts) = per_sequence(
        before_scan,
        [hidden, halo, gain_one, w_scan, taps, offset, bias, rate],
        [
            ((seqs, CH, D), BF),
            ((seqs, HALO, D), BF),
            ((seqs, HALO + CH, CONV), BF),
            ((seqs, CH, CONV), F32),
            ((seqs, CH, CONV), BF),
            ((seqs, CH, 128), F32),
            ((seqs, 32, CH), F32),
            ((seqs, CH, 128), F32),
            ((seqs, CH, 128), F32),
            ((seqs, N, STATE), BF),
        ],
        [pltpu.VMEM((HALO + CH, CONV), F32)],
        name="before_scan",
    )
    starts = scan_states(parts, scan_groups, blocks, False)

    stept = jnp.swapaxes(step, 1, 2)[:, :32]
    (within,) = per_sequence(
        within_block, [conv, cum, cumt, stept], [((seqs, CH, DI), F32)], name="within_block"
    )
    normed_rows = normed.reshape(tokens, D)
    gate = jnp.dot(normed_rows, w_gate, preferred_element_type=F32).reshape(seqs, CH, DI)
    cotangent = out_grad.reshape(tokens, D)
    d_mixed_in = jnp.dot(cotangent, w_out, preferred_element_type=F32).reshape(seqs, CH, DI)

    mixed_in, d_gate, d_y, dot_y, parts_back, row_sums = per_sequence(
        around_norm,
        [within, conv, cum, starts, gate, d_mixed_in, gain_two, skip],
        [
            ((seqs, CH, DI), BF),
            ((seqs, CH, DI), BF),
            ((seqs, CH, DI), BF),
            ((seqs, CH, 128), F32),
            ((seqs, N, STATE), BF),
            ((seqs, 8, DI), F32),
        ],
        name="around_norm",
    )
    afters = scan_states(parts_back, scan_groups, blocks, True)

    mixed_rows = mixed_in.reshape(tokens, DI)
    branch = dot(mixed_rows, w_out, (1, 1)).reshape(seqs, CH, D)
    widened = hidden.astype(F32)
    mixed = (widened + branch).astype(BF)
    d_gate_rows = d_gate.reshape(tokens, DI)
    out_rows = scatter_rows(dot(cotangent, mixed_rows, (0, 0)).astype(BF))
    gate_rows = scatter_rows(dot(normed_rows, d_gate_rows, (0, 0)).astype(BF))

    dx_within, d_keys, d_queries = per_sequence(
        within_block_back,
        [conv, cum, cumt, step, d_y, starts],
        [((seqs, CH, DI), F32), ((seqs, CH, N), F32), ((seqs, CH, N), F32)],
        [pltpu.VMEM((CH, CH), F32)],
        name="within_block_back",
    )
    d_scan, d_halo, conv_sums, head_sums = per_sequence(
        after_scan,
        [
            conv, pre, ext, cum, step, arg, d_y, dx_within, d_keys, d_queries, dot_y, starts,
            afters, skip, rate, taps,
        ],
        [
            ((seqs, CH, WIDE), BF),
            ((seqs, HALO, WIDE), BF),
            ((seqs, 8, CONV), F32),
            ((seqs, 8, 128), F32),
        ],
        [pltpu.VMEM((HALO + CH + 8, CONV), F32), pltpu.VMEM((HALO + CH, CONV), F32)],
        name="after_scan",
    )
    d_scan_rows = d_scan.reshape(tokens, WIDE)
    d_halo_rows = d_halo.reshape(seqs * HALO, WIDE)
    scan_term = dot(normed_rows, d_scan_rows, (0, 0)) + dot(
        normed_halo.reshape(seqs * HALO, D), d_halo_rows, (0, 0)
    )
    scan_rows = scatter_rows(scan_term.astype(BF))

    d_normed_halo = dot(d_halo_rows, w_scan, (1, 1)).reshape(seqs, HALO, D)
    from_next = lax.ppermute(d_normed_halo[:, HALO - 8 :], BOTH, backward)
    d_normed = (dot(d_gate_rows, w_gate, (1, 1)) + dot(d_scan_rows, w_scan, (1, 1))).reshape(
        seqs, CH, D
    )
    d_normed = d_normed + jnp.pad(from_next, ((0, 0), (CH - 8, 0), (0, 0)))
    scale_one = lax.rsqrt(jnp.mean(widened * widened, axis=-1, keepdims=True) + EPSILON)
    unit_one = widened * scale_one
    norm_part = jnp.sum(d_normed * unit_one, axis=(0, 1))
    d_unit_one = d_normed * norm_gain
    hidden_grad = out_grad.astype(F32) + scale_one * (
        d_unit_one - unit_one * jnp.mean(d_unit_one * unit_one, axis=-1, keepdims=True)
    )
    if near > 1:
        mixed, hidden_grad = from_blocks(mixed), from_blocks(hidden_grad)

    row_sums = jnp.sum(row_sums, axis=0)
    conv_sums = jnp.sum(conv_sums, axis=0)
    head_sums = jnp.sum(head_sums, axis=0)
    pieces = (
        norm_part,
        conv_sums[:KERNEL].reshape(-1),
        conv_sums[KERNEL],
        head_sums[0, :H],
        head_sums[1, :H],
        jnp.sum(row_sums[1].reshape(H, P_SIZE), axis=1),
        row_sums[0],
    )
    summed = lax.psum(jnp.concatenate(pieces), BOTH)
    outs, at = [], 0
    for piece in pieces:
        outs.append(summed[at : at + piece.shape[0]])
        at += piece.shape[0]
    in_rows = jnp.concatenate([gate_rows, scan_rows[:, : CONV + H]], axis=1)
    return (
        mixed,
        hidden_grad,
        outs[0],
        in_rows,
        outs[1].reshape(KERNEL, CONV),
        outs[2],
        outs[3],
        outs[4],
        outs[5],
        outs[6],
        out_rows,
    )


def solution(mesh):
    rows = P(None, BOTH, None)
    weight = P(BOTH, None)
    return jax.shard_map(
        on_device,
        mesh=mesh,
        in_specs=(rows, rows, P(), weight, P(), P(), P(), P(), P(), P(), weight),
        out_specs=(rows, rows, P(), weight, P(), P(), P(), P(), P(), P(), weight),
        check_vma=False,
    )
```

```python
from functools import partial

import jax
import jax.numpy as jnp
from jax import lax
from jax.experimental import pallas as pl
from jax.experimental.pallas import tpu as pltpu
from jax.sharding import PartitionSpec as P

D = 768
H = 24
P_SIZE = 64
N = 128
KERNEL = 4
CH = 256
DI = H * P_SIZE
CONV = DI + 2 * N
STEP_AT = CONV
WIDE = CONV + 128
SPLIT = 896
STATE = DI + 128
HALO = 16
EPSILON = 1e-05
BF = jnp.bfloat16
F32 = jnp.float32
BOTH = ("seq", "head")
PARAMS = pltpu.CompilerParams(vmem_limit_bytes=56 * 1024 * 1024)


def dot(a, b, contract=(1, 0)):
    return lax.dot_general(
        a, b, (((contract[0],), (contract[1],)), ((), ())), preferred_element_type=F32
    )


def halves(v):
    high = v.astype(BF)
    return high, (v - high.astype(F32)).astype(BF)


def head_map(rows, period=None):
    row = lax.broadcasted_iota(jnp.int32, (rows, DI), 0)
    col = lax.broadcasted_iota(jnp.int32, (rows, DI), 1)
    if period is not None:
        row = jnp.bitwise_and(row, period - 1)
    return (row == jnp.right_shift(col, 6)).astype(F32).astype(BF)


def spread_heads(v, heads):
    high, low = halves(v)
    return dot(high, heads) + dot(low, heads)


def sum_heads(v, heads):
    high, low = halves(v)
    return dot(high, heads, (1, 1)) + dot(low, heads, (1, 1))


def sigmoid(v):
    return 1.0 / (1.0 + jnp.exp(-v))


def softplus(v):
    return jnp.maximum(v, 0.0) + jnp.log1p(jnp.exp(-jnp.abs(v)))


def triangle(flip):
    row = lax.broadcasted_iota(jnp.int32, (CH, CH), 0)
    col = lax.broadcasted_iota(jnp.int32, (CH, CH), 1)
    return row <= col if flip else row >= col


def last_lanes(last):
    high = last.astype(BF).astype(F32)
    rest = last - high
    mid = rest.astype(BF).astype(F32)
    low = rest - mid
    return high + pltpu.roll(mid, 32, 1) + pltpu.roll(low, 64, 1)


def before_scan(
    plan, me, hid, halo, gain, taps, offset, bias, rate, *refs
):
    pieces = refs[: len(plan)]
    (
        normed_out, normed_halo_out, ext_out, pre_out, conv_out, cum_out, cumt_out,
        step_out, arg_out, state_out, weight_out, ext32, weight, in_sems, out_sem,
    ) = refs[len(plan) :]
    keep_weight = pltpu.make_async_copy(weight, weight_out, out_sem)

    @pl.when(pl.program_id(0) == 0)
    def _():
        copies = []
        for piece, (masks, left) in zip(pieces, plan):
            size, width = piece.shape[0] // len(masks), piece.shape[1]
            for at, mask in enumerate(masks):
                row = pl.multiple_of(jnp.bitwise_xor(me[0], mask) * size, size)
                copies.append(
                    pltpu.make_async_copy(
                        piece.at[pl.ds(at * size, size)],
                        weight.at[pl.ds(row, size), pl.ds(left, width)],
                        in_sems.at[len(copies)],
                    )
                )
        for copy in copies:
            copy.start()
        for copy in copies:
            copy.wait()
        keep_weight.start()

    def norm(v):
        v = v.astype(F32)
        scale = lax.rsqrt(jnp.mean(v * v, axis=-1, keepdims=True) + EPSILON)
        return (v * scale * gain[...]).astype(BF)

    rows = norm(hid[0])
    rows_halo = norm(halo[0])
    normed_out[0] = rows
    normed_halo_out[0] = rows_halo
    projected = dot(rows, weight[...])
    projected_halo = dot(rows_halo, weight[:, :CONV])
    low = projected[:, :CONV].astype(BF)
    low_halo = projected_halo.astype(BF)
    ext_out[0, :HALO] = low_halo
    ext_out[0, HALO:] = low
    ext32[:HALO] = low_halo.astype(F32)
    ext32[HALO:] = low.astype(F32)
    for at in range(0, CONV, 128):
        cols = slice(at, at + 128)
        pre = offset[:, cols] + taps[0:1, cols] * ext32[HALO - 3 : HALO - 3 + CH, cols]
        for k in range(1, KERNEL):
            pre = pre + taps[k : k + 1, cols] * ext32[HALO - 3 + k : HALO - 3 + k + CH, cols]
        pre_out[0, :, cols] = pre
        conv_out[0, :, cols] = (pre * sigmoid(pre)).astype(BF)
    arg = projected[:, STEP_AT:].astype(BF).astype(F32) + bias[...]
    step = softplus(arg)
    cum = jnp.dot(
        triangle(False).astype(F32),
        step * rate[...],
        precision=lax.Precision.HIGHEST,
        preferred_element_type=F32,
    )
    arg_out[0] = arg
    step_out[0] = step
    cum_out[0] = cum
    cumt_out[0] = jnp.transpose(cum)[:32]
    last = cum[CH - 1 : CH]
    heads = head_map(128)
    w = spread_heads(jnp.exp(last - cum) * step, heads)
    weighted = (conv_out[0, :, :DI].astype(F32) * w).astype(BF)
    keys = conv_out[0, :, DI : DI + N]
    state_out[0, :, :DI] = dot(keys, weighted, (0, 0)).astype(BF)
    state_out[0, :, DI:] = jnp.broadcast_to(last_lanes(last), (N, 128)).astype(BF)

    @pl.when(pl.program_id(0) == pl.num_programs(0) - 1)
    def _():
        keep_weight.wait()


def within_block(conv, cum, cumt, stept, y_out):
    keys = conv[0, :, DI : DI + N]
    queries = conv[0, :, DI + N :]
    scores = jnp.where(triangle(False), dot(queries, keys, (1, 1)), 0.0)
    half = CH // 2
    lane = lax.broadcasted_iota(jnp.int32, (half, 128), 1) < P_SIZE
    for pair in range(H // 2):
        cols = slice(pair * 128, pair * 128 + 128)
        for top, width in ((0, half), (half, CH)):
            x = conv[0, :width, cols]
            parts = []
            for h in (2 * pair, 2 * pair + 1):
                spread = cum[0, top : top + half, h : h + 1] - cumt[0, h : h + 1, :width]
                decay = jnp.exp(jnp.minimum(spread, 0.0))
                mixing = scores[top : top + half, :width] * decay * stept[0, h : h + 1, :width]
                parts.append(dot(mixing.astype(BF), x))
            y_out[0, top : top + half, cols] = jnp.where(lane, parts[0], parts[1])


def state_scan(reverse, blocks, rows, parts_in, out, decay):
    heads = head_map(128, 32)
    lane = lax.broadcasted_iota(jnp.int32, (blocks * rows, 128), 1)
    last = parts_in[:, :, DI:].reshape(blocks * rows, 128)
    last = jnp.where(lane < 96, last.astype(F32), 0.0).astype(BF)
    decay[...] = jnp.exp(dot(last, heads)).reshape(blocks, rows, DI)
    carry = jnp.zeros((rows, DI), F32)
    for k in range(blocks - 1, -1, -1) if reverse else range(blocks):
        out[k] = carry.astype(BF)
        carry = decay[k] * carry + parts_in[k, :, :DI].astype(F32)


def around_norm(
    within, conv, cum, start, gate, dmi, gain, skip,
    mixed_in_out, d_gate_out, d_y_out, dot_y_out, state_out, sums_out,
):
    heads = head_map(128)
    x = conv[0, :, :DI].astype(F32)
    queries = conv[0, :, DI + N :]
    cum_here = cum[0]
    e_cum = spread_heads(jnp.exp(cum_here), heads)
    y_scan = within[0] + dot(queries, start[0]) * e_cum
    y = (y_scan + skip[...] * x).astype(BF).astype(F32)
    gate_here = gate[0]
    sig = sigmoid(gate_here)
    act = gate_here * sig
    gated = y * act
    scale = lax.rsqrt(jnp.mean(gated * gated, axis=-1, keepdims=True) + EPSILON)
    unit = gated * scale
    mixed_in_out[0] = (unit * gain[...]).astype(BF)
    d_mixed_in = dmi[0]
    gain_part = jnp.sum(d_mixed_in * unit, axis=0, keepdims=True)
    d_unit = d_mixed_in * gain[...]
    d_gated = scale * (d_unit - unit * jnp.mean(d_unit * unit, axis=-1, keepdims=True))
    d_y_low = (d_gated * act).astype(BF)
    d_y_out[0] = d_y_low
    d_gate_out[0] = (d_gated * y * (sig * (1.0 + gate_here * (1.0 - sig)))).astype(BF)
    d_y = d_y_low.astype(F32)
    dot_y_out[0] = sum_heads(d_y * y_scan, heads)
    skip_part = jnp.sum(d_y * x, axis=0, keepdims=True)
    sums_out[0] = jnp.concatenate([gain_part, skip_part, jnp.zeros((6, DI), F32)], axis=0)
    scaled = (d_y * e_cum).astype(BF)
    state_out[0, :, :DI] = dot(queries, scaled, (0, 0)).astype(BF)
    state_out[0, :, DI:] = jnp.broadcast_to(last_lanes(cum_here[CH - 1 : CH]), (N, 128)).astype(BF)


def within_block_back(
    conv, cum, cumt, step, d_y, start, dx_out, d_keys_out, d_queries_out, scores_grad
):
    keys = conv[0, :, DI : DI + N]
    queries = conv[0, :, DI + N :]
    scores = jnp.where(triangle(True), dot(keys, queries, (1, 1)), 0.0)
    scores_grad[...] = jnp.zeros_like(scores_grad)
    half = CH // 2
    lane = lax.broadcasted_iota(jnp.int32, (half, 128), 1) < P_SIZE
    for pair in range(H // 2):
        cols = slice(pair * 128, pair * 128 + 128)
        for top, left in ((0, 0), (half, half)):
            x = conv[0, top : top + half, cols].astype(F32)
            dy = d_y[0, left:, cols]
            parts = []
            for side, h in enumerate((2 * pair, 2 * pair + 1)):
                spread = cumt[0, h : h + 1, left:] - cum[0, top : top + half, h : h + 1]
                decay = jnp.exp(jnp.minimum(spread, 0.0)) * step[0, top : top + half, h : h + 1]
                mixing = (scores[top : top + half, left:] * decay).astype(BF)
                parts.append(dot(mixing, dy))
                x_one = jnp.where(lane if side == 0 else ~lane, x, 0.0).astype(BF)
                d_mixing = dot(x_one, dy, (1, 1))
                scores_grad[top : top + half, left:] += d_mixing * decay
            dx_out[0, top : top + half, cols] = jnp.where(lane, parts[0], parts[1])
    d_scores = jnp.where(triangle(True), scores_grad[...], 0.0)
    high, low = halves(d_scores)
    d_keys_out[0] = dot(high, queries) + dot(low, queries)
    heads = head_map(128)
    scaled = (d_y[0].astype(F32) * spread_heads(jnp.exp(cum[0]), heads)).astype(BF)
    d_queries_out[0] = (
        dot(high, keys, (0, 0)) + dot(low, keys, (0, 0)) + dot(scaled, start[0], (1, 1))
    )


def after_scan(
    conv, pre, ext, cum, step, arg, d_y, dx_within, d_keys_in, d_queries, dot_y, start, after,
    skip, rate, taps,
    d_proj_out, d_halo_out, conv_sums_out, head_sums_out, d_pre, ext32,
):
    heads = head_map(128)
    x = conv[0, :, :DI].astype(F32)
    keys = conv[0, :, DI : DI + N]
    cum_here = cum[0]
    step_here = step[0]
    last = cum_here[CH - 1 : CH]
    w = spread_heads(jnp.exp(last - cum_here) * step_here, heads)
    weighted = (x * w).astype(BF)
    dx_state = dot(keys, after[0]) * w
    d_keys = d_keys_in[0] + dot(weighted, after[0], (1, 1))
    sum_within = sum_heads(x * dx_within[0], heads)
    sum_state = sum_heads(x * dx_state, heads)
    passing = jnp.sum(start[0].astype(F32) * after[0].astype(F32), axis=0, keepdims=True)
    passing = sum_heads(jnp.broadcast_to(passing, (8, DI)), heads)[0:1]
    d_last = jnp.sum(sum_state, axis=0, keepdims=True) + jnp.exp(last) * passing
    row = lax.broadcasted_iota(jnp.int32, (CH, 128), 0)
    d_cum = dot_y[0] - sum_within - sum_state + jnp.where(row == CH - 1, d_last, 0.0)
    later = jnp.dot(
        triangle(True).astype(F32),
        d_cum,
        precision=lax.Precision.HIGHEST,
        preferred_element_type=F32,
    )
    arg_here = arg[0]
    sig = sigmoid(arg_here)
    ratio = jnp.where(step_here > 1e-30, sig / jnp.maximum(step_here, 1e-30), 1.0)
    d_arg = (sum_within + sum_state) * ratio + rate[...] * later * sig
    bias_part = jnp.sum(d_arg, axis=0, keepdims=True)
    decay_part = rate[...] * jnp.sum(step_here * later, axis=0, keepdims=True)
    head_sums_out[0] = jnp.concatenate([bias_part, decay_part, jnp.zeros((6, 128), F32)], axis=0)

    dx = dx_within[0] + dx_state + skip[...] * d_y[0].astype(F32)
    ext32[...] = ext[0].astype(F32)
    d_pre[:HALO] = jnp.zeros((HALO, CONV), F32)
    d_pre[HALO + CH :] = jnp.zeros((8, CONV), F32)
    for at in range(0, CONV, 128):
        cols = slice(at, at + 128)
        v = pre[0, :, cols]
        s = sigmoid(v)
        slope = s * (1.0 + v * (1.0 - s))
        if at < DI:
            d_out = dx[:, cols]
        else:
            d_out = d_keys if at == DI else d_queries[0]
        d_here = d_out * slope
        d_pre[HALO : HALO + CH, cols] = d_here
        sums = [
            jnp.sum(
                d_here * ext32[HALO - 3 + k : HALO - 3 + k + CH, cols], axis=0, keepdims=True
            )
            for k in range(KERNEL)
        ]
        sums.append(jnp.sum(d_here, axis=0, keepdims=True))
        sums.append(jnp.zeros((3, 128), F32))
        conv_sums_out[0, :, cols] = jnp.concatenate(sums, axis=0)
        d_in = taps[0:1, cols] * d_pre[3 : 3 + HALO + CH, cols]
        for k in range(1, KERNEL):
            d_in = d_in + taps[k : k + 1, cols] * d_pre[3 - k : 3 - k + HALO + CH, cols]
        d_halo_out[0, :, cols] = d_in[:HALO].astype(BF)
        d_proj_out[0, :, cols] = d_in[HALO:].astype(BF)
    d_halo_out[0, :, STEP_AT:] = jnp.zeros((HALO, 128), BF)
    d_proj_out[0, :, STEP_AT:] = d_arg.astype(BF)


def scan_weight_grad(plan, me, rows, rows_halo, grad, grad_halo, *refs):
    outs, (total, sems) = refs[: len(plan)], refs[len(plan) :]
    half = total.shape[1] // 2
    for left in (0, half):
        cols = slice(left, left + half)
        part = dot(rows[...], grad[:, cols], (0, 0))
        part = part + dot(rows_halo[...], grad_halo[:, cols], (0, 0))
        total[:, cols] = part.astype(BF)
    copies = []
    for out, (masks, left) in zip(outs, plan):
        size, width = out.shape[0] // len(masks), out.shape[1]
        for at, mask in enumerate(masks):
            row = pl.multiple_of(jnp.bitwise_xor(me[0], mask) * size, size)
            copies.append(
                pltpu.make_async_copy(
                    total.at[pl.ds(row, size), pl.ds(left, width)],
                    out.at[pl.ds(at * size, size)],
                    sems.at[len(copies)],
                )
            )
    for copy in copies:
        copy.start()
    for copy in copies:
        copy.wait()


def trade(v, axis, mask):
    return lax.ppermute(v, axis, [(i, i ^ mask) for i in range(lax.axis_size(axis))])


def mask_order(bits):
    masks = [0]
    for bit in reversed(bits):
        masks = masks + [bit | m for m in masks]
    return masks


def routes():
    bits = []
    bit = 2
    while bit < lax.axis_size("seq"):
        bits.append(bit)
        bit *= 2
    return bits[::-1], bits


def paired():
    seq, head = lax.axis_size("seq"), lax.axis_size("head")
    return seq & (seq - 1) == 0 and head & (head - 1) == 0 and (D // seq) % 16 == 0


def gather_head(v):
    count, me = lax.axis_size("head"), lax.axis_index("head")
    parts = [v] + [
        lax.ppermute(v, "head", [(i, (i - k) % count) for i in range(count)])
        for k in range(1, count)
    ]
    both = jnp.concatenate(parts + parts, axis=0)
    at = (count - me) * v.shape[0]
    return lax.dynamic_slice_in_dim(both, at, count * v.shape[0], axis=0)


def gather_pieces(v, split):
    mine = gather_head(v)
    pieces, plan = [], []
    for cols, bits, left in (
        (mine[:, :split], routes()[0], 0),
        (mine[:, split:], routes()[1], split),
    ):
        for bit in bits[::-1]:
            cols = jnp.concatenate([cols, trade(cols, "seq", bit)], axis=0)
        masks = mask_order(bits)
        pieces += [cols, trade(cols, "seq", 1)]
        plan += [(masks, left), ([m | 1 for m in masks], left)]
    return pieces, plan


def scatter_plan(split):
    plan = []
    for extra in (0, 1):
        for bits, left in zip(routes(), (0, split)):
            plan.append(([m | extra for m in mask_order(bits)], left))
    return plan


def add(a, b):
    return (a.astype(F32) + b.astype(F32)).astype(BF)


def scatter_pieces(pieces):
    sums = []
    for kept, sent, bits in zip(pieces[:2], pieces[2:], routes()):
        part = add(kept, trade(sent, "seq", 1))
        for bit in bits:
            half = part.shape[0] // 2
            part = add(part[:half], trade(part[half:], "seq", bit))
        sums.append(part)
    part = jnp.concatenate(sums, axis=1)
    count, me = lax.axis_size("head"), lax.axis_index("head")
    size = part.shape[0] // count
    total = lax.dynamic_slice_in_dim(part, me * size, size, axis=0).astype(F32)
    for k in range(1, count):
        away = lax.dynamic_slice_in_dim(part, lax.rem(me + k, count) * size, size, axis=0)
        got = lax.ppermute(away, "head", [(i, (i + k) % count) for i in range(count)])
        total = total + got.astype(F32)
    return total


def sum_all(v):
    for axis in BOTH:
        mask = 1
        while mask < lax.axis_size(axis):
            v = v + trade(v, axis, mask)
            mask *= 2
    return v


def per_sequence(body, ins, outs, scratch=(), loose=(), loose_outs=0, name=None):
    seqs = next(v.shape[0] for v in ins if v.ndim == 3)
    free = pl.BlockSpec(memory_space=pl.ANY)

    def spec(shape):
        if len(shape) == 1:
            return pl.BlockSpec(memory_space=pltpu.SMEM)
        if len(shape) == 2:
            return pl.BlockSpec(shape, lambda s: (0, 0))
        return pl.BlockSpec((1,) + tuple(shape[1:]), lambda s: (s, 0, 0))

    return pl.pallas_call(
        body,
        grid=(seqs,),
        in_specs=[spec(v.shape) for v in ins] + [free] * len(loose),
        out_specs=[spec(shape) for shape, _ in outs[: len(outs) - loose_outs]]
        + [free] * loose_outs,
        out_shape=[jax.ShapeDtypeStruct(shape, kind) for shape, kind in outs],
        scratch_shapes=list(scratch),
        compiler_params=PARAMS,
        name=name,
    )(*ins, *loose)


def scan_states(parts, groups, blocks, reverse):
    seqs = parts.shape[0]
    rows = seqs * N // blocks
    sent = lax.all_to_all(
        parts.reshape(seqs * N, STATE), BOTH, split_axis=0, concat_axis=0, tiled=True,
        axis_index_groups=groups,
    ).reshape(blocks, rows, STATE)
    if rows % 8 == 0:
        out = pl.pallas_call(
            lambda *refs: state_scan(reverse, blocks, rows, *refs),
            out_shape=jax.ShapeDtypeStruct((blocks, rows, DI), BF),
            scratch_shapes=[pltpu.VMEM((blocks, rows, DI), F32)],
            compiler_params=PARAMS,
            name="state_scan",
        )(sent)
    else:
        last = sent[:, :, DI:].astype(F32)
        last = last[..., :H] + last[..., 32 : 32 + H] + last[..., 64 : 64 + H]
        decay = jnp.repeat(jnp.exp(last), P_SIZE, axis=-1)

        def move(carry, at):
            return at[0] * carry + at[1], carry.astype(BF)

        _, out = lax.scan(
            move,
            jnp.zeros((rows, DI), F32),
            (decay, sent[:, :, :DI].astype(F32)),
            reverse=reverse,
        )
    back = lax.all_to_all(
        out.reshape(seqs * N, DI), BOTH, split_axis=0, concat_axis=0, tiled=True,
        axis_index_groups=groups,
    )
    return back.reshape(seqs, N, DI)


def pad_lanes(v, width):
    return jnp.pad(v, [(0, 0)] * (v.ndim - 1) + [(0, width - v.shape[-1])])


def gather_rows(v):
    return lax.all_gather(lax.all_gather(v, "head", axis=0, tiled=True), "seq", axis=0, tiled=True)


def scatter_rows(v):
    part = lax.psum_scatter(v, "seq", scatter_dimension=0, tiled=True)
    part = lax.psum_scatter(part, "head", scatter_dimension=0, tiled=True)
    return lax.optimization_barrier(part).astype(F32)


def on_device(
    hidden,
    out_grad,
    norm_gain,
    input_projection_weight,
    conv_weight,
    conv_bias,
    step_bias,
    decay_log,
    skip_weight,
    gate_gain,
    output_projection_weight,
):
    devices = lax.axis_size("seq") * lax.axis_size("head")
    given_rows = hidden.shape[1]
    near = CH // given_rows
    if near > 1:
        near_groups = [
            [i + j for j in range(near)] for i in range(0, lax.axis_size("head"), near)
        ]

        def to_blocks(v):
            return lax.all_to_all(
                v, "head", split_axis=0, concat_axis=1, tiled=True, axis_index_groups=near_groups
            )

        def from_blocks(v):
            return lax.all_to_all(
                v, "head", split_axis=1, concat_axis=0, tiled=True, axis_index_groups=near_groups
            )

        hidden, out_grad = to_blocks(hidden), to_blocks(out_grad)
    blocks = devices // near
    scan_groups = None
    if near > 1:
        scan_groups = [[d for d in range(devices) if d % near == r] for r in range(near)]
    seqs = hidden.shape[0]
    tokens = seqs * CH
    onward = [(i, i + near) for i in range(devices - near)]
    backward = [(i + near, i) for i in range(devices - near)]

    halo = lax.ppermute(hidden[:, CH - HALO :], BOTH, onward)
    fast = paired()
    me = lax.axis_index("seq").astype(jnp.int32)[None]
    scan_part = pad_lanes(input_projection_weight[:, DI:], WIDE)
    other_part = jnp.concatenate([input_projection_weight[:, :DI], output_projection_weight], 1)
    if fast:
        pieces, plan = gather_pieces(scan_part, SPLIT)
        others = lax.all_gather(gather_head(other_part), "seq", axis=0, tiled=True)
    else:
        pieces, plan = [gather_rows(scan_part)], [([0], 0)]
        me = jnp.zeros_like(me)
        others = gather_rows(other_part)
    w_gate, w_out = others[:, :DI], others[:, DI:]

    gain_one = norm_gain[None]
    gain_two = gate_gain[None]
    taps = jnp.pad(conv_weight, ((0, 4), (0, 0)))
    offset = conv_bias[None]
    bias = pad_lanes(step_bias[None], 128)
    rate = pad_lanes(-jnp.exp(decay_log)[None], 128)
    skip = jnp.repeat(skip_weight, P_SIZE)[None]

    (normed, normed_halo, ext, pre, conv, cum, cumt, step, arg, parts, w_scan) = per_sequence(
        partial(before_scan, plan),
        [me, hidden, halo, gain_one, taps, offset, bias, rate],
        [
            ((seqs, CH, D), BF),
            ((seqs, HALO, D), BF),
            ((seqs, HALO + CH, CONV), BF),
            ((seqs, CH, CONV), F32),
            ((seqs, CH, CONV), BF),
            ((seqs, CH, 128), F32),
            ((seqs, 32, CH), F32),
            ((seqs, CH, 128), F32),
            ((seqs, CH, 128), F32),
            ((seqs, N, STATE), BF),
            ((D, WIDE), BF),
        ],
        [
            pltpu.VMEM((HALO + CH, CONV), F32),
            pltpu.VMEM((D, WIDE), BF),
            pltpu.SemaphoreType.DMA((sum(len(masks) for masks, _ in plan),)),
            pltpu.SemaphoreType.DMA,
        ],
        loose=pieces,
        loose_outs=1,
        name="before_scan",
    )
    starts = scan_states(parts, scan_groups, blocks, False)

    stept = jnp.swapaxes(step, 1, 2)[:, :32]
    (within,) = per_sequence(
        within_block, [conv, cum, cumt, stept], [((seqs, CH, DI), F32)], name="within_block"
    )
    normed_rows = normed.reshape(tokens, D)
    gate = jnp.dot(normed_rows, w_gate, preferred_element_type=F32).reshape(seqs, CH, DI)
    cotangent = out_grad.reshape(tokens, D)
    d_mixed_in = jnp.dot(cotangent, w_out, preferred_element_type=F32).reshape(seqs, CH, DI)

    mixed_in, d_gate, d_y, dot_y, parts_back, row_sums = per_sequence(
        around_norm,
        [within, conv, cum, starts, gate, d_mixed_in, gain_two, skip],
        [
            ((seqs, CH, DI), BF),
            ((seqs, CH, DI), BF),
            ((seqs, CH, DI), BF),
            ((seqs, CH, 128), F32),
            ((seqs, N, STATE), BF),
            ((seqs, 8, DI), F32),
        ],
        name="around_norm",
    )
    afters = scan_states(parts_back, scan_groups, blocks, True)

    mixed_rows = mixed_in.reshape(tokens, DI)
    branch = dot(mixed_rows, w_out, (1, 1)).reshape(seqs, CH, D)
    widened = hidden.astype(F32)
    mixed = (widened + branch).astype(BF)
    d_gate_rows = d_gate.reshape(tokens, DI)
    other_term = jnp.concatenate(
        [
            dot(normed_rows, d_gate_rows, (0, 0)).astype(BF),
            dot(cotangent, mixed_rows, (0, 0)).astype(BF),
        ],
        axis=1,
    )
    other_rows = scatter_rows(other_term)

    dx_within, d_keys, d_queries = per_sequence(
        within_block_back,
        [conv, cum, cumt, step, d_y, starts],
        [((seqs, CH, DI), F32), ((seqs, CH, N), F32), ((seqs, CH, N), F32)],
        [pltpu.VMEM((CH, CH), F32)],
        name="within_block_back",
    )
    d_scan, d_halo, conv_sums, head_sums = per_sequence(
        after_scan,
        [
            conv, pre, ext, cum, step, arg, d_y, dx_within, d_keys, d_queries, dot_y, starts,
            afters, skip, rate, taps,
        ],
        [
            ((seqs, CH, WIDE), BF),
            ((seqs, HALO, WIDE), BF),
            ((seqs, 8, CONV), F32),
            ((seqs, 8, 128), F32),
        ],
        [pltpu.VMEM((HALO + CH + 8, CONV), F32), pltpu.VMEM((HALO + CH, CONV), F32)],
        name="after_scan",
    )
    d_scan_rows = d_scan.reshape(tokens, WIDE)
    d_halo_rows = d_halo.reshape(seqs * HALO, WIDE)
    normed_halo_rows = normed_halo.reshape(seqs * HALO, D)
    plan = scatter_plan(SPLIT) if fast else [([0], 0)]
    terms = pl.pallas_call(
        partial(scan_weight_grad, plan),
        in_specs=[pl.BlockSpec(memory_space=pltpu.SMEM)]
        + [pl.BlockSpec(memory_space=pltpu.VMEM)] * 4,
        out_specs=[pl.BlockSpec(memory_space=pl.ANY)] * len(plan),
        out_shape=[
            jax.ShapeDtypeStruct(
                (
                    D // lax.axis_size("seq") * len(masks) if fast else D,
                    (WIDE - SPLIT if left else SPLIT) if fast else WIDE,
                ),
                BF,
            )
            for masks, left in plan
        ],
        scratch_shapes=[
            pltpu.VMEM((D, WIDE), BF),
            pltpu.SemaphoreType.DMA((sum(len(masks) for masks, _ in plan),)),
        ],
        compiler_params=PARAMS,
        name="scan_weight_grad",
    )(me, normed_rows, normed_halo_rows, d_scan_rows, d_halo_rows)
    scan_rows = scatter_pieces(terms) if fast else scatter_rows(terms[0])

    d_normed_halo = dot(d_halo_rows, w_scan, (1, 1)).reshape(seqs, HALO, D)
    from_next = lax.ppermute(d_normed_halo[:, HALO - 8 :], BOTH, backward)
    d_normed = (dot(d_gate_rows, w_gate, (1, 1)) + dot(d_scan_rows, w_scan, (1, 1))).reshape(
        seqs, CH, D
    )
    d_normed = d_normed + jnp.pad(from_next, ((0, 0), (CH - 8, 0), (0, 0)))
    scale_one = lax.rsqrt(jnp.mean(widened * widened, axis=-1, keepdims=True) + EPSILON)
    unit_one = widened * scale_one
    norm_part = jnp.sum(d_normed * unit_one, axis=(0, 1))
    d_unit_one = d_normed * norm_gain
    hidden_grad = out_grad.astype(F32) + scale_one * (
        d_unit_one - unit_one * jnp.mean(d_unit_one * unit_one, axis=-1, keepdims=True)
    )
    if near > 1:
        mixed, hidden_grad = from_blocks(mixed), from_blocks(hidden_grad)

    row_sums = jnp.sum(row_sums, axis=0)
    conv_sums = jnp.sum(conv_sums, axis=0)
    head_sums = jnp.sum(head_sums, axis=0)
    pieces = (
        norm_part,
        conv_sums[:KERNEL].reshape(-1),
        conv_sums[KERNEL],
        head_sums[0, :H],
        head_sums[1, :H],
        jnp.sum(row_sums[1].reshape(H, P_SIZE), axis=1),
        row_sums[0],
    )
    flat = jnp.concatenate(pieces)
    summed = sum_all(jnp.pad(flat, (0, -flat.shape[0] % 1024))) if fast else lax.psum(flat, BOTH)
    outs, at = [], 0
    for piece in pieces:
        outs.append(summed[at : at + piece.shape[0]])
        at += piece.shape[0]
    in_rows = jnp.concatenate([other_rows[:, :DI], scan_rows[:, : CONV + H]], axis=1)
    return (
        mixed,
        hidden_grad,
        outs[0],
        in_rows,
        outs[1].reshape(KERNEL, CONV),
        outs[2],
        outs[3],
        outs[4],
        outs[5],
        outs[6],
        other_rows[:, DI:],
    )


def solution(mesh):
    rows = P(None, BOTH, None)
    weight = P(BOTH, None)
    return jax.shard_map(
        on_device,
        mesh=mesh,
        in_specs=(rows, rows, P(), weight, P(), P(), P(), P(), P(), P(), weight),
        out_specs=(rows, rows, P(), weight, P(), P(), P(), P(), P(), P(), weight),
        check_vma=False,
    )
```

```python
from functools import partial

import jax
import jax.numpy as jnp
from jax import lax
from jax.experimental import pallas as pl
from jax.experimental.pallas import tpu as pltpu
from jax.sharding import PartitionSpec as P

D = 768
H = 24
P_SIZE = 64
N = 128
KERNEL = 4
CH = 256
DI = H * P_SIZE
CONV = DI + 2 * N
STEP_AT = CONV
WIDE = CONV + 128
STATE = DI + 128
HALO = 16
SMALL = 512
EPSILON = 1e-05
BF = jnp.bfloat16
F32 = jnp.float32
BOTH = ("seq", "head")
PARAMS = pltpu.CompilerParams(vmem_limit_bytes=56 * 1024 * 1024)


def cost(micros):
    return pl.CostEstimate(
        flops=int(micros * 1.1e9), bytes_accessed=int(micros * 3e6), transcendentals=0
    )


def dot(a, b, contract=(1, 0)):
    return lax.dot_general(
        a, b, (((contract[0],), (contract[1],)), ((), ())), preferred_element_type=F32
    )


def halves(v):
    high = v.astype(BF)
    return high, (v - high.astype(F32)).astype(BF)


def head_map(rows, period=None):
    row = lax.broadcasted_iota(jnp.int32, (rows, DI), 0)
    col = lax.broadcasted_iota(jnp.int32, (rows, DI), 1)
    if period is not None:
        row = jnp.bitwise_and(row, period - 1)
    return (row == jnp.right_shift(col, 6)).astype(F32).astype(BF)


def spread_heads(v, heads):
    high, low = halves(v)
    return dot(high, heads) + dot(low, heads)


def sum_heads(v, heads):
    high, low = halves(v)
    return dot(high, heads, (1, 1)) + dot(low, heads, (1, 1))


def sigmoid(v):
    return 1.0 / (1.0 + jnp.exp(-v))


def softplus(v):
    return jnp.maximum(v, 0.0) + jnp.log1p(jnp.exp(-jnp.abs(v)))


def triangle(flip):
    row = lax.broadcasted_iota(jnp.int32, (CH, CH), 0)
    col = lax.broadcasted_iota(jnp.int32, (CH, CH), 1)
    return row <= col if flip else row >= col


def last_lanes(last):
    high = last.astype(BF).astype(F32)
    rest = last - high
    mid = rest.astype(BF).astype(F32)
    low = rest - mid
    return high + pltpu.roll(mid, 32, 1) + pltpu.roll(low, 64, 1)


def store_state(out, state, last):
    out[:, :DI] = state.astype(BF)
    out[:, DI:] = jnp.broadcast_to(last_lanes(last), (N, 128)).astype(BF)


def spread_row(v, heads):
    return spread_heads(jnp.broadcast_to(v, (8, 128)), heads)[0:1]


def block_copies(me, pieces, whole, sems, way, outward=False):
    copies = []
    for at, piece in enumerate(pieces):
        if len(pieces) == 1:
            pairs = [(piece, whole)]
        else:
            seq = jnp.bitwise_xor(me[0], at)
            core = jnp.bitwise_and(seq, 1)
            near = 2 + 2 * core
            count = 8 if way == "core" else 4
            size = piece.shape[0] // count
            pairs = []
            for k in range(count):
                if way == "core":
                    mask = (k & 1) + ((k >> 1) & 1) * near + (k >> 2) * (6 - near)
                    row = (jnp.bitwise_xor(seq, mask) * 2 + core) * size
                else:
                    mask = (k & 1) * 2 + (k >> 1) * 4 if way == "x" else (k & 1) * 4 + (k >> 1) * 2
                    row = jnp.bitwise_xor(seq, mask) * size
                rows = pl.ds(pl.multiple_of(row, size), size)
                pairs.append((piece.at[pl.ds(k * size, size)], whole.at[rows]))
        for block, rows in pairs:
            pair = (rows, block) if outward else (block, rows)
            copies.append(pltpu.make_async_copy(*pair, sems.at[len(copies)]))
    return copies


def start_all(copies):
    for copy in copies:
        copy.start()


def wait_all(copies):
    for copy in copies:
        copy.wait()


def before_scan(
    count, me, hid, halo, gain, taps, offset, bias, rate, *refs
):
    pieces = refs[:count]
    (
        normed_out, normed_halo_out, ext_out, conv_out, cum_out, cumt_out, step_out, stept_out,
        arg_out, local_out, state_out, weight_out,
        ext32, weight, total, total_last, in_sems, out_sem,
    ) = refs[count:]
    keep_weight = pltpu.make_async_copy(weight, weight_out, out_sem)

    @pl.when(pl.program_id(0) == 0)
    def _():
        copies = block_copies(me, pieces, weight, in_sems, "core")
        start_all(copies)
        wait_all(copies)
        keep_weight.start()
        total[...] = jnp.zeros_like(total)
        total_last[...] = jnp.zeros_like(total_last)

    def norm(v):
        v = v.astype(F32)
        scale = lax.rsqrt(jnp.mean(v * v, axis=-1, keepdims=True) + EPSILON)
        return (v * scale * gain[...]).astype(BF)

    rows = norm(hid[...])
    rows_halo = norm(halo[...])
    normed_out[...] = rows
    normed_halo_out[...] = rows_halo
    projected = dot(rows, weight[...])
    projected_halo = dot(rows_halo, weight[:, :CONV])
    low = projected[:, :CONV].astype(BF)
    low_halo = projected_halo.astype(BF)
    ext_out[:HALO] = low_halo
    ext_out[HALO:] = low
    ext32[:HALO] = low_halo.astype(F32)
    ext32[HALO:] = low.astype(F32)
    for at in range(0, CONV, 128):
        cols = slice(at, at + 128)
        pre = offset[:, cols] + taps[0:1, cols] * ext32[HALO - 3 : HALO - 3 + CH, cols]
        for k in range(1, KERNEL):
            pre = pre + taps[k : k + 1, cols] * ext32[HALO - 3 + k : HALO - 3 + k + CH, cols]
        conv_out[:, cols] = (pre * sigmoid(pre)).astype(BF)
    arg = projected[:, STEP_AT:].astype(BF).astype(F32) + bias[...]
    step = softplus(arg)
    cum = jnp.dot(
        triangle(False).astype(F32),
        step * rate[...],
        precision=lax.Precision.HIGHEST,
        preferred_element_type=F32,
    )
    arg_out[...] = arg
    step_out[...] = step
    stept_out[...] = jnp.transpose(step)[:32]
    cum_out[...] = cum
    cumt_out[...] = jnp.transpose(cum)[:32]
    last = cum[CH - 1 : CH]
    heads = head_map(128)
    w = spread_heads(jnp.exp(last - cum) * step, heads)
    weighted = (conv_out[:, :DI].astype(F32) * w).astype(BF)
    local = dot(conv_out[:, DI : DI + N], weighted, (0, 0))
    local_out[...] = local
    total[...] = total[...] * spread_row(jnp.exp(last), heads) + local
    total_last[...] += jnp.broadcast_to(last, total_last.shape)

    @pl.when(pl.program_id(0) == pl.num_programs(0) - 1)
    def _():
        keep_weight.wait()
        store_state(state_out, total[...], total_last[0:1])


def within_block(conv, cum, cumt, stept, y_out):
    keys = conv[:, DI : DI + N]
    queries = conv[:, DI + N :]
    scores = jnp.where(triangle(False), dot(queries, keys, (1, 1)), 0.0)
    half = CH // 2
    lane = lax.broadcasted_iota(jnp.int32, (half, 128), 1) < P_SIZE
    for pair in range(H // 2):
        cols = slice(pair * 128, pair * 128 + 128)
        for top, width in ((0, half), (half, CH)):
            x = conv[:width, cols]
            parts = []
            for h in (2 * pair, 2 * pair + 1):
                spread = cum[top : top + half, h : h + 1] - cumt[h : h + 1, :width]
                decay = jnp.exp(jnp.minimum(spread, 0.0))
                mixing = scores[top : top + half, :width] * decay * stept[h : h + 1, :width]
                parts.append(dot(mixing.astype(BF), x))
            y_out[top : top + half, cols] = jnp.where(lane, parts[0], parts[1])


def state_scan(reverse, blocks, rows, parts_in, out, decay):
    heads = head_map(128, 32)
    lane = lax.broadcasted_iota(jnp.int32, (blocks * rows, 128), 1)
    last = parts_in[:, :, DI:].reshape(blocks * rows, 128)
    last = jnp.where(lane < 96, last.astype(F32), 0.0).astype(BF)
    decay[...] = jnp.exp(dot(last, heads)).reshape(blocks, rows, DI)
    carry = jnp.zeros((rows, DI), F32)
    for k in range(blocks - 1, -1, -1) if reverse else range(blocks):
        out[k] = carry.astype(out.dtype)
        carry = decay[k] * carry + parts_in[k, :, :DI].astype(F32)


def around_norm(
    within, conv, cum, local, incoming, gate, dmi, gain, skip,
    mixed_in_out, d_gate_out, d_y_out, dot_y_out, start_out, local_back_out, state_out, sums_out,
    start, total, total_last,
):
    @pl.when(pl.program_id(0) == 0)
    def _():
        start[...] = incoming[...].astype(F32)
        total[...] = jnp.zeros_like(total)
        total_last[...] = jnp.zeros_like(total_last)
        sums_out[...] = jnp.zeros_like(sums_out)

    start_high, start_low = halves(start[...])
    start_out[...] = start[...]
    heads = head_map(128)
    x = conv[:, :DI].astype(F32)
    queries = conv[:, DI + N :]
    cum_here = cum[...]
    e_cum = spread_heads(jnp.exp(cum_here), heads)
    y_scan = within[...] + (dot(queries, start_high) + dot(queries, start_low)) * e_cum
    y = (y_scan + skip[...] * x).astype(BF).astype(F32)
    gate_here = gate[...]
    sig = sigmoid(gate_here)
    act = gate_here * sig
    gated = y * act
    scale = lax.rsqrt(jnp.mean(gated * gated, axis=-1, keepdims=True) + EPSILON)
    unit = gated * scale
    mixed_in_out[...] = (unit * gain[...]).astype(BF)
    d_mixed_in = dmi[...]
    gain_part = jnp.sum(d_mixed_in * unit, axis=0, keepdims=True)
    d_unit = d_mixed_in * gain[...]
    d_gated = scale * (d_unit - unit * jnp.mean(d_unit * unit, axis=-1, keepdims=True))
    d_y_low = (d_gated * act).astype(BF)
    d_y_out[...] = d_y_low
    d_gate_out[...] = (d_gated * y * (sig * (1.0 + gate_here * (1.0 - sig)))).astype(BF)
    d_y = d_y_low.astype(F32)
    dot_y_out[...] = sum_heads(d_y * y_scan, heads)
    skip_part = jnp.sum(d_y * x, axis=0, keepdims=True)
    sums_out[5:6, :DI] += gain_part
    sums_out[6:7, :128] += sum_heads(jnp.broadcast_to(skip_part, (8, DI)), heads)[0:1]
    scaled, scaled_low = halves(d_y * e_cum)
    local_back = dot(queries, scaled, (0, 0)) + dot(queries, scaled_low, (0, 0))
    local_back_out[...] = local_back.astype(BF)
    last = cum_here[CH - 1 : CH]
    start[...] = start[...] * spread_row(jnp.exp(last), heads) + local[...]
    total[...] += spread_row(jnp.exp(total_last[0:1]), heads) * local_back
    total_last[...] += jnp.broadcast_to(last, total_last.shape)

    @pl.when(pl.program_id(0) == pl.num_programs(0) - 1)
    def _():
        store_state(state_out, total[...], total_last[0:1])


def within_block_back(
    conv, cum, cumt, step, d_y, start, dx_out, d_keys_out, d_queries_out, scores_grad
):
    keys = conv[:, DI : DI + N]
    queries = conv[:, DI + N :]
    scores = jnp.where(triangle(True), dot(keys, queries, (1, 1)), 0.0)
    scores_grad[...] = jnp.zeros_like(scores_grad)
    half = CH // 2
    lane = lax.broadcasted_iota(jnp.int32, (half, 128), 1) < P_SIZE
    for pair in range(H // 2):
        cols = slice(pair * 128, pair * 128 + 128)
        for top, left in ((0, 0), (half, half)):
            x = conv[top : top + half, cols].astype(F32)
            dy = d_y[left:, cols]
            parts = []
            for side, h in enumerate((2 * pair, 2 * pair + 1)):
                spread = cumt[h : h + 1, left:] - cum[top : top + half, h : h + 1]
                decay = jnp.exp(jnp.minimum(spread, 0.0)) * step[top : top + half, h : h + 1]
                mixing = (scores[top : top + half, left:] * decay).astype(BF)
                parts.append(dot(mixing, dy))
                x_one = jnp.where(lane if side == 0 else ~lane, x, 0.0).astype(BF)
                d_mixing = dot(x_one, dy, (1, 1))
                scores_grad[top : top + half, left:] += d_mixing * decay
            dx_out[top : top + half, cols] = jnp.where(lane, parts[0], parts[1])
    d_scores = jnp.where(triangle(True), scores_grad[...], 0.0)
    high, low = halves(d_scores)
    d_keys_out[...] = dot(high, queries) + dot(low, queries)
    scaled, scaled_low = halves(
        d_y[...].astype(F32) * spread_heads(jnp.exp(cum[...]), head_map(128))
    )
    start_high, start_low = halves(start[...])
    d_queries_out[...] = (
        dot(high, keys, (0, 0))
        + dot(low, keys, (0, 0))
        + dot(scaled, start_high, (1, 1))
        + dot(scaled_low, start_high, (1, 1))
        + dot(scaled, start_low, (1, 1))
    )


def after_scan(
    conv, ext, cum, step, arg, d_y, dx_within, d_keys_in, d_queries, dot_y, start, local_back,
    incoming, skip, rate, taps, offset,
    d_proj_out, d_halo_out, sums_out, d_pre, ext32, after,
):
    @pl.when(pl.program_id(0) == 0)
    def _():
        after[...] = incoming[...].astype(F32)
        sums_out[...] = jnp.zeros_like(sums_out)

    after_high = after[...].astype(BF)
    heads = head_map(128)
    x = conv[:, :DI].astype(F32)
    keys = conv[:, DI : DI + N]
    cum_here = cum[...]
    step_here = step[...]
    last = cum_here[CH - 1 : CH]
    w = spread_heads(jnp.exp(last - cum_here) * step_here, heads)
    weighted = (x * w).astype(BF)
    dx_state = dot(keys, after_high) * w
    d_keys = d_keys_in[...] + dot(weighted, after_high, (1, 1))
    sum_within = sum_heads(x * dx_within[...], heads)
    sum_state = sum_heads(x * dx_state, heads)
    passing = jnp.sum(start[...] * after[...], axis=0, keepdims=True)
    passing = sum_heads(jnp.broadcast_to(passing, (8, DI)), heads)[0:1]
    d_last = jnp.sum(sum_state, axis=0, keepdims=True) + jnp.exp(last) * passing
    row = lax.broadcasted_iota(jnp.int32, (CH, 128), 0)
    d_cum = dot_y[...] - sum_within - sum_state + jnp.where(row == CH - 1, d_last, 0.0)
    later = jnp.dot(
        triangle(True).astype(F32),
        d_cum,
        precision=lax.Precision.HIGHEST,
        preferred_element_type=F32,
    )
    sig = sigmoid(arg[...])
    ratio = jnp.where(step_here > 1e-30, sig / jnp.maximum(step_here, 1e-30), 1.0)
    d_arg = (sum_within + sum_state) * ratio + rate[...] * later * sig
    bias_part = jnp.sum(d_arg, axis=0, keepdims=True)
    decay_part = rate[...] * jnp.sum(step_here * later, axis=0, keepdims=True)

    dx = dx_within[...] + dx_state + skip[...] * d_y[...].astype(F32)
    ext32[...] = ext[...].astype(F32)
    d_pre[:HALO] = jnp.zeros((HALO, CONV), F32)
    d_pre[HALO + CH :] = jnp.zeros((8, CONV), F32)
    for at in range(0, CONV, 128):
        cols = slice(at, at + 128)
        shifted = [ext32[HALO - 3 + k : HALO - 3 + k + CH, cols] for k in range(KERNEL)]
        v = offset[:, cols] + taps[0:1, cols] * shifted[0]
        for k in range(1, KERNEL):
            v = v + taps[k : k + 1, cols] * shifted[k]
        s = sigmoid(v)
        slope = s * (1.0 + v * (1.0 - s))
        if at < DI:
            d_out = dx[:, cols]
        else:
            d_out = d_keys if at == DI else d_queries[...]
        d_here = d_out * slope
        d_pre[HALO : HALO + CH, cols] = d_here
        sums = [jnp.sum(d_here * shifted[k], axis=0, keepdims=True) for k in range(KERNEL)]
        sums.append(jnp.sum(d_here, axis=0, keepdims=True))
        if at < DI:
            sums.append(jnp.zeros((1, 128), F32))
        else:
            sums.append(bias_part if at == DI else decay_part)
        sums.append(jnp.zeros((2, 128), F32))
        sums_out[:, cols] += jnp.concatenate(sums, axis=0)
        d_in = taps[0:1, cols] * d_pre[3 : 3 + HALO + CH, cols]
        for k in range(1, KERNEL):
            d_in = d_in + taps[k : k + 1, cols] * d_pre[3 - k : 3 - k + HALO + CH, cols]
        d_halo_out[:, cols] = d_in[:HALO].astype(BF)
        d_proj_out[:, cols] = d_in[HALO:].astype(BF)
    d_halo_out[:, STEP_AT:] = jnp.zeros((HALO, 128), BF)
    d_proj_out[:, STEP_AT:] = d_arg.astype(BF)
    after[...] = after[...] * spread_row(jnp.exp(last), heads) + local_back[...].astype(F32)


def scan_weight_grad(count, me, rows, rows_halo, grad, grad_halo, *refs):
    outs, (total, sems) = refs[:count], refs[count:]
    half = total.shape[1] // 2
    for left in (0, half):
        cols = slice(left, left + half)
        part = dot(rows[...], grad[:, cols], (0, 0))
        part = part + dot(rows_halo[...], grad_halo[:, cols], (0, 0))
        total[:, cols] = part.astype(BF)
    copies = block_copies(me, outs, total, sems, "core", outward=True)
    start_all(copies)
    wait_all(copies)


def other_weight_grad(me, normed, d_gate, cotangent, mixed_in, *refs):
    outs, (total, sems) = refs[:-2], refs[-2:]
    step = pl.program_id(0)

    def keep(part):
        cols = pl.ds(pl.multiple_of(step * part.shape[1], 128), part.shape[1])
        total[:, cols] = part.astype(BF)

    @pl.when(step < 2)
    def _():
        keep(dot(normed[...], d_gate[...], (0, 0)))

    @pl.when(step >= 2)
    def _():
        keep(dot(cotangent[...], mixed_in[...], (0, 0)))

    @pl.when(step == 3)
    def _():
        copies = block_copies(me, outs, total, sems, "core", outward=True)
        start_all(copies)
        wait_all(copies)


def through_others(count, me, normed, cotangent, *refs):
    gates, outs, refs = refs[:count], refs[count : 2 * count], refs[2 * count :]
    gate_out, back_out, w_gate_out, w_out_out, w_gate, w_out, in_sems, out_sems = refs
    step = pl.program_id(0)
    gate_in = block_copies(me, gates, w_gate, in_sems.at[0], "x")
    out_in = block_copies(me, outs, w_out, in_sems.at[1], "y")
    keep_gate = pltpu.make_async_copy(w_gate, w_gate_out, out_sems.at[0])
    keep_out = pltpu.make_async_copy(w_out, w_out_out, out_sems.at[1])

    @pl.when(step == 0)
    def _():
        start_all(gate_in)
        start_all(out_in)
        wait_all(gate_in)
        keep_gate.start()

    @pl.when(step == 2)
    def _():
        wait_all(out_in)
        keep_out.start()

    cols = pl.ds(pl.multiple_of((step % 2) * (DI // 2), 128), DI // 2)

    @pl.when(step < 2)
    def _():
        gate_out[...] = dot(normed[...], w_gate[:, cols])

    @pl.when(step >= 2)
    def _():
        back_out[...] = dot(cotangent[...], w_out[:, cols])

    @pl.when(step == 3)
    def _():
        keep_gate.wait()
        keep_out.wait()


def unit_rows(v):
    v = v.astype(F32)
    scale = lax.rsqrt(jnp.mean(v * v, axis=-1, keepdims=True) + EPSILON)
    return v * scale, scale


def back_to_normed(
    hidden, halo, d_normed_gate, d_scan, d_halo, weight, row_sums, conv_sums,
    out, halo_out, sums_out, total,
):
    @pl.when(pl.program_id(0) == 0)
    def _():
        total[...] = row_sums[...] + conv_sums[...]
        sums_out[...] = jnp.zeros_like(sums_out)

    d_normed = d_normed_gate[...] + dot(d_scan[...], weight[...], (1, 1))
    d_normed_halo = dot(d_halo[...], weight[...], (1, 1))
    out[...] = d_normed
    halo_out[...] = d_normed_halo[HALO - 8 :]
    part = jnp.sum(d_normed * unit_rows(hidden[...])[0], axis=0, keepdims=True)
    part = part + jnp.sum(d_normed_halo * unit_rows(halo[...])[0], axis=0, keepdims=True)
    total[7:8, :D] += part

    @pl.when(pl.program_id(0) == pl.num_programs(0) - 1)
    def _():
        for row in range(8):
            for at in range(0, CONV, SMALL):
                width = min(SMALL, CONV - at)
                out_row = row * 4 + at // SMALL
                sums_out[out_row : out_row + 1, :width] = total[row : row + 1, at : at + width]


def finish(hidden, out_grad, d_normed_in, from_next, gain, grad_out):
    unit, scale = unit_rows(hidden[...])
    tail = jnp.concatenate([jnp.zeros((CH - 8, D), F32), from_next[...]], axis=0)
    d_unit = (d_normed_in[...] + tail) * gain[...]
    grad_out[...] = out_grad[...].astype(F32) + scale * (
        d_unit - unit * jnp.mean(d_unit * unit, axis=-1, keepdims=True)
    )


def tie(*values):
    return lax.optimization_barrier(values)


def trade(v, axis, mask):
    return lax.ppermute(v, axis, [(i, i ^ mask) for i in range(lax.axis_size(axis))])


def trade_near(v, first):
    pairs = [(i, i ^ (2 if (i % 2 == 0) == first else 4)) for i in range(lax.axis_size("seq"))]
    return lax.ppermute(v, "seq", pairs)


def paired():
    seq, head = lax.axis_size("seq"), lax.axis_size("head")
    return seq == 8 and head & (head - 1) == 0 and D % (seq * 32) == 0


def half_rows(v, of):
    size = v.shape[0] // 2
    return lax.dynamic_slice_in_dim(v, of * size, size, axis=0)


def gather_head(v):
    count = lax.axis_size("head")
    return lax.all_to_all(
        jnp.concatenate([v] * count, axis=0), "head", split_axis=0, concat_axis=0, tiled=True
    )


def gather_head_by_turns(v):
    count, me = lax.axis_size("head"), lax.axis_index("head")
    parts = [v] + [
        lax.ppermute(v, "head", [(i, (i - k) % count) for i in range(count)])
        for k in range(1, count)
    ]
    return parts


def in_order(parts):
    count, me = lax.axis_size("head"), lax.axis_index("head")
    both = jnp.concatenate(list(parts) * 2, axis=0)
    size = parts[0].shape[0]
    return lax.dynamic_slice_in_dim(both, (count - me) * size, count * size, axis=0)


def gather_core(mine, later):
    core = lax.rem(lax.axis_index("seq"), 2)
    got = trade(half_rows(mine, 1 - core), "seq", 1)
    part = jnp.concatenate([half_rows(mine, core), got], axis=0)
    got, *later = tie(trade_near(part, True), *later)
    part = jnp.concatenate([part, got], axis=0)
    part = jnp.concatenate([part, trade_near(part, False)], axis=0)
    return [part, trade(part, "seq", 1)], later


def add(a, b):
    return (a.astype(F32) + b.astype(F32)).astype(BF)


def fold(kept, got):
    size = kept.shape[0] // 2
    sent = add(kept[size:], got[size:])
    return add(kept[:size], got[:size]), sent


def join_cores(kept, got):
    core = lax.rem(lax.axis_index("seq"), 2)
    first, second = jnp.where(core == 0, kept, got), jnp.where(core == 0, got, kept)
    return jnp.concatenate([first, second], axis=0)


def scatter_head(part):
    count = lax.axis_size("head")
    got = lax.all_to_all(part, "head", split_axis=0, concat_axis=0, tiled=True)
    got = got.reshape(count, -1, part.shape[1]).astype(F32)
    return jnp.sum(got, axis=0)


def scatter_head_by_turns(part):
    count, me = lax.axis_size("head"), lax.axis_index("head")
    size = part.shape[0] // count
    total = lax.dynamic_slice_in_dim(part, me * size, size, axis=0).astype(F32)
    for k in range(1, count):
        away = lax.dynamic_slice_in_dim(part, lax.rem(me + k, count) * size, size, axis=0)
        got = lax.ppermute(away, "head", [(i, (i + k) % count) for i in range(count)])
        total = total + got.astype(F32)
    return total


def tail(kept, sent, other, other_got, work, rest, trade_rest):
    other = scatter_head_by_turns(join_cores(other, other_got))
    part, sent = fold(kept, trade(sent, "seq", 1))
    d_normed, from_next, small = work(sent)
    small = lax.all_to_all(small, BOTH, split_axis=0, concat_axis=0, tiled=True)
    got, d_normed, from_next, other = tie(trade_near(sent, False), d_normed, from_next, other)
    part, sent = fold(part, got)
    d_normed, from_next, sent = tie(d_normed, from_next, sent)
    grad = rest(d_normed, from_next)
    got, grad, small = tie(trade_near(sent, True), grad, small)
    grad = trade_rest(grad)
    small = jnp.broadcast_to(jnp.sum(small, axis=0, keepdims=True), small.shape)
    small = lax.all_to_all(small, BOTH, split_axis=0, concat_axis=0, tiled=True)
    part, sent = fold(part, got)
    part = join_cores(part, trade(sent, "seq", 1))
    part, small = tie(part, small)
    return scatter_head(part), other, small, grad


def per_block(
    body, ins, outs, scratch=(), loose=(), loose_outs=0, reverse=False, micros=1, name=None
):
    blocks = next(v.shape[0] for v in ins if v.ndim == 3)
    free = pl.BlockSpec(memory_space=pl.ANY)

    def spec(shape):
        if len(shape) == 1:
            return pl.BlockSpec(memory_space=pltpu.SMEM)
        if len(shape) == 2:
            return pl.BlockSpec(shape, lambda s: (0, 0))
        return pl.BlockSpec(
            (None,) + tuple(shape[1:]), lambda s: (blocks - 1 - s if reverse else s, 0, 0)
        )

    return pl.pallas_call(
        body,
        grid=(blocks,),
        in_specs=[spec(v.shape) for v in ins] + [free] * len(loose),
        out_specs=[spec(shape) for shape, _ in outs[: len(outs) - loose_outs]]
        + [free] * loose_outs,
        out_shape=[jax.ShapeDtypeStruct(shape, kind) for shape, kind in outs],
        scratch_shapes=list(scratch),
        compiler_params=PARAMS,
        cost_estimate=cost(micros),
        name=name,
    )(*ins, *loose)


def send_states(part, groups, spans):
    sent = lax.all_to_all(
        part, BOTH, split_axis=0, concat_axis=0, tiled=True, axis_index_groups=groups
    )
    return sent.reshape(spans, N // spans, STATE)


def return_states(sent, groups, spans, reverse):
    rows = N // spans
    if rows % 8 == 0:
        out = pl.pallas_call(
            partial(state_scan, reverse, spans, rows),
            out_shape=jax.ShapeDtypeStruct((spans, rows, DI), F32 if not reverse else BF),
            scratch_shapes=[pltpu.VMEM((spans, rows, DI), F32)],
            compiler_params=PARAMS,
            cost_estimate=cost(2),
            name="state_scan",
        )(sent)
    else:
        last = sent[:, :, DI:].astype(F32)
        last = last[..., :H] + last[..., 32 : 32 + H] + last[..., 64 : 64 + H]
        decay = jnp.repeat(jnp.exp(last), P_SIZE, axis=-1)

        def move(carry, at):
            return at[0] * carry + at[1], carry.astype(BF)

        _, out = lax.scan(
            move,
            jnp.zeros((rows, DI), F32),
            (decay, sent[:, :, :DI].astype(F32)),
            reverse=reverse,
        )
    back = lax.all_to_all(
        out.reshape(N, DI), BOTH, split_axis=0, concat_axis=0, tiled=True,
        axis_index_groups=groups,
    )
    return back


def to_span(v):
    seqs, rows, width = v.shape
    if seqs == 2:
        mine = lax.rem(lax.axis_index("head"), 2)
        got = trade(lax.dynamic_index_in_dim(v, 1 - mine, keepdims=False), "head", 1)

        def join(got):
            keep = lax.dynamic_index_in_dim(v, mine, keepdims=False)
            first, second = jnp.where(mine == 0, keep, got), jnp.where(mine == 0, got, keep)
            return jnp.concatenate([first, second], axis=0).reshape(-1, CH, width)

        return got, join
    groups = [[i + j for j in range(seqs)] for i in range(0, lax.axis_size("head"), seqs)]
    v = lax.all_to_all(
        v, "head", split_axis=0, concat_axis=1, tiled=True, axis_index_groups=groups
    )
    return v, lambda got: got.reshape(-1, CH, width)


def from_span(v, seqs):
    rows = v.shape[0] // seqs
    if seqs == 2:
        mine = lax.rem(lax.axis_index("head"), 2)
        keep = half_rows(v, mine)
        got = trade(half_rows(v, 1 - mine).astype(BF), "head", 1).astype(v.dtype)
        return jnp.stack([jnp.where(mine == 0, keep, got), jnp.where(mine == 0, got, keep)])
    groups = [[i + j for j in range(seqs)] for i in range(0, lax.axis_size("head"), seqs)]
    v = v.reshape(1, seqs * rows, v.shape[-1])
    return lax.all_to_all(
        v, "head", split_axis=1, concat_axis=0, tiled=True, axis_index_groups=groups
    )


def pad_lanes(v, width):
    return jnp.pad(v, [(0, 0)] * (v.ndim - 1) + [(0, width - v.shape[-1])])


def gather_rows(v):
    return lax.all_gather(lax.all_gather(v, "head", axis=0, tiled=True), "seq", axis=0, tiled=True)


def scatter_rows(v):
    part = lax.psum_scatter(v, "seq", scatter_dimension=0, tiled=True)
    part = lax.psum_scatter(part, "head", scatter_dimension=0, tiled=True)
    return lax.optimization_barrier(part).astype(F32)


def on_device(
    hidden,
    out_grad,
    norm_gain,
    input_projection_weight,
    conv_weight,
    conv_bias,
    step_bias,
    decay_log,
    skip_weight,
    gate_gain,
    output_projection_weight,
):
    devices = lax.axis_size("seq") * lax.axis_size("head")
    seqs = hidden.shape[0]
    spans = devices // seqs
    groups = [[d for d in range(devices) if d % seqs == r] for r in range(seqs)]
    onward = [(i, i + seqs) for i in range(devices - seqs)]
    backward = [(i + seqs, i) for i in range(devices - seqs)]
    tokens = seqs * hidden.shape[1]
    blocks = tokens // CH

    def with_halo(v):
        tails = v[:, CH - HALO :]
        return jnp.concatenate([lax.ppermute(tails[-1:], BOTH, onward), tails[:-1]], axis=0)

    fast = paired()
    me = lax.axis_index("seq").astype(jnp.int32)[None]
    scan_part = pad_lanes(input_projection_weight[:, DI:], WIDE)
    other_part = jnp.concatenate([input_projection_weight[:, :DI], output_projection_weight], 1)
    hidden, join_hidden = to_span(hidden)
    if fast:
        pieces, (hidden, other_part) = gather_core(
            gather_head(scan_part), (hidden, other_part)
        )
        conv_bias, *turns = tie(conv_bias, *gather_head_by_turns(other_part))
        other_mine = in_order(turns)
        w_gate, w_out = other_mine[:, :DI], other_mine[:, DI:]
        gate_got, out_got = trade(w_gate, "seq", 2), trade(w_out, "seq", 4)
    else:
        pieces = [gather_rows(scan_part)]
        others = gather_rows(other_part)
        w_gate, w_out = others[:, :DI], others[:, DI:]
    hidden = join_hidden(hidden)
    halo = with_halo(hidden)
    out_grad, join_out_grad = to_span(out_grad)
    copies = 16 if fast else 1

    gain_one = norm_gain[None]
    gain_two = gate_gain[None]
    taps = jnp.pad(conv_weight, ((0, 4), (0, 0)))
    offset = conv_bias[None]
    bias = pad_lanes(step_bias[None], 128)
    rate = pad_lanes(-jnp.exp(decay_log)[None], 128)
    skip = jnp.repeat(skip_weight, P_SIZE)[None]

    (
        normed, normed_halo, ext, conv, cum, cumt, step, stept, arg, local, part, w_scan,
    ) = per_block(
        partial(before_scan, len(pieces)),
        [me, hidden, halo, gain_one, taps, offset, bias, rate],
        [
            ((blocks, CH, D), BF),
            ((blocks, HALO, D), BF),
            ((blocks, HALO + CH, CONV), BF),
            ((blocks, CH, CONV), BF),
            ((blocks, CH, 128), F32),
            ((blocks, 32, CH), F32),
            ((blocks, CH, 128), F32),
            ((blocks, 32, CH), F32),
            ((blocks, CH, 128), F32),
            ((blocks, N, DI), F32),
            ((N, STATE), BF),
            ((D, WIDE), BF),
        ],
        [
            pltpu.VMEM((HALO + CH, CONV), F32),
            pltpu.VMEM((D, WIDE), BF),
            pltpu.VMEM((N, DI), F32),
            pltpu.VMEM((8, 128), F32),
            pltpu.SemaphoreType.DMA((copies,)),
            pltpu.SemaphoreType.DMA,
        ],
        loose=pieces,
        loose_outs=1,
        micros=12, name="before_scan",
    )
    if fast:
        cumt, gate_got, out_got = tie(cumt, gate_got, out_got)
        w_gate = jnp.concatenate([w_gate, gate_got], axis=0)
        w_out = jnp.concatenate([w_out, out_got], axis=0)
        ways = (trade(w_gate, "seq", 4), trade(w_out, "seq", 2))
    else:
        ways = ()
    (within,) = per_block(
        within_block, [conv, cum, cumt, stept], [((blocks, CH, DI), F32)],
        micros=5, name="within_block",
    )
    sent, within, out_grad, ways = tie(send_states(part, groups, spans), within, out_grad, ways)
    if fast:
        w_gate = jnp.concatenate([w_gate, ways[0]], axis=0)
        w_out = jnp.concatenate([w_out, ways[1]], axis=0)
        gates, outs = [w_gate, trade(w_gate, "seq", 1)], [w_out, trade(w_out, "seq", 1)]
    else:
        gates, outs = [w_gate], [w_out]
    incoming = return_states(sent, groups, spans, False)

    normed_rows = normed.reshape(tokens, D)
    out_grad = join_out_grad(out_grad)
    cotangent = out_grad.reshape(tokens, D)
    gate, d_mixed_in, w_gate, w_out = pl.pallas_call(
        partial(through_others, len(gates)),
        grid=(4,),
        in_specs=[
            pl.BlockSpec(memory_space=pltpu.SMEM),
            pl.BlockSpec((tokens, D), lambda j: (0, 0)),
            pl.BlockSpec((tokens, D), lambda j: (0, 0)),
        ]
        + [pl.BlockSpec(memory_space=pl.ANY)] * (2 * len(gates)),
        out_specs=[
            pl.BlockSpec((tokens, DI // 2), lambda j: (0, jnp.minimum(j, 1))),
            pl.BlockSpec((tokens, DI // 2), lambda j: (0, jnp.maximum(j - 2, 0))),
            pl.BlockSpec(memory_space=pl.ANY),
            pl.BlockSpec(memory_space=pl.ANY),
        ],
        out_shape=[jax.ShapeDtypeStruct((tokens, DI), F32)] * 2
        + [jax.ShapeDtypeStruct((D, DI), BF)] * 2,
        scratch_shapes=[
            pltpu.VMEM((D, DI), BF),
            pltpu.VMEM((D, DI), BF),
            pltpu.SemaphoreType.DMA((2, 8 if fast else 1)),
            pltpu.SemaphoreType.DMA((2,)),
        ],
        compiler_params=PARAMS,
        cost_estimate=cost(8),
        name="through_others",
    )(me, normed_rows, cotangent, *gates, *outs)
    gate, d_mixed_in = gate.reshape(blocks, CH, DI), d_mixed_in.reshape(blocks, CH, DI)

    mixed_in, d_gate, d_y, dot_y, starts, local_back, part, row_sums = per_block(
        around_norm,
        [within, conv, cum, local, incoming, gate, d_mixed_in, gain_two, skip],
        [
            ((blocks, CH, DI), BF),
            ((blocks, CH, DI), BF),
            ((blocks, CH, DI), BF),
            ((blocks, CH, 128), F32),
            ((blocks, N, DI), F32),
            ((blocks, N, DI), BF),
            ((N, STATE), BF),
            ((8, CONV), F32),
        ],
        [pltpu.VMEM((N, DI), F32), pltpu.VMEM((N, DI), F32), pltpu.VMEM((8, 128), F32)],
        micros=13, name="around_norm",
    )

    mixed_rows = mixed_in.reshape(tokens, DI)
    d_gate_rows = d_gate.reshape(tokens, DI)
    other_terms = pl.pallas_call(
        other_weight_grad,
        grid=(4,),
        in_specs=[
            pl.BlockSpec(memory_space=pltpu.SMEM),
            pl.BlockSpec((tokens, D), lambda j: (0, 0)),
            pl.BlockSpec((tokens, DI // 2), lambda j: (0, jnp.minimum(j, 1))),
            pl.BlockSpec((tokens, D), lambda j: (0, 0)),
            pl.BlockSpec((tokens, DI // 2), lambda j: (0, jnp.maximum(j - 2, 0))),
        ],
        out_specs=[pl.BlockSpec(memory_space=pl.ANY)] * len(pieces),
        out_shape=[jax.ShapeDtypeStruct((D // len(pieces), 2 * DI), BF)] * len(pieces),
        scratch_shapes=[pltpu.VMEM((D, 2 * DI), BF), pltpu.SemaphoreType.DMA((copies,))],
        compiler_params=PARAMS,
        cost_estimate=cost(8),
        name="other_weight_grad",
    )(me, normed_rows, d_gate_rows, cotangent, mixed_rows)
    sent, other_terms, mixed_rows, d_gate_rows, d_y = tie(
        send_states(part, groups, spans), other_terms, mixed_rows, d_gate_rows, d_y
    )
    incoming = return_states(sent, groups, spans, True)
    branch = dot(mixed_rows, w_out, (1, 1))
    mixed = (hidden.reshape(tokens, D).astype(F32) + branch).astype(BF)
    d_normed_gate = dot(d_gate_rows, w_gate, (1, 1)).reshape(blocks, CH, D)
    if fast:
        other, other_sent = fold(other_terms[0], trade(other_terms[1], "seq", 1))
    else:
        other = other_terms[0]

    dx_within, d_keys, d_queries = per_block(
        within_block_back,
        [conv, cum, cumt, step, d_y, starts],
        [((blocks, CH, DI), F32), ((blocks, CH, N), F32), ((blocks, CH, N), F32)],
        [pltpu.VMEM((CH, CH), F32)],
        micros=9, name="within_block_back",
    )
    if fast:
        got = trade_near(other_sent, False)
    d_scan, d_halo, conv_sums = per_block(
        after_scan,
        [
            conv, ext, cum, step, arg, d_y, dx_within, d_keys, d_queries, dot_y, starts,
            local_back, incoming, skip, rate, taps, offset,
        ],
        [
            ((blocks, CH, WIDE), BF),
            ((blocks, HALO, WIDE), BF),
            ((8, CONV), F32),
        ],
        [
            pltpu.VMEM((HALO + CH + 8, CONV), F32),
            pltpu.VMEM((HALO + CH, CONV), F32),
            pltpu.VMEM((N, DI), F32),
        ],
        reverse=True,
        micros=20, name="after_scan",
    )

    if fast:
        d_scan, got = tie(d_scan, got)
        other, other_sent = fold(other, got)
        other, other_sent = fold(other, trade_near(other_sent, True))
        other_got = trade(other_sent, "seq", 1)
    mixed, d_scan = tie(from_span(mixed, seqs), d_scan)
    terms = pl.pallas_call(
        partial(scan_weight_grad, len(pieces)),
        in_specs=[pl.BlockSpec(memory_space=pltpu.SMEM)]
        + [pl.BlockSpec(memory_space=pltpu.VMEM)] * 4,
        out_specs=[pl.BlockSpec(memory_space=pl.ANY)] * len(pieces),
        out_shape=[jax.ShapeDtypeStruct((D // len(pieces), WIDE), BF)] * len(pieces),
        scratch_shapes=[pltpu.VMEM((D, WIDE), BF), pltpu.SemaphoreType.DMA((copies,))],
        compiler_params=PARAMS,
        cost_estimate=cost(6),
        name="scan_weight_grad",
    )(
        me,
        normed_rows,
        normed_halo.reshape(blocks * HALO, D),
        d_scan.reshape(tokens, WIDE),
        d_halo.reshape(blocks * HALO, WIDE),
    )

    def to_normed(go):
        d_scan_now = tie(d_scan, go)[0]
        d_normed, d_normed_halo, small = per_block(
            back_to_normed,
            [hidden, halo, d_normed_gate, d_scan_now, d_halo, w_scan, row_sums, conv_sums],
            [((blocks, CH, D), F32), ((blocks, 8, D), F32), ((32, SMALL), F32)],
            [pltpu.VMEM((8, CONV), F32)],
            micros=7, name="back_to_normed",
        )
        from_next = lax.ppermute(d_normed_halo[:1], BOTH, backward)
        return d_normed, jnp.concatenate([d_normed_halo[1:], from_next], axis=0), small

    def to_hidden(d_normed, from_next):
        return per_block(
            finish,
            [hidden, out_grad, d_normed, from_next, gain_one],
            [((blocks, CH, D), F32)],
            micros=3, name="finish",
        )[0].reshape(tokens, D)

    def grad_back(grad):
        return from_span(grad, seqs)

    if fast:
        scan_rows, other_rows, small, hidden_grad = tail(
            *terms, other, other_got, to_normed, to_hidden, grad_back
        )
    else:
        d_normed, from_next, small = to_normed(jnp.zeros((8, 128), F32))
        other_rows = scatter_rows(other)
        scan_rows = scatter_rows(terms[0])
        small = lax.psum(small, BOTH)
        hidden_grad = grad_back(to_hidden(d_normed, from_next))
    small = small.reshape(8, 4 * SMALL)[:, :CONV]
    in_rows = jnp.concatenate([other_rows[:, :DI], scan_rows[:, : CONV + H]], axis=1)
    return (
        mixed,
        hidden_grad,
        small[7, :D],
        in_rows,
        small[:KERNEL],
        small[4],
        small[5, DI : DI + H],
        small[5, DI + 128 : DI + 128 + H],
        small[6, :H],
        small[5, :DI],
        other_rows[:, DI:],
    )


def solution(mesh):
    rows = P(None, BOTH, None)
    weight = P(BOTH, None)
    return jax.shard_map(
        on_device,
        mesh=mesh,
        in_specs=(rows, rows, P(), weight, P(), P(), P(), P(), P(), P(), weight),
        out_specs=(rows, rows, P(), weight, P(), P(), P(), P(), P(), P(), weight),
        check_vma=False,
    )
```

```python
from functools import partial

import jax
import jax.numpy as jnp
from jax import lax
from jax.experimental import pallas as pl
from jax.experimental.pallas import tpu as pltpu
from jax.sharding import PartitionSpec as P

D = 768
H = 24
P_SIZE = 64
N = 128
KERNEL = 4
CH = 256
DI = H * P_SIZE
CONV = DI + 2 * N
STEP_AT = CONV
WIDE = CONV + 128
STATE = DI + 128
HALO = 16
EPSILON = 1e-05
BF = jnp.bfloat16
F32 = jnp.float32
BOTH = ("seq", "head")
PARAMS = pltpu.CompilerParams(vmem_limit_bytes=56 * 1024 * 1024)


def cost(micros):
    return pl.CostEstimate(
        flops=int(micros * 1.1e9), bytes_accessed=int(micros * 3e6), transcendentals=0
    )


def dot(a, b, contract=(1, 0)):
    return lax.dot_general(
        a, b, (((contract[0],), (contract[1],)), ((), ())), preferred_element_type=F32
    )


def halves(v):
    high = v.astype(BF)
    return high, (v - high.astype(F32)).astype(BF)


def head_map(rows, period=None):
    row = lax.broadcasted_iota(jnp.int32, (rows, DI), 0)
    col = lax.broadcasted_iota(jnp.int32, (rows, DI), 1)
    if period is not None:
        row = jnp.bitwise_and(row, period - 1)
    return (row == jnp.right_shift(col, 6)).astype(F32).astype(BF)


def spread_heads(v, heads):
    high, low = halves(v)
    return dot(high, heads) + dot(low, heads)


def sum_heads(v, heads):
    high, low = halves(v)
    return dot(high, heads, (1, 1)) + dot(low, heads, (1, 1))


def sigmoid(v):
    return 0.5 * jnp.tanh(0.5 * v) + 0.5


def softplus(v):
    return jnp.maximum(v, 0.0) + jnp.log1p(jnp.exp(-jnp.abs(v)))


def cumulate(v, flip):
    ones = triangle(flip).astype(F32).astype(BF)
    high, rest = halves(v)
    low = (v - high.astype(F32) - rest.astype(F32)).astype(BF)
    return dot(ones, high) + dot(ones, rest) + dot(ones, low)


def triangle(flip):
    row = lax.broadcasted_iota(jnp.int32, (CH, CH), 0)
    col = lax.broadcasted_iota(jnp.int32, (CH, CH), 1)
    return row <= col if flip else row >= col


def last_lanes(last):
    high = last.astype(BF).astype(F32)
    rest = last - high
    mid = rest.astype(BF).astype(F32)
    low = rest - mid
    return high + pltpu.roll(mid, 32, 1) + pltpu.roll(low, 64, 1)


def store_state(out, state, last):
    out[:, :DI] = state.astype(BF)
    out[:, DI:] = jnp.broadcast_to(last_lanes(last), (N, 128)).astype(BF)


def spread_row(v, heads):
    return spread_heads(jnp.broadcast_to(v, (8, 128)), heads)[0:1]


def block_copies(me, pieces, whole, sems, way, outward=False):
    copies = []
    for at, piece in enumerate(pieces):
        if len(pieces) == 1:
            pairs = [(piece, whole)]
        else:
            seq = jnp.bitwise_xor(me[0], at)
            core = jnp.bitwise_and(seq, 1)
            near = 2 + 2 * core
            count = 8 if way == "core" else 4
            size = piece.shape[0] // count
            pairs = []
            for k in range(count):
                if way == "core":
                    mask = (k & 1) + ((k >> 1) & 1) * near + (k >> 2) * (6 - near)
                    row = (jnp.bitwise_xor(seq, mask) * 2 + core) * size
                else:
                    mask = (k & 1) * 2 + (k >> 1) * 4 if way == "x" else (k & 1) * 4 + (k >> 1) * 2
                    row = jnp.bitwise_xor(seq, mask) * size
                rows = pl.ds(pl.multiple_of(row, size), size)
                pairs.append((piece.at[pl.ds(k * size, size)], whole.at[rows]))
        for block, rows in pairs:
            pair = (rows, block) if outward else (block, rows)
            copies.append(pltpu.make_async_copy(*pair, sems.at[len(copies)]))
    return copies


def start_all(copies):
    for copy in copies:
        copy.start()


def wait_all(copies):
    for copy in copies:
        copy.wait()


def before_scan(
    count, me, hid, halo, gain, taps, offset, bias, rate, *refs
):
    pieces = refs[:count]
    (
        normed_out, normed_halo_out, ext_out, slope_out, conv_out, cum_out, cumt_out, step_out, stept_out,
        arg_out, local_out, state_out, weight_out,
        ext32, weight, total, total_last, in_sems, out_sem,
    ) = refs[count:]
    keep_weight = pltpu.make_async_copy(weight, weight_out, out_sem)

    @pl.when(pl.program_id(0) == 0)
    def _():
        copies = block_copies(me, pieces, weight, in_sems, "core")
        start_all(copies)
        wait_all(copies)
        keep_weight.start()
        total[...] = jnp.zeros_like(total)
        total_last[...] = jnp.zeros_like(total_last)

    def norm(v):
        v = v.astype(F32)
        scale = lax.rsqrt(jnp.mean(v * v, axis=-1, keepdims=True) + EPSILON)
        return (v * scale * gain[...]).astype(BF)

    rows = norm(hid[...])
    rows_halo = norm(halo[...])
    normed_out[...] = rows
    normed_halo_out[...] = rows_halo
    projected = dot(rows, weight[...])
    projected_halo = dot(rows_halo, weight[:, :CONV])
    low = projected[:, :CONV].astype(BF)
    low_halo = projected_halo.astype(BF)
    ext_out[:HALO] = low_halo
    ext_out[HALO:] = low
    ext32[:HALO] = low_halo.astype(F32)
    ext32[HALO:] = low.astype(F32)
    for at in range(0, CONV, 128):
        cols = slice(at, at + 128)
        pre = offset[:, cols] + taps[0:1, cols] * ext32[HALO - 3 : HALO - 3 + CH, cols]
        for k in range(1, KERNEL):
            pre = pre + taps[k : k + 1, cols] * ext32[HALO - 3 + k : HALO - 3 + k + CH, cols]
        sig = sigmoid(pre)
        act = pre * sig
        conv_out[:, cols] = act.astype(BF)
        slope_out[:, cols] = (sig + act * (1.0 - sig)).astype(BF)
    arg = projected[:, STEP_AT:].astype(BF).astype(F32) + bias[...]
    step = softplus(arg)
    cum = cumulate(step * rate[...], False)
    arg_out[...] = arg
    step_out[...] = step
    stept_out[...] = jnp.transpose(step)[:32]
    cum_out[...] = cum
    cumt_out[...] = jnp.transpose(cum)[:32]
    last = cum[CH - 1 : CH]
    heads = head_map(128)
    w = spread_heads(jnp.exp(last - cum) * step, heads)
    weighted = (conv_out[:, :DI].astype(F32) * w).astype(BF)
    local = dot(conv_out[:, DI : DI + N], weighted, (0, 0))
    local_out[...] = local
    total[...] = total[...] * spread_row(jnp.exp(last), heads) + local
    total_last[...] += jnp.broadcast_to(last, total_last.shape)

    @pl.when(pl.program_id(0) == pl.num_programs(0) - 1)
    def _():
        keep_weight.wait()
        store_state(state_out, total[...], total_last[0:1])


def within_block(conv, cum, cumt, stept, y_out):
    keys = conv[:, DI : DI + N]
    queries = conv[:, DI + N :]
    scores = jnp.where(triangle(False), dot(queries, keys, (1, 1)), 0.0)
    half = CH // 2
    lane = lax.broadcasted_iota(jnp.int32, (half, 128), 1) < P_SIZE
    for pair in range(H // 2):
        cols = slice(pair * 128, pair * 128 + 128)
        for top, width in ((0, half), (half, CH)):
            x = conv[:width, cols]
            parts = []
            for h in (2 * pair, 2 * pair + 1):
                spread = cum[top : top + half, h : h + 1] - cumt[h : h + 1, :width]
                decay = jnp.exp(jnp.minimum(spread, 0.0))
                mixing = scores[top : top + half, :width] * decay * stept[h : h + 1, :width]
                parts.append(dot(mixing.astype(BF), x))
            y_out[top : top + half, cols] = jnp.where(lane, parts[0], parts[1])


def state_scan(reverse, blocks, rows, parts_in, out, decay):
    heads = head_map(128, 32)
    lane = lax.broadcasted_iota(jnp.int32, (blocks * rows, 128), 1)
    last = parts_in[:, :, DI:].reshape(blocks * rows, 128)
    last = jnp.where(lane < 96, last.astype(F32), 0.0).astype(BF)
    decay[...] = jnp.exp(dot(last, heads)).reshape(blocks, rows, DI)
    carry = jnp.zeros((rows, DI), F32)
    for k in range(blocks - 1, -1, -1) if reverse else range(blocks):
        out[k] = carry.astype(out.dtype)
        carry = decay[k] * carry + parts_in[k, :, :DI].astype(F32)


def around_norm(
    within, conv, cum, local, incoming, gate, dmi, gain, skip,
    mixed_in_out, d_gate_out, d_y_out, dot_y_out, start_out, local_back_out, state_out, sums_out,
    start, total, total_last,
):
    @pl.when(pl.program_id(0) == 0)
    def _():
        start[...] = incoming[...].astype(F32)
        total[...] = jnp.zeros_like(total)
        total_last[...] = jnp.zeros_like(total_last)
        sums_out[...] = jnp.zeros_like(sums_out)

    start_high, start_low = halves(start[...])
    start_out[...] = start[...]
    heads = head_map(128)
    x = conv[:, :DI].astype(F32)
    queries = conv[:, DI + N :]
    cum_here = cum[...]
    e_cum = spread_heads(jnp.exp(cum_here), heads)
    y_scan = within[...] + (dot(queries, start_high) + dot(queries, start_low)) * e_cum
    y = (y_scan + skip[...] * x).astype(BF).astype(F32)
    gate_here = gate[...]
    sig = sigmoid(gate_here)
    act = gate_here * sig
    gated = y * act
    scale = lax.rsqrt(jnp.mean(gated * gated, axis=-1, keepdims=True) + EPSILON)
    unit = gated * scale
    mixed_in_out[...] = (unit * gain[...]).astype(BF)
    d_mixed_in = dmi[...]
    gain_part = jnp.sum(d_mixed_in * unit, axis=0, keepdims=True)
    d_unit = d_mixed_in * gain[...]
    d_gated = scale * (d_unit - unit * jnp.mean(d_unit * unit, axis=-1, keepdims=True))
    d_y_low = (d_gated * act).astype(BF)
    d_y_out[...] = d_y_low
    d_gate_out[...] = (d_gated * y * (sig * (1.0 + gate_here * (1.0 - sig)))).astype(BF)
    d_y = d_y_low.astype(F32)
    dot_y_out[...] = sum_heads(d_y * y_scan, heads)
    skip_part = jnp.sum(d_y * x, axis=0, keepdims=True)
    sums_out[5:6, :DI] += gain_part
    sums_out[6:7, :128] += sum_heads(jnp.broadcast_to(skip_part, (8, DI)), heads)[0:1]
    scaled, scaled_low = halves(d_y * e_cum)
    local_back = dot(queries, scaled, (0, 0)) + dot(queries, scaled_low, (0, 0))
    local_back_out[...] = local_back.astype(BF)
    last = cum_here[CH - 1 : CH]
    start[...] = start[...] * spread_row(jnp.exp(last), heads) + local[...]
    total[...] += spread_row(jnp.exp(total_last[0:1]), heads) * local_back
    total_last[...] += jnp.broadcast_to(last, total_last.shape)

    @pl.when(pl.program_id(0) == pl.num_programs(0) - 1)
    def _():
        store_state(state_out, total[...], total_last[0:1])


def within_block_back(
    conv, cum, cumt, step, d_y, start, dx_out, d_keys_out, d_queries_out, scores_grad
):
    keys = conv[:, DI : DI + N]
    queries = conv[:, DI + N :]
    scores = jnp.where(triangle(True), dot(keys, queries, (1, 1)), 0.0)
    scores_grad[...] = jnp.zeros_like(scores_grad)
    half = CH // 2
    lane = lax.broadcasted_iota(jnp.int32, (half, 128), 1) < P_SIZE
    for pair in range(H // 2):
        cols = slice(pair * 128, pair * 128 + 128)
        for top, left in ((0, 0), (half, half)):
            x = conv[top : top + half, cols].astype(F32)
            dy = d_y[left:, cols]
            parts = []
            for side, h in enumerate((2 * pair, 2 * pair + 1)):
                spread = cumt[h : h + 1, left:] - cum[top : top + half, h : h + 1]
                decay = jnp.exp(jnp.minimum(spread, 0.0)) * step[top : top + half, h : h + 1]
                mixing = (scores[top : top + half, left:] * decay).astype(BF)
                parts.append(dot(mixing, dy))
                x_one = jnp.where(lane if side == 0 else ~lane, x, 0.0).astype(BF)
                d_mixing = dot(x_one, dy, (1, 1))
                scores_grad[top : top + half, left:] += d_mixing * decay
            dx_out[top : top + half, cols] = jnp.where(lane, parts[0], parts[1])
    d_scores = jnp.where(triangle(True), scores_grad[...], 0.0)
    high, low = halves(d_scores)
    d_keys_out[...] = dot(high, queries) + dot(low, queries)
    scaled, scaled_low = halves(
        d_y[...].astype(F32) * spread_heads(jnp.exp(cum[...]), head_map(128))
    )
    start_high, start_low = halves(start[...])
    d_queries_out[...] = (
        dot(high, keys, (0, 0))
        + dot(low, keys, (0, 0))
        + dot(scaled, start_high, (1, 1))
        + dot(scaled_low, start_high, (1, 1))
        + dot(scaled, start_low, (1, 1))
    )


def after_scan(
    conv, slope, ext, cum, step, arg, d_y, dx_within, d_keys_in, d_queries, dot_y, start, local_back,
    incoming, skip, rate, taps,
    d_proj_out, d_halo_out, sums_out, d_pre, after,
):
    @pl.when(pl.program_id(0) == 0)
    def _():
        after[...] = incoming[...].astype(F32)
        sums_out[...] = jnp.zeros_like(sums_out)

    after_high = after[...].astype(BF)
    heads = head_map(128)
    x = conv[:, :DI].astype(F32)
    keys = conv[:, DI : DI + N]
    cum_here = cum[...]
    step_here = step[...]
    last = cum_here[CH - 1 : CH]
    w = spread_heads(jnp.exp(last - cum_here) * step_here, heads)
    weighted = (x * w).astype(BF)
    dx_state = dot(keys, after_high) * w
    d_keys = d_keys_in[...] + dot(weighted, after_high, (1, 1))
    dx_scan = dx_within[...] + dx_state
    sum_scan = sum_heads(x * dx_scan, heads)
    passing = jnp.sum(start[...] * after[...], axis=0, keepdims=True)
    state_part = jnp.sum(x * dx_state, axis=0, keepdims=True)
    rows = jnp.concatenate([passing, state_part, jnp.zeros((6, DI), F32)], axis=0)
    rows = sum_heads(rows, heads)
    d_last = rows[1:2] + jnp.exp(last) * rows[0:1]
    row = lax.broadcasted_iota(jnp.int32, (CH, 128), 0)
    d_cum = dot_y[...] - sum_scan + jnp.where(row == CH - 1, d_last, 0.0)
    later = cumulate(d_cum, True)
    sig = sigmoid(arg[...])
    ratio = jnp.where(step_here > 1e-30, sig / jnp.maximum(step_here, 1e-30), 1.0)
    d_arg = sum_scan * ratio + rate[...] * later * sig
    bias_part = jnp.sum(d_arg, axis=0, keepdims=True)
    decay_part = rate[...] * jnp.sum(step_here * later, axis=0, keepdims=True)

    dx = dx_scan + skip[...] * d_y[...].astype(F32)
    d_pre[:HALO] = jnp.zeros((HALO, CONV), F32)
    d_pre[HALO + CH :] = jnp.zeros((8, CONV), F32)
    for at in range(0, CONV, 128):
        cols = slice(at, at + 128)
        if at < DI:
            d_out = dx[:, cols]
        else:
            d_out = d_keys if at == DI else d_queries[...]
        d_here = d_out * slope[:, cols].astype(F32)
        d_pre[HALO : HALO + CH, cols] = d_here
        inputs = ext[:, cols].astype(F32)
        d_in, sums = None, []
        for k in range(KERNEL):
            shifted = d_pre[3 - k : 3 - k + HALO + CH, cols]
            part = taps[k : k + 1, cols] * shifted
            d_in = part if d_in is None else d_in + part
            sums.append(jnp.sum(shifted * inputs, axis=0, keepdims=True))
        sums.append(jnp.sum(d_here, axis=0, keepdims=True))
        if at < DI:
            sums.append(jnp.zeros((1, 128), F32))
        else:
            sums.append(bias_part if at == DI else decay_part)
        sums.append(jnp.zeros((2, 128), F32))
        sums_out[:, cols] += jnp.concatenate(sums, axis=0)
        d_halo_out[:, cols] = d_in[:HALO].astype(BF)
        d_proj_out[:, cols] = d_in[HALO:].astype(BF)
    d_halo_out[:, STEP_AT:] = jnp.zeros((HALO, 128), BF)
    d_proj_out[:, STEP_AT:] = d_arg.astype(BF)
    after[...] = after[...] * spread_row(jnp.exp(last), heads) + local_back[...].astype(F32)


def scan_weight_grad(count, me, rows, rows_halo, grad, grad_halo, *refs):
    outs, (total, sems) = refs[:count], refs[count:]
    half = total.shape[1] // 2
    for left in (0, half):
        cols = slice(left, left + half)
        part = dot(rows[...], grad[:, cols], (0, 0))
        part = part + dot(rows_halo[...], grad_halo[:, cols], (0, 0))
        total[:, cols] = part.astype(BF)
    copies = block_copies(me, outs, total, sems, "core", outward=True)
    start_all(copies)
    wait_all(copies)


def other_weight_grad(me, normed, d_gate, cotangent, mixed_in, *refs):
    outs, (total, sems) = refs[:-2], refs[-2:]
    step = pl.program_id(0)

    def keep(part):
        cols = pl.ds(pl.multiple_of(step * part.shape[1], 128), part.shape[1])
        total[:, cols] = part.astype(BF)

    @pl.when(step < 2)
    def _():
        keep(dot(normed[...], d_gate[...], (0, 0)))

    @pl.when(step >= 2)
    def _():
        keep(dot(cotangent[...], mixed_in[...], (0, 0)))

    @pl.when(step == 3)
    def _():
        copies = block_copies(me, outs, total, sems, "core", outward=True)
        start_all(copies)
        wait_all(copies)


def through_others(count, me, normed, cotangent, *refs):
    gates, outs, refs = refs[:count], refs[count : 2 * count], refs[2 * count :]
    gate_out, back_out, w_gate_out, w_out_out, w_gate, w_out, in_sems, out_sems = refs
    step = pl.program_id(0)
    gate_in = block_copies(me, gates, w_gate, in_sems.at[0], "x")
    out_in = block_copies(me, outs, w_out, in_sems.at[1], "y")
    keep_gate = pltpu.make_async_copy(w_gate, w_gate_out, out_sems.at[0])
    keep_out = pltpu.make_async_copy(w_out, w_out_out, out_sems.at[1])

    @pl.when(step == 0)
    def _():
        start_all(gate_in)
        start_all(out_in)
        wait_all(gate_in)
        keep_gate.start()

    @pl.when(step == 2)
    def _():
        wait_all(out_in)
        keep_out.start()

    cols = pl.ds(pl.multiple_of((step % 2) * (DI // 2), 128), DI // 2)

    @pl.when(step < 2)
    def _():
        gate_out[...] = dot(normed[...], w_gate[:, cols])

    @pl.when(step >= 2)
    def _():
        back_out[...] = dot(cotangent[...], w_out[:, cols])

    @pl.when(step == 3)
    def _():
        keep_gate.wait()
        keep_out.wait()


def unit_rows(v):
    v = v.astype(F32)
    scale = lax.rsqrt(jnp.mean(v * v, axis=-1, keepdims=True) + EPSILON)
    return v * scale, scale


def back_to_normed(
    hidden, halo, d_gate, d_scan, d_halo, weight_gate, weight, row_sums, conv_sums,
    out, halo_out, sums_out, total,
):
    @pl.when(pl.program_id(0) == 0)
    def _():
        total[...] = row_sums[...] + conv_sums[...]

    d_normed = dot(d_gate[...], weight_gate[...], (1, 1)) + dot(d_scan[...], weight[...], (1, 1))
    d_normed_halo = dot(d_halo[...], weight[...], (1, 1))
    out[...] = d_normed
    halo_out[...] = d_normed_halo[HALO - 8 :]
    part = jnp.sum(d_normed * unit_rows(hidden[...])[0], axis=0, keepdims=True)
    part = part + jnp.sum(d_normed_halo * unit_rows(halo[...])[0], axis=0, keepdims=True)
    total[7:8, :D] += part

    @pl.when(pl.program_id(0) == pl.num_programs(0) - 1)
    def _():
        high, low = halves(total[...])
        sums_out[:, CONV:] = jnp.zeros((16, WIDE - CONV), BF)
        sums_out[:, :CONV] = jnp.concatenate(
            [high.astype(F32), low.astype(F32)], axis=0
        ).astype(BF)


def finish(hidden, out_grad, d_normed_in, from_next, gain, grad_out):
    unit, scale = unit_rows(hidden[...])
    tail = jnp.concatenate([jnp.zeros((CH - 8, D), F32), from_next[...]], axis=0)
    d_unit = (d_normed_in[...] + tail) * gain[...]
    grad_out[...] = out_grad[...].astype(F32) + scale * (
        d_unit - unit * jnp.mean(d_unit * unit, axis=-1, keepdims=True)
    )


def tie(*values):
    return lax.optimization_barrier(values)


def after(v, other):
    one = other[tuple(slice(0, 1) for _ in other.shape)].reshape((1,) * v.ndim)
    return jnp.where(one == one, v, jnp.zeros_like(v))


def trade(v, axis, mask):
    return lax.ppermute(v, axis, [(i, i ^ mask) for i in range(lax.axis_size(axis))])


def trade_near(v, first):
    pairs = [(i, i ^ (2 if (i % 2 == 0) == first else 4)) for i in range(lax.axis_size("seq"))]
    return lax.ppermute(v, "seq", pairs)


def paired():
    seq, head = lax.axis_size("seq"), lax.axis_size("head")
    return seq == 8 and head & (head - 1) == 0 and D % (seq * 32) == 0


def half_rows(v, of):
    size = v.shape[0] // 2
    return lax.dynamic_slice_in_dim(v, of * size, size, axis=0)


def gather_head(v):
    count = lax.axis_size("head")
    return lax.all_to_all(
        jnp.concatenate([v] * count, axis=0), "head", split_axis=0, concat_axis=0, tiled=True
    )


def gather_head_by_turns(v):
    count, me = lax.axis_size("head"), lax.axis_index("head")
    parts = [v] + [
        lax.ppermute(v, "head", [(i, (i - k) % count) for i in range(count)])
        for k in range(1, count)
    ]
    return parts


def in_order(parts):
    count, me = lax.axis_size("head"), lax.axis_index("head")
    both = jnp.concatenate(list(parts) * 2, axis=0)
    size = parts[0].shape[0]
    return lax.dynamic_slice_in_dim(both, (count - me) * size, count * size, axis=0)


def gather_core(mine, later):
    core = lax.rem(lax.axis_index("seq"), 2)
    got = trade(half_rows(mine, 1 - core), "seq", 1)
    part = jnp.concatenate([half_rows(mine, core), got], axis=0)
    got, *later = tie(trade_near(part, True), *later)
    part = jnp.concatenate([part, got], axis=0)
    part = jnp.concatenate([part, trade_near(part, False)], axis=0)
    return [part, trade(part, "seq", 1)], later


def add(a, b):
    return (a.astype(F32) + b.astype(F32)).astype(BF)


def fold(kept, got):
    size = kept.shape[0] // 2
    sent = add(kept[size:], got[size:])
    return add(kept[:size], got[:size]), sent


def whole_small(small):
    return small[..., :8, :].astype(F32) + small[..., 8:, :].astype(F32)


def add_small(a, b):
    total = whole_small(a) + whole_small(b)
    high = lax.reduce_precision(total, exponent_bits=8, mantissa_bits=7)
    return jnp.concatenate([high, total - high], axis=0).astype(BF)


def join_cores(kept, got):
    core = lax.rem(lax.axis_index("seq"), 2)
    first, second = jnp.where(core == 0, kept, got), jnp.where(core == 0, got, kept)
    return jnp.concatenate([first, second], axis=0)


def scatter_head_by_turns(part):
    count, me = lax.axis_size("head"), lax.axis_index("head")
    size = part.shape[0] // count
    total = lax.dynamic_slice_in_dim(part, me * size, size, axis=0).astype(F32)
    for k in range(1, count):
        away = lax.dynamic_slice_in_dim(part, lax.rem(me + k, count) * size, size, axis=0)
        got = lax.ppermute(away, "head", [(i, (i + k) % count) for i in range(count)])
        total = total + got.astype(F32)
    return total


def tail(kept, sent, other, other_got, work, rest, trade_rest, last):
    part, sent = fold(kept, trade(sent, "seq", 1))
    d_normed, from_next, small = work(sent)
    other = scatter_head_by_turns(join_cores(other, other_got))
    for near in (False, True):
        size = sent.shape[0]
        got = trade_near(jnp.concatenate([sent, small], axis=0), near)
        if not near:
            got, grad = tie(got, rest(d_normed, from_next))
        small = add_small(small, got[size:])
        part, sent = fold(part, got[:size])
    size = sent.shape[0]
    got = trade(jnp.concatenate([sent, small], axis=0), "seq", 1)
    small = add_small(small, got[size:])
    part = join_cores(part, got[:size])
    part, small, grad, mixed = tie(part, small, trade_rest(grad), last())
    got = lax.all_to_all(part, "head", split_axis=0, concat_axis=0, tiled=True)
    turns = in_order(gather_head_by_turns(small))
    small = jnp.sum(whole_small(turns.reshape((-1,) + small.shape)), axis=0)
    got = got.reshape(lax.axis_size("head"), -1, WIDE).astype(F32)
    return jnp.sum(got, axis=0), other, small, grad, mixed


def per_block(
    body, ins, outs, scratch=(), loose=(), loose_outs=0, reverse=False, micros=1, name=None
):
    blocks = next(v.shape[0] for v in ins if v.ndim == 3)
    free = pl.BlockSpec(memory_space=pl.ANY)

    def spec(shape):
        if len(shape) == 1:
            return pl.BlockSpec(memory_space=pltpu.SMEM)
        if len(shape) == 2:
            return pl.BlockSpec(shape, lambda s: (0, 0))
        return pl.BlockSpec(
            (None,) + tuple(shape[1:]), lambda s: (blocks - 1 - s if reverse else s, 0, 0)
        )

    return pl.pallas_call(
        body,
        grid=(blocks,),
        in_specs=[spec(v.shape) for v in ins] + [free] * len(loose),
        out_specs=[spec(shape) for shape, _ in outs[: len(outs) - loose_outs]]
        + [free] * loose_outs,
        out_shape=[jax.ShapeDtypeStruct(shape, kind) for shape, kind in outs],
        scratch_shapes=list(scratch),
        compiler_params=PARAMS,
        cost_estimate=cost(micros),
        name=name,
    )(*ins, *loose)


def send_states(part, groups, spans):
    sent = lax.all_to_all(
        part, BOTH, split_axis=0, concat_axis=0, tiled=True, axis_index_groups=groups
    )
    return sent.reshape(spans, N // spans, STATE)


def return_states(sent, groups, spans, reverse):
    rows = N // spans
    if rows % 8 == 0:
        out = pl.pallas_call(
            partial(state_scan, reverse, spans, rows),
            out_shape=jax.ShapeDtypeStruct((spans, rows, DI), F32 if not reverse else BF),
            scratch_shapes=[pltpu.VMEM((spans, rows, DI), F32)],
            compiler_params=PARAMS,
            cost_estimate=cost(2),
            name="state_scan",
        )(sent)
    else:
        last = sent[:, :, DI:].astype(F32)
        last = last[..., :H] + last[..., 32 : 32 + H] + last[..., 64 : 64 + H]
        decay = jnp.repeat(jnp.exp(last), P_SIZE, axis=-1)

        def move(carry, at):
            return at[0] * carry + at[1], carry.astype(BF)

        _, out = lax.scan(
            move,
            jnp.zeros((rows, DI), F32),
            (decay, sent[:, :, :DI].astype(F32)),
            reverse=reverse,
        )
    back = lax.all_to_all(
        out.reshape(N, DI), BOTH, split_axis=0, concat_axis=0, tiled=True,
        axis_index_groups=groups,
    )
    return back


def to_span(v):
    seqs, rows, width = v.shape
    if seqs == 2:
        mine = lax.rem(lax.axis_index("head"), 2)
        got = trade(lax.dynamic_index_in_dim(v, 1 - mine, keepdims=False), "head", 1)

        def join(got):
            keep = lax.dynamic_index_in_dim(v, mine, keepdims=False)
            first, second = jnp.where(mine == 0, keep, got), jnp.where(mine == 0, got, keep)
            return jnp.concatenate([first, second], axis=0).reshape(-1, CH, width)

        return got, join
    groups = [[i + j for j in range(seqs)] for i in range(0, lax.axis_size("head"), seqs)]
    v = lax.all_to_all(
        v, "head", split_axis=0, concat_axis=1, tiled=True, axis_index_groups=groups
    )
    return v, lambda got: got.reshape(-1, CH, width)


def from_span(v, seqs):
    rows = v.shape[0] // seqs
    if seqs == 2:
        mine = lax.rem(lax.axis_index("head"), 2)
        got = trade(half_rows(v, 1 - mine).astype(BF), "head", 1)

        def join(got):
            keep, got = half_rows(v, mine), got.astype(v.dtype)
            return jnp.stack([jnp.where(mine == 0, keep, got), jnp.where(mine == 0, got, keep)])

        return got, join
    groups = [[i + j for j in range(seqs)] for i in range(0, lax.axis_size("head"), seqs)]
    v = v.reshape(1, seqs * rows, v.shape[-1])
    got = lax.all_to_all(
        v, "head", split_axis=1, concat_axis=0, tiled=True, axis_index_groups=groups
    )
    return got, lambda got: got


def pad_lanes(v, width):
    return jnp.pad(v, [(0, 0)] * (v.ndim - 1) + [(0, width - v.shape[-1])])


def gather_rows(v):
    return lax.all_gather(lax.all_gather(v, "head", axis=0, tiled=True), "seq", axis=0, tiled=True)


def scatter_rows(v):
    part = lax.psum_scatter(v, "seq", scatter_dimension=0, tiled=True)
    part = lax.psum_scatter(part, "head", scatter_dimension=0, tiled=True)
    return lax.optimization_barrier(part).astype(F32)


def on_device(
    hidden,
    out_grad,
    norm_gain,
    input_projection_weight,
    conv_weight,
    conv_bias,
    step_bias,
    decay_log,
    skip_weight,
    gate_gain,
    output_projection_weight,
):
    devices = lax.axis_size("seq") * lax.axis_size("head")
    seqs = hidden.shape[0]
    spans = devices // seqs
    groups = [[d for d in range(devices) if d % seqs == r] for r in range(seqs)]
    onward = [(i, i + seqs) for i in range(devices - seqs)]
    backward = [(i + seqs, i) for i in range(devices - seqs)]
    tokens = seqs * hidden.shape[1]
    blocks = tokens // CH

    def tails_before(v):
        if seqs != 2:
            return None
        odd = [d for d in range(devices) if d % 2]
        got = [
            lax.ppermute(
                v[s : s + 1, v.shape[1] - HALO :],
                BOTH,
                [(d, d + 1 + s) for d in odd if d + 1 + s < devices],
            )
            for s in range(2)
        ]
        return got[0] + got[1]

    def with_halo(v, before):
        tails = v[:, CH - HALO :]
        if before is None:
            before = lax.ppermute(tails[-1:], BOTH, onward)
        return jnp.concatenate([before, tails[:-1]], axis=0)

    fast = paired()
    me = lax.axis_index("seq").astype(jnp.int32)[None]
    scan_part = pad_lanes(input_projection_weight[:, DI:], WIDE)
    other_part = jnp.concatenate([input_projection_weight[:, :DI], output_projection_weight], 1)
    before = tails_before(hidden)
    hidden, join_hidden = to_span(hidden)
    if fast:
        pieces, (hidden, other_part) = gather_core(
            gather_head(scan_part), (hidden, other_part)
        )
        conv_bias, *turns = tie(conv_bias, *gather_head_by_turns(other_part))
        other_mine = in_order(turns)
        w_gate, w_out = other_mine[:, :DI], other_mine[:, DI:]
        gate_got, out_got = trade(w_gate, "seq", 2), trade(w_out, "seq", 4)
    else:
        pieces = [gather_rows(scan_part)]
        others = gather_rows(other_part)
        w_gate, w_out = others[:, :DI], others[:, DI:]
    hidden = join_hidden(hidden)
    halo = with_halo(hidden, before)
    out_grad, join_out_grad = to_span(out_grad)
    copies = 16 if fast else 1

    gain_one = norm_gain[None]
    gain_two = gate_gain[None]
    taps = jnp.pad(conv_weight, ((0, 4), (0, 0)))
    offset = conv_bias[None]
    bias = pad_lanes(step_bias[None], 128)
    rate = pad_lanes(-jnp.exp(decay_log)[None], 128)
    skip = jnp.repeat(skip_weight, P_SIZE)[None]

    (
        normed, normed_halo, ext, slope, conv, cum, cumt, step, stept, arg, local, part, w_scan,
    ) = per_block(
        partial(before_scan, len(pieces)),
        [me, hidden, halo, gain_one, taps, offset, bias, rate],
        [
            ((blocks, CH, D), BF),
            ((blocks, HALO, D), BF),
            ((blocks, HALO + CH, CONV), BF),
            ((blocks, CH, CONV), BF),
            ((blocks, CH, CONV), BF),
            ((blocks, CH, 128), F32),
            ((blocks, 32, CH), F32),
            ((blocks, CH, 128), F32),
            ((blocks, 32, CH), F32),
            ((blocks, CH, 128), F32),
            ((blocks, N, DI), F32),
            ((N, STATE), BF),
            ((D, WIDE), BF),
        ],
        [
            pltpu.VMEM((HALO + CH, CONV), F32),
            pltpu.VMEM((D, WIDE), BF),
            pltpu.VMEM((N, DI), F32),
            pltpu.VMEM((8, 128), F32),
            pltpu.SemaphoreType.DMA((copies,)),
            pltpu.SemaphoreType.DMA,
        ],
        loose=pieces,
        loose_outs=1,
        micros=12, name="before_scan",
    )
    if fast:
        cumt, gate_got, out_got = tie(cumt, gate_got, out_got)
        w_gate = jnp.concatenate([w_gate, gate_got], axis=0)
        w_out = jnp.concatenate([w_out, out_got], axis=0)
        ways = (trade(w_gate, "seq", 4), trade(w_out, "seq", 2))
    else:
        ways = ()
    (within,) = per_block(
        within_block, [conv, cum, cumt, stept], [((blocks, CH, DI), F32)],
        micros=5, name="within_block",
    )
    sent, within, out_grad, ways = tie(send_states(part, groups, spans), within, out_grad, ways)
    if fast:
        w_gate = jnp.concatenate([w_gate, ways[0]], axis=0)
        w_out = jnp.concatenate([w_out, ways[1]], axis=0)
        gates, outs = [w_gate, trade(w_gate, "seq", 1)], [w_out, trade(w_out, "seq", 1)]
    else:
        gates, outs = [w_gate], [w_out]
    incoming = return_states(sent, groups, spans, False)

    normed_rows = normed.reshape(tokens, D)
    out_grad = join_out_grad(out_grad)
    cotangent = out_grad.reshape(tokens, D)
    gate, d_mixed_in, w_gate, w_out = pl.pallas_call(
        partial(through_others, len(gates)),
        grid=(4,),
        in_specs=[
            pl.BlockSpec(memory_space=pltpu.SMEM),
            pl.BlockSpec((tokens, D), lambda j: (0, 0)),
            pl.BlockSpec((tokens, D), lambda j: (0, 0)),
        ]
        + [pl.BlockSpec(memory_space=pl.ANY)] * (2 * len(gates)),
        out_specs=[
            pl.BlockSpec((tokens, DI // 2), lambda j: (0, jnp.minimum(j, 1))),
            pl.BlockSpec((tokens, DI // 2), lambda j: (0, jnp.maximum(j - 2, 0))),
            pl.BlockSpec(memory_space=pl.ANY),
            pl.BlockSpec(memory_space=pl.ANY),
        ],
        out_shape=[jax.ShapeDtypeStruct((tokens, DI), F32)] * 2
        + [jax.ShapeDtypeStruct((D, DI), BF)] * 2,
        scratch_shapes=[
            pltpu.VMEM((D, DI), BF),
            pltpu.VMEM((D, DI), BF),
            pltpu.SemaphoreType.DMA((2, 8 if fast else 1)),
            pltpu.SemaphoreType.DMA((2,)),
        ],
        compiler_params=PARAMS,
        cost_estimate=cost(8),
        name="through_others",
    )(me, normed_rows, cotangent, *gates, *outs)
    gate, d_mixed_in = gate.reshape(blocks, CH, DI), d_mixed_in.reshape(blocks, CH, DI)

    mixed_in, d_gate, d_y, dot_y, starts, local_back, part, row_sums = per_block(
        around_norm,
        [within, conv, cum, local, incoming, gate, d_mixed_in, gain_two, skip],
        [
            ((blocks, CH, DI), BF),
            ((blocks, CH, DI), BF),
            ((blocks, CH, DI), BF),
            ((blocks, CH, 128), F32),
            ((blocks, N, DI), F32),
            ((blocks, N, DI), BF),
            ((N, STATE), BF),
            ((8, CONV), F32),
        ],
        [pltpu.VMEM((N, DI), F32), pltpu.VMEM((N, DI), F32), pltpu.VMEM((8, 128), F32)],
        micros=13, name="around_norm",
    )

    mixed_rows = mixed_in.reshape(tokens, DI)
    d_gate_rows = d_gate.reshape(tokens, DI)
    other_terms = pl.pallas_call(
        other_weight_grad,
        grid=(4,),
        in_specs=[
            pl.BlockSpec(memory_space=pltpu.SMEM),
            pl.BlockSpec((tokens, D), lambda j: (0, 0)),
            pl.BlockSpec((tokens, DI // 2), lambda j: (0, jnp.minimum(j, 1))),
            pl.BlockSpec((tokens, D), lambda j: (0, 0)),
            pl.BlockSpec((tokens, DI // 2), lambda j: (0, jnp.maximum(j - 2, 0))),
        ],
        out_specs=[pl.BlockSpec(memory_space=pl.ANY)] * len(pieces),
        out_shape=[jax.ShapeDtypeStruct((D // len(pieces), 2 * DI), BF)] * len(pieces),
        scratch_shapes=[pltpu.VMEM((D, 2 * DI), BF), pltpu.SemaphoreType.DMA((copies,))],
        compiler_params=PARAMS,
        cost_estimate=cost(8),
        name="other_weight_grad",
    )(me, normed_rows, d_gate_rows, cotangent, mixed_rows)
    sent, other_terms, mixed_rows, d_y = tie(
        send_states(part, groups, spans), other_terms, mixed_rows, d_y
    )
    incoming = return_states(sent, groups, spans, True)
    branch = dot(mixed_rows, w_out, (1, 1))
    mixed = (hidden.reshape(tokens, D).astype(F32) + branch).astype(BF)
    if fast:
        other, other_sent = fold(other_terms[0], trade(other_terms[1], "seq", 1))
    else:
        other = other_terms[0]

    dx_within, d_keys, d_queries = per_block(
        within_block_back,
        [conv, cum, cumt, step, d_y, starts],
        [((blocks, CH, DI), F32), ((blocks, CH, N), F32), ((blocks, CH, N), F32)],
        [pltpu.VMEM((CH, CH), F32)],
        micros=9, name="within_block_back",
    )
    if fast:
        got = trade_near(other_sent, False)
    d_scan, d_halo, conv_sums = per_block(
        after_scan,
        [
            conv, slope, ext, cum, step, arg, d_y, dx_within, d_keys, d_queries, dot_y, starts,
            local_back, incoming, skip, rate, taps,
        ],
        [
            ((blocks, CH, WIDE), BF),
            ((blocks, HALO, WIDE), BF),
            ((8, CONV), F32),
        ],
        [
            pltpu.VMEM((HALO + CH + 8, CONV), F32),
            pltpu.VMEM((N, DI), F32),
        ],
        reverse=True,
        micros=16, name="after_scan",
    )

    if fast:
        d_scan, got = tie(d_scan, got)
        other, other_sent = fold(other, got)
        other, other_sent = fold(other, trade_near(other_sent, True))
        other_got = trade(other_sent, "seq", 1)
    mixed, join_mixed = from_span(mixed, seqs)
    mixed, d_scan = tie(mixed, d_scan)
    if not fast:
        mixed = join_mixed(mixed)
    terms = pl.pallas_call(
        partial(scan_weight_grad, len(pieces)),
        in_specs=[pl.BlockSpec(memory_space=pltpu.SMEM)]
        + [pl.BlockSpec(memory_space=pltpu.VMEM)] * 4,
        out_specs=[pl.BlockSpec(memory_space=pl.ANY)] * len(pieces),
        out_shape=[jax.ShapeDtypeStruct((D // len(pieces), WIDE), BF)] * len(pieces),
        scratch_shapes=[pltpu.VMEM((D, WIDE), BF), pltpu.SemaphoreType.DMA((copies,))],
        compiler_params=PARAMS,
        cost_estimate=cost(6),
        name="scan_weight_grad",
    )(
        me,
        normed_rows,
        normed_halo.reshape(blocks * HALO, D),
        d_scan.reshape(tokens, WIDE),
        d_halo.reshape(blocks * HALO, WIDE),
    )

    def to_normed(go):
        d_scan_now = tie(d_scan, go)[0]
        d_normed, d_normed_halo, small = per_block(
            back_to_normed,
            [
                hidden, halo, d_gate, d_scan_now, d_halo, w_gate, w_scan, row_sums, conv_sums,
            ],
            [((blocks, CH, D), F32), ((blocks, 8, D), F32), ((16, WIDE), BF)],
            [pltpu.VMEM((8, CONV), F32)],
            micros=7, name="back_to_normed",
        )
        from_next = lax.ppermute(d_normed_halo[:1], BOTH, backward)
        return d_normed, jnp.concatenate([d_normed_halo[1:], from_next], axis=0), small

    def to_hidden(d_normed, from_next):
        return per_block(
            finish,
            [hidden, out_grad, d_normed, from_next, gain_one],
            [((blocks, CH, D), F32)],
            micros=3, name="finish",
        )[0].reshape(tokens, D)

    def grad_back(grad):
        got, join = from_span(grad, seqs)
        return join(got)

    if fast:
        scan_rows, other_rows, small, hidden_grad, mixed = tail(
            *terms, other, other_got, to_normed, to_hidden, grad_back, lambda: join_mixed(mixed)
        )
    else:
        d_normed, from_next, small = to_normed(jnp.zeros((8, 128), F32))
        other_rows = scatter_rows(other)
        scan_rows = scatter_rows(terms[0])
        small = lax.psum(whole_small(small), BOTH)
        hidden_grad = grad_back(to_hidden(d_normed, from_next))
    small = small[:, :CONV]
    in_rows = jnp.concatenate([other_rows[:, :DI], scan_rows[:, : CONV + H]], axis=1)
    return (
        mixed,
        hidden_grad,
        small[7, :D],
        in_rows,
        small[:KERNEL],
        small[4],
        small[5, DI : DI + H],
        small[5, DI + 128 : DI + 128 + H],
        small[6, :H],
        small[5, :DI],
        other_rows[:, DI:],
    )


def solution(mesh):
    rows = P(None, BOTH, None)
    weight = P(BOTH, None)
    return jax.shard_map(
        on_device,
        mesh=mesh,
        in_specs=(rows, rows, P(), weight, P(), P(), P(), P(), P(), P(), weight),
        out_specs=(rows, rows, P(), weight, P(), P(), P(), P(), P(), P(), weight),
        check_vma=False,
    )
```

```python
from functools import partial

import jax
import jax.numpy as jnp
from jax import lax
from jax.experimental import pallas as pl
from jax.experimental.pallas import tpu as pltpu
from jax.sharding import PartitionSpec as P

D = 768
H = 24
P_SIZE = 64
N = 128
KERNEL = 4
CH = 256
DI = H * P_SIZE
CONV = DI + 2 * N
STEP_AT = CONV
WIDE = CONV + 128
STATE = DI + 128
HALO = 16
EPSILON = 1e-05
BF = jnp.bfloat16
F32 = jnp.float32
BOTH = ("seq", "head")
PARAMS = pltpu.CompilerParams(vmem_limit_bytes=56 * 1024 * 1024)


def cost(micros):
    return pl.CostEstimate(
        flops=int(micros * 1.1e9), bytes_accessed=int(micros * 3e6), transcendentals=0
    )


def dot(a, b, contract=(1, 0)):
    return lax.dot_general(
        a, b, (((contract[0],), (contract[1],)), ((), ())), preferred_element_type=F32
    )


def halves(v):
    high = v.astype(BF)
    return high, (v - high.astype(F32)).astype(BF)


def head_map(rows, period=None):
    row = lax.broadcasted_iota(jnp.int32, (rows, DI), 0)
    col = lax.broadcasted_iota(jnp.int32, (rows, DI), 1)
    if period is not None:
        row = jnp.bitwise_and(row, period - 1)
    return (row == jnp.right_shift(col, 6)).astype(F32).astype(BF)


def spread_heads(v, heads):
    high, low = halves(v)
    return dot(high, heads) + dot(low, heads)


def sum_heads(v, heads):
    high, low = halves(v)
    return dot(high, heads, (1, 1)) + dot(low, heads, (1, 1))


def sigmoid(v):
    return 0.5 * jnp.tanh(0.5 * v) + 0.5


def softplus(v):
    return jnp.maximum(v, 0.0) + jnp.log1p(jnp.exp(-jnp.abs(v)))


def cumulate(v, flip):
    ones = triangle(flip).astype(F32).astype(BF)
    high, rest = halves(v)
    low = (v - high.astype(F32) - rest.astype(F32)).astype(BF)
    return dot(ones, high) + dot(ones, rest) + dot(ones, low)


def triangle(flip):
    row = lax.broadcasted_iota(jnp.int32, (CH, CH), 0)
    col = lax.broadcasted_iota(jnp.int32, (CH, CH), 1)
    return row <= col if flip else row >= col


def last_lanes(last):
    high = last.astype(BF).astype(F32)
    rest = last - high
    mid = rest.astype(BF).astype(F32)
    low = rest - mid
    return high + pltpu.roll(mid, 32, 1) + pltpu.roll(low, 64, 1)


def store_state(out, state, last):
    out[:, :DI] = state.astype(BF)
    out[:, DI:] = jnp.broadcast_to(last_lanes(last), (N, 128)).astype(BF)


def spread_row(v, heads):
    return spread_heads(jnp.broadcast_to(v, (8, 128)), heads)[0:1]


def block_copies(me, pieces, whole, sems, way, outward=False):
    copies = []
    for at, piece in enumerate(pieces):
        if len(pieces) == 1:
            pairs = [(piece, whole)]
        else:
            seq = jnp.bitwise_xor(me[0], at if way == "core" else at // 2)
            core = jnp.bitwise_and(seq, 1)
            near = 2 + 2 * core
            count = 8 if way == "core" else 2
            size = piece.shape[0] // count
            pairs = []
            for k in range(count):
                if way == "core":
                    mask = (k & 1) + ((k >> 1) & 1) * near + (k >> 2) * (6 - near)
                    row = (jnp.bitwise_xor(seq, mask) * 2 + core) * size
                else:
                    first, second = (2, 4) if way == "x" else (4, 2)
                    row = jnp.bitwise_xor(seq, k * first + (at % 2) * second) * size
                rows = pl.ds(pl.multiple_of(row, size), size)
                pairs.append((piece.at[pl.ds(k * size, size)], whole.at[rows]))
        for block, rows in pairs:
            pair = (rows, block) if outward else (block, rows)
            copies.append(pltpu.make_async_copy(*pair, sems.at[len(copies)]))
    return copies


def start_all(copies):
    for copy in copies:
        copy.start()


def wait_all(copies):
    for copy in copies:
        copy.wait()


def before_scan(
    count, me, hid, halo, gain, taps, offset, bias, rate, *refs
):
    pieces = refs[:count]
    (
        normed_out, normed_halo_out, ext_out, slope_out, conv_out, cum_out, cumt_out, step_out, stept_out,
        arg_out, local_out, state_out, weight_out,
        ext32, weight, total, total_last, in_sems, out_sem,
    ) = refs[count:]
    keep_weight = pltpu.make_async_copy(weight, weight_out, out_sem)

    @pl.when(pl.program_id(0) == 0)
    def _():
        copies = block_copies(me, pieces, weight, in_sems, "core")
        start_all(copies)
        wait_all(copies)
        keep_weight.start()
        total[...] = jnp.zeros_like(total)
        total_last[...] = jnp.zeros_like(total_last)

    def norm(v):
        v = v.astype(F32)
        scale = lax.rsqrt(jnp.mean(v * v, axis=-1, keepdims=True) + EPSILON)
        return (v * scale * gain[...]).astype(BF)

    rows = norm(hid[...])
    rows_halo = norm(halo[...])
    normed_out[...] = rows
    normed_halo_out[...] = rows_halo
    projected = dot(rows, weight[...])
    projected_halo = dot(rows_halo, weight[:, :CONV])
    low = projected[:, :CONV].astype(BF)
    low_halo = projected_halo.astype(BF)
    ext_out[:HALO] = low_halo
    ext_out[HALO:] = low
    ext32[:HALO] = low_halo.astype(F32)
    ext32[HALO:] = low.astype(F32)
    for at in range(0, CONV, 128):
        cols = slice(at, at + 128)
        pre = offset[:, cols] + taps[0:1, cols] * ext32[HALO - 3 : HALO - 3 + CH, cols]
        for k in range(1, KERNEL):
            pre = pre + taps[k : k + 1, cols] * ext32[HALO - 3 + k : HALO - 3 + k + CH, cols]
        sig = sigmoid(pre)
        act = pre * sig
        conv_out[:, cols] = act.astype(BF)
        slope_out[:, cols] = (sig + act * (1.0 - sig)).astype(BF)
    arg = projected[:, STEP_AT:].astype(BF).astype(F32) + bias[...]
    step = softplus(arg)
    cum = cumulate(step * rate[...], False)
    arg_out[...] = arg
    step_out[...] = step
    stept_out[...] = jnp.transpose(step)[:32]
    cum_out[...] = cum
    cumt_out[...] = jnp.transpose(cum)[:32]
    last = cum[CH - 1 : CH]
    heads = head_map(128)
    w = spread_heads(jnp.exp(last - cum) * step, heads)
    weighted = (conv_out[:, :DI].astype(F32) * w).astype(BF)
    local = dot(conv_out[:, DI : DI + N], weighted, (0, 0))
    local_out[...] = local
    total[...] = total[...] * spread_row(jnp.exp(last), heads) + local
    total_last[...] += jnp.broadcast_to(last, total_last.shape)

    @pl.when(pl.program_id(0) == pl.num_programs(0) - 1)
    def _():
        keep_weight.wait()
        store_state(state_out, total[...], total_last[0:1])


def within_block(conv, cum, cumt, stept, y_out):
    keys = conv[:, DI : DI + N]
    queries = conv[:, DI + N :]
    scores = jnp.where(triangle(False), dot(queries, keys, (1, 1)), 0.0)
    half = CH // 2
    lane = lax.broadcasted_iota(jnp.int32, (half, 128), 1) < P_SIZE
    for pair in range(H // 2):
        cols = slice(pair * 128, pair * 128 + 128)
        for top, width in ((0, half), (half, CH)):
            x = conv[:width, cols]
            parts = []
            for h in (2 * pair, 2 * pair + 1):
                spread = cum[top : top + half, h : h + 1] - cumt[h : h + 1, :width]
                decay = jnp.exp(jnp.minimum(spread, 0.0))
                mixing = scores[top : top + half, :width] * decay * stept[h : h + 1, :width]
                parts.append(dot(mixing.astype(BF), x))
            y_out[top : top + half, cols] = jnp.where(lane, parts[0], parts[1])


def state_scan(reverse, blocks, rows, parts_in, out, decay):
    heads = head_map(128, 32)
    lane = lax.broadcasted_iota(jnp.int32, (blocks * rows, 128), 1)
    last = parts_in[:, :, DI:].reshape(blocks * rows, 128)
    last = jnp.where(lane < 96, last.astype(F32), 0.0).astype(BF)
    decay[...] = jnp.exp(dot(last, heads)).reshape(blocks, rows, DI)
    carry = jnp.zeros((rows, DI), F32)
    for k in range(blocks - 1, -1, -1) if reverse else range(blocks):
        if reverse:
            out[k] = carry.astype(BF)
        else:
            top = jnp.max(jnp.abs(carry), axis=-1, keepdims=True)
            power = jnp.ceil(jnp.log2(jnp.maximum(top, 1e-30)))
            out[k, :, :DI] = carry * jnp.exp2(-power)
            out[k, :, DI:] = jnp.broadcast_to(power, (rows, 128))
        carry = decay[k] * carry + parts_in[k, :, :DI].astype(F32)


def around_norm(
    within, conv, cum, local, incoming, gate, dmi, gain, skip,
    mixed_in_out, d_gate_out, d_y_out, dot_y_out, start_out, local_back_out, state_out, sums_out,
    start, total, total_last,
):
    @pl.when(pl.program_id(0) == 0)
    def _():
        start[...] = incoming[...].astype(F32)
        total[...] = jnp.zeros_like(total)
        total_last[...] = jnp.zeros_like(total_last)
        sums_out[...] = jnp.zeros_like(sums_out)

    start_high, start_low = halves(start[...])
    start_out[...] = start[...]
    heads = head_map(128)
    x = conv[:, :DI].astype(F32)
    queries = conv[:, DI + N :]
    cum_here = cum[...]
    e_cum = spread_heads(jnp.exp(cum_here), heads)
    y_scan = within[...] + (dot(queries, start_high) + dot(queries, start_low)) * e_cum
    y = (y_scan + skip[...] * x).astype(BF).astype(F32)
    gate_here = gate[...]
    sig = sigmoid(gate_here)
    act = gate_here * sig
    gated = y * act
    scale = lax.rsqrt(jnp.mean(gated * gated, axis=-1, keepdims=True) + EPSILON)
    unit = gated * scale
    mixed_in_out[...] = (unit * gain[...]).astype(BF)
    d_mixed_in = dmi[...]
    gain_part = jnp.sum(d_mixed_in * unit, axis=0, keepdims=True)
    d_unit = d_mixed_in * gain[...]
    d_gated = scale * (d_unit - unit * jnp.mean(d_unit * unit, axis=-1, keepdims=True))
    d_y_low = (d_gated * act).astype(BF)
    d_y_out[...] = d_y_low
    d_gate_out[...] = (d_gated * y * (sig * (1.0 + gate_here * (1.0 - sig)))).astype(BF)
    d_y = d_y_low.astype(F32)
    dot_y_out[...] = sum_heads(d_y * y_scan, heads)
    skip_part = jnp.sum(d_y * x, axis=0, keepdims=True)
    sums_out[5:6, :DI] += gain_part
    sums_out[6:7, :128] += sum_heads(jnp.broadcast_to(skip_part, (8, DI)), heads)[0:1]
    scaled, scaled_low = halves(d_y * e_cum)
    local_back = dot(queries, scaled, (0, 0)) + dot(queries, scaled_low, (0, 0))
    local_back_out[...] = local_back.astype(BF)
    last = cum_here[CH - 1 : CH]
    start[...] = start[...] * spread_row(jnp.exp(last), heads) + local[...]
    total[...] += spread_row(jnp.exp(total_last[0:1]), heads) * local_back
    total_last[...] += jnp.broadcast_to(last, total_last.shape)

    @pl.when(pl.program_id(0) == pl.num_programs(0) - 1)
    def _():
        store_state(state_out, total[...], total_last[0:1])


def within_block_back(
    conv, cum, cumt, step, d_y, start, dx_out, d_keys_out, d_queries_out, scores_grad
):
    keys = conv[:, DI : DI + N]
    queries = conv[:, DI + N :]
    scores = jnp.where(triangle(True), dot(keys, queries, (1, 1)), 0.0)
    scores_grad[...] = jnp.zeros_like(scores_grad)
    half = CH // 2
    lane = lax.broadcasted_iota(jnp.int32, (half, 128), 1) < P_SIZE
    for pair in range(H // 2):
        cols = slice(pair * 128, pair * 128 + 128)
        for top, left in ((0, 0), (half, half)):
            x = conv[top : top + half, cols].astype(F32)
            dy = d_y[left:, cols]
            parts = []
            for side, h in enumerate((2 * pair, 2 * pair + 1)):
                spread = cumt[h : h + 1, left:] - cum[top : top + half, h : h + 1]
                decay = jnp.exp(jnp.minimum(spread, 0.0)) * step[top : top + half, h : h + 1]
                mixing = (scores[top : top + half, left:] * decay).astype(BF)
                parts.append(dot(mixing, dy))
                x_one = jnp.where(lane if side == 0 else ~lane, x, 0.0).astype(BF)
                d_mixing = dot(x_one, dy, (1, 1))
                scores_grad[top : top + half, left:] += d_mixing * decay
            dx_out[top : top + half, cols] = jnp.where(lane, parts[0], parts[1])
    d_scores = jnp.where(triangle(True), scores_grad[...], 0.0)
    high, low = halves(d_scores)
    d_keys_out[...] = dot(high, queries) + dot(low, queries)
    scaled, scaled_low = halves(
        d_y[...].astype(F32) * spread_heads(jnp.exp(cum[...]), head_map(128))
    )
    start_high, start_low = halves(start[...])
    d_queries_out[...] = (
        dot(high, keys, (0, 0))
        + dot(low, keys, (0, 0))
        + dot(scaled, start_high, (1, 1))
        + dot(scaled_low, start_high, (1, 1))
        + dot(scaled, start_low, (1, 1))
    )


def after_scan(
    conv, slope, ext, cum, step, arg, d_y, dx_within, d_keys_in, d_queries, dot_y, start, local_back,
    incoming, skip, rate, taps,
    d_proj_out, d_halo_out, sums_out, d_pre, after,
):
    @pl.when(pl.program_id(0) == 0)
    def _():
        after[...] = incoming[...].astype(F32)
        sums_out[...] = jnp.zeros_like(sums_out)

    after_high = after[...].astype(BF)
    heads = head_map(128)
    x = conv[:, :DI].astype(F32)
    keys = conv[:, DI : DI + N]
    cum_here = cum[...]
    step_here = step[...]
    last = cum_here[CH - 1 : CH]
    w = spread_heads(jnp.exp(last - cum_here) * step_here, heads)
    weighted = (x * w).astype(BF)
    dx_state = dot(keys, after_high) * w
    d_keys = d_keys_in[...] + dot(weighted, after_high, (1, 1))
    dx_scan = dx_within[...] + dx_state
    sum_scan = sum_heads(x * dx_scan, heads)
    passing = jnp.sum(start[...] * after[...], axis=0, keepdims=True)
    state_part = jnp.sum(x * dx_state, axis=0, keepdims=True)
    rows = jnp.concatenate([passing, state_part, jnp.zeros((6, DI), F32)], axis=0)
    rows = sum_heads(rows, heads)
    d_last = rows[1:2] + jnp.exp(last) * rows[0:1]
    row = lax.broadcasted_iota(jnp.int32, (CH, 128), 0)
    d_cum = dot_y[...] - sum_scan + jnp.where(row == CH - 1, d_last, 0.0)
    later = cumulate(d_cum, True)
    sig = sigmoid(arg[...])
    ratio = jnp.where(step_here > 1e-30, sig / jnp.maximum(step_here, 1e-30), 1.0)
    d_arg = sum_scan * ratio + rate[...] * later * sig
    bias_part = jnp.sum(d_arg, axis=0, keepdims=True)
    decay_part = rate[...] * jnp.sum(step_here * later, axis=0, keepdims=True)

    dx = dx_scan + skip[...] * d_y[...].astype(F32)
    d_pre[:HALO] = jnp.zeros((HALO, CONV), F32)
    d_pre[HALO + CH :] = jnp.zeros((8, CONV), F32)
    for at in range(0, CONV, 128):
        cols = slice(at, at + 128)
        if at < DI:
            d_out = dx[:, cols]
        else:
            d_out = d_keys if at == DI else d_queries[...]
        d_here = d_out * slope[:, cols].astype(F32)
        d_pre[HALO : HALO + CH, cols] = d_here
        inputs = ext[:, cols].astype(F32)
        d_in, sums = None, []
        for k in range(KERNEL):
            shifted = d_pre[3 - k : 3 - k + HALO + CH, cols]
            part = taps[k : k + 1, cols] * shifted
            d_in = part if d_in is None else d_in + part
            sums.append(jnp.sum(shifted * inputs, axis=0, keepdims=True))
        sums.append(jnp.sum(d_here, axis=0, keepdims=True))
        if at < DI:
            sums.append(jnp.zeros((1, 128), F32))
        else:
            sums.append(bias_part if at == DI else decay_part)
        sums.append(jnp.zeros((2, 128), F32))
        sums_out[:, cols] += jnp.concatenate(sums, axis=0)
        d_halo_out[:, cols] = d_in[:HALO].astype(BF)
        d_proj_out[:, cols] = d_in[HALO:].astype(BF)
    d_halo_out[:, STEP_AT:] = jnp.zeros((HALO, 128), BF)
    d_proj_out[:, STEP_AT:] = d_arg.astype(BF)
    after[...] = after[...] * spread_row(jnp.exp(last), heads) + local_back[...].astype(F32)


def scan_weight_grad(count, me, rows, rows_halo, grad, grad_halo, *refs):
    outs, (total, sems) = refs[:count], refs[count:]
    half = total.shape[1] // 2
    for left in (0, half):
        cols = slice(left, left + half)
        part = dot(rows[...], grad[:, cols], (0, 0))
        part = part + dot(rows_halo[...], grad_halo[:, cols], (0, 0))
        total[:, cols] = part.astype(BF)
    copies = block_copies(me, outs, total, sems, "core", outward=True)
    start_all(copies)
    wait_all(copies)


def other_weight_grad(me, normed, d_gate, cotangent, mixed_in, *refs):
    outs, (total, sems) = refs[:-2], refs[-2:]
    step = pl.program_id(0)

    def keep(part):
        cols = pl.ds(pl.multiple_of(step * part.shape[1], 128), part.shape[1])
        total[:, cols] = part.astype(BF)

    @pl.when(step < 2)
    def _():
        keep(dot(normed[...], d_gate[...], (0, 0)))

    @pl.when(step >= 2)
    def _():
        keep(dot(cotangent[...], mixed_in[...], (0, 0)))

    @pl.when(step == 3)
    def _():
        copies = block_copies(me, outs, total, sems, "core", outward=True)
        start_all(copies)
        wait_all(copies)


def through_others(count, me, normed, cotangent, *refs):
    gates, outs, refs = refs[:count], refs[count : 2 * count], refs[2 * count :]
    gate_out, back_out, w_gate_out, w_out_out, w_gate, w_out, in_sems, out_sems = refs
    step = pl.program_id(0)
    gate_in = block_copies(me, gates, w_gate, in_sems.at[0], "x")
    out_in = block_copies(me, outs, w_out, in_sems.at[1], "y")
    keep_gate = pltpu.make_async_copy(w_gate, w_gate_out, out_sems.at[0])
    keep_out = pltpu.make_async_copy(w_out, w_out_out, out_sems.at[1])

    @pl.when(step == 0)
    def _():
        start_all(gate_in)
        start_all(out_in)
        wait_all(gate_in)
        keep_gate.start()

    @pl.when(step == 2)
    def _():
        wait_all(out_in)
        keep_out.start()

    cols = pl.ds(pl.multiple_of((step % 2) * (DI // 2), 128), DI // 2)

    @pl.when(step < 2)
    def _():
        gate_out[...] = dot(normed[...], w_gate[:, cols])

    @pl.when(step >= 2)
    def _():
        back_out[...] = dot(cotangent[...], w_out[:, cols])

    @pl.when(step == 3)
    def _():
        keep_gate.wait()
        keep_out.wait()


def unit_rows(v):
    v = v.astype(F32)
    scale = lax.rsqrt(jnp.mean(v * v, axis=-1, keepdims=True) + EPSILON)
    return v * scale, scale


def back_to_normed(
    hidden, halo, d_gate, d_scan, d_halo, weight_gate, weight, row_sums, conv_sums,
    out, halo_out, sums_out, total,
):
    @pl.when(pl.program_id(0) == 0)
    def _():
        total[...] = row_sums[...] + conv_sums[...]

    d_normed = dot(d_gate[...], weight_gate[...], (1, 1)) + dot(d_scan[...], weight[...], (1, 1))
    d_normed_halo = dot(d_halo[...], weight[...], (1, 1))
    out[...] = d_normed
    halo_out[...] = d_normed_halo[HALO - 8 :]
    part = jnp.sum(d_normed * unit_rows(hidden[...])[0], axis=0, keepdims=True)
    part = part + jnp.sum(d_normed_halo * unit_rows(halo[...])[0], axis=0, keepdims=True)
    total[7:8, :D] += part

    @pl.when(pl.program_id(0) == pl.num_programs(0) - 1)
    def _():
        high, low = halves(total[...])
        sums_out[:, CONV:] = jnp.zeros((16, WIDE - CONV), BF)
        sums_out[:, :CONV] = jnp.concatenate(
            [high.astype(F32), low.astype(F32)], axis=0
        ).astype(BF)


def finish(hidden, out_grad, d_normed_in, from_next, gain, grad_out):
    unit, scale = unit_rows(hidden[...])
    tail = jnp.concatenate([jnp.zeros((CH - 8, D), F32), from_next[...]], axis=0)
    d_unit = (d_normed_in[...] + tail) * gain[...]
    grad_out[...] = out_grad[...].astype(F32) + scale * (
        d_unit - unit * jnp.mean(d_unit * unit, axis=-1, keepdims=True)
    )


def tie(*values):
    return lax.optimization_barrier(values)


def after(v, other):
    one = other[tuple(slice(0, 1) for _ in other.shape)].reshape((1,) * v.ndim)
    return jnp.where(one == one, v, jnp.zeros_like(v))


def trade(v, axis, mask):
    return lax.ppermute(v, axis, [(i, i ^ mask) for i in range(lax.axis_size(axis))])


def trade_near(v, first):
    pairs = [(i, i ^ (2 if (i % 2 == 0) == first else 4)) for i in range(lax.axis_size("seq"))]
    return lax.ppermute(v, "seq", pairs)


def paired():
    seq, head = lax.axis_size("seq"), lax.axis_size("head")
    return seq == 8 and head & (head - 1) == 0 and D % (seq * 32) == 0


def half_rows(v, of):
    size = v.shape[0] // 2
    return lax.dynamic_slice_in_dim(v, of * size, size, axis=0)


def gather_head(v):
    count = lax.axis_size("head")
    return lax.all_to_all(
        jnp.concatenate([v] * count, axis=0), "head", split_axis=0, concat_axis=0, tiled=True
    )


def gather_head_by_turns(v):
    count, me = lax.axis_size("head"), lax.axis_index("head")
    parts = [v] + [
        lax.ppermute(v, "head", [(i, (i - k) % count) for i in range(count)])
        for k in range(1, count)
    ]
    return parts


def in_order(parts):
    count, me = lax.axis_size("head"), lax.axis_index("head")
    both = jnp.concatenate(list(parts) * 2, axis=0)
    size = parts[0].shape[0]
    return lax.dynamic_slice_in_dim(both, (count - me) * size, count * size, axis=0)


def gather_core(mine, later):
    core = lax.rem(lax.axis_index("seq"), 2)
    got = trade(half_rows(mine, 1 - core), "seq", 1)
    part = jnp.concatenate([half_rows(mine, core), got], axis=0)
    got, *later = tie(trade_near(part, True), *later)
    part = jnp.concatenate([part, got], axis=0)
    part = jnp.concatenate([part, trade_near(part, False)], axis=0)
    return [part, trade(part, "seq", 1)], later


def add(a, b):
    return (a.astype(F32) + b.astype(F32)).astype(BF)


def fold(kept, got):
    size = kept.shape[0] // 2
    sent = add(kept[size:], got[size:])
    return add(kept[:size], got[:size]), sent


def whole_small(small):
    return small[..., :8, :].astype(F32) + small[..., 8:, :].astype(F32)


def add_small(a, b):
    total = whole_small(a) + whole_small(b)
    high = lax.reduce_precision(total, exponent_bits=8, mantissa_bits=7)
    return jnp.concatenate([high, total - high], axis=0).astype(BF)


def join_cores(kept, got):
    core = lax.rem(lax.axis_index("seq"), 2)
    first, second = jnp.where(core == 0, kept, got), jnp.where(core == 0, got, kept)
    return jnp.concatenate([first, second], axis=0)


def scatter_head_by_turns(part):
    count, me = lax.axis_size("head"), lax.axis_index("head")
    size = part.shape[0] // count
    total = lax.dynamic_slice_in_dim(part, me * size, size, axis=0).astype(F32)
    for k in range(1, count):
        away = lax.dynamic_slice_in_dim(part, lax.rem(me + k, count) * size, size, axis=0)
        got = lax.ppermute(away, "head", [(i, (i + k) % count) for i in range(count)])
        total = total + got.astype(F32)
    return total


def tail(kept, sent, other, other_got, work, rest, trade_rest, last):
    part, sent = fold(kept, trade(sent, "seq", 1))
    d_normed, from_next, small = work(sent)
    other = scatter_head_by_turns(join_cores(other, other_got))
    for near in (False, True):
        size = sent.shape[0]
        got = trade_near(jnp.concatenate([sent, small], axis=0), near)
        if not near:
            got, grad = tie(got, rest(d_normed, from_next))
        small = add_small(small, got[size:])
        part, sent = fold(part, got[:size])
    size = sent.shape[0]
    got = trade(jnp.concatenate([sent, small], axis=0), "seq", 1)
    small = add_small(small, got[size:])
    part = join_cores(part, got[:size])
    part, small, grad, mixed = tie(part, small, trade_rest(grad), last())
    got = lax.all_to_all(part, "head", split_axis=0, concat_axis=0, tiled=True)
    turns = in_order(gather_head_by_turns(small))
    small = jnp.sum(whole_small(turns.reshape((-1,) + small.shape)), axis=0)
    got = got.reshape(lax.axis_size("head"), -1, WIDE).astype(F32)
    return jnp.sum(got, axis=0), other, small, grad, mixed


def per_block(
    body, ins, outs, scratch=(), loose=(), loose_outs=0, reverse=False, micros=1, name=None
):
    blocks = next(v.shape[0] for v in ins if v.ndim == 3)
    free = pl.BlockSpec(memory_space=pl.ANY)

    def spec(shape):
        if len(shape) == 1:
            return pl.BlockSpec(memory_space=pltpu.SMEM)
        if len(shape) == 2:
            return pl.BlockSpec(shape, lambda s: (0, 0))
        return pl.BlockSpec(
            (None,) + tuple(shape[1:]), lambda s: (blocks - 1 - s if reverse else s, 0, 0)
        )

    return pl.pallas_call(
        body,
        grid=(blocks,),
        in_specs=[spec(v.shape) for v in ins] + [free] * len(loose),
        out_specs=[spec(shape) for shape, _ in outs[: len(outs) - loose_outs]]
        + [free] * loose_outs,
        out_shape=[jax.ShapeDtypeStruct(shape, kind) for shape, kind in outs],
        scratch_shapes=list(scratch),
        compiler_params=PARAMS,
        cost_estimate=cost(micros),
        name=name,
    )(*ins, *loose)


def send_states(part, groups, spans):
    sent = lax.all_to_all(
        part, BOTH, split_axis=0, concat_axis=0, tiled=True, axis_index_groups=groups
    )
    return sent.reshape(spans, N // spans, STATE)


def return_states(sent, groups, spans, reverse, later=()):
    rows = N // spans
    width, kind = (DI, BF) if reverse else (STATE, F32)
    if rows % 8 == 0:
        out = pl.pallas_call(
            partial(state_scan, reverse, spans, rows),
            out_shape=jax.ShapeDtypeStruct((spans, rows, width), kind),
            scratch_shapes=[pltpu.VMEM((spans, rows, DI), F32)],
            compiler_params=PARAMS,
            cost_estimate=cost(2),
            name="state_scan",
        )(sent)
    else:
        last = sent[:, :, DI:].astype(F32)
        last = last[..., :H] + last[..., 32 : 32 + H] + last[..., 64 : 64 + H]
        decay = jnp.repeat(jnp.exp(last), P_SIZE, axis=-1)

        def move(carry, at):
            return at[0] * carry + at[1], carry

        _, out = lax.scan(
            move,
            jnp.zeros((rows, DI), F32),
            (decay, sent[:, :, :DI].astype(F32)),
            reverse=reverse,
        )
        if reverse:
            out = out.astype(BF)
        else:
            top = jnp.max(jnp.abs(out), axis=-1, keepdims=True)
            power = jnp.ceil(jnp.log2(jnp.maximum(top, 1e-30)))
            out = jnp.concatenate(
                [out * jnp.exp2(-power), jnp.broadcast_to(power, out.shape[:-1] + (128,))], axis=-1
            )
    if not reverse:
        out = out.astype(jnp.float16)
    out, later = tie(out, later)
    back = lax.all_to_all(
        out.reshape(N, width), BOTH, split_axis=0, concat_axis=0, tiled=True,
        axis_index_groups=groups,
    )
    return back, later


def unscaled(v):
    v = v.astype(F32)
    return v[:, :DI] * jnp.exp2(v[:, DI : DI + 1])


def to_span(v):
    seqs, rows, width = v.shape
    if seqs == 2:
        mine = lax.rem(lax.axis_index("head"), 2)
        got = trade(lax.dynamic_index_in_dim(v, 1 - mine, keepdims=False), "head", 1)

        def join(got):
            keep = lax.dynamic_index_in_dim(v, mine, keepdims=False)
            first, second = jnp.where(mine == 0, keep, got), jnp.where(mine == 0, got, keep)
            return jnp.concatenate([first, second], axis=0).reshape(-1, CH, width)

        return got, join
    groups = [[i + j for j in range(seqs)] for i in range(0, lax.axis_size("head"), seqs)]
    v = lax.all_to_all(
        v, "head", split_axis=0, concat_axis=1, tiled=True, axis_index_groups=groups
    )
    return v, lambda got: got.reshape(-1, CH, width)


def from_span(v, seqs):
    rows = v.shape[0] // seqs
    if seqs == 2:
        mine = lax.rem(lax.axis_index("head"), 2)
        got = trade(half_rows(v, 1 - mine).astype(BF), "head", 1)

        def join(got):
            keep, got = half_rows(v, mine), got.astype(v.dtype)
            return jnp.stack([jnp.where(mine == 0, keep, got), jnp.where(mine == 0, got, keep)])

        return got, join
    groups = [[i + j for j in range(seqs)] for i in range(0, lax.axis_size("head"), seqs)]
    v = v.reshape(1, seqs * rows, v.shape[-1])
    got = lax.all_to_all(
        v, "head", split_axis=1, concat_axis=0, tiled=True, axis_index_groups=groups
    )
    return got, lambda got: got


def pad_lanes(v, width):
    return jnp.pad(v, [(0, 0)] * (v.ndim - 1) + [(0, width - v.shape[-1])])


def gather_rows(v):
    return lax.all_gather(lax.all_gather(v, "head", axis=0, tiled=True), "seq", axis=0, tiled=True)


def scatter_rows(v):
    part = lax.psum_scatter(v, "seq", scatter_dimension=0, tiled=True)
    part = lax.psum_scatter(part, "head", scatter_dimension=0, tiled=True)
    return lax.optimization_barrier(part).astype(F32)


def on_device(
    hidden,
    out_grad,
    norm_gain,
    input_projection_weight,
    conv_weight,
    conv_bias,
    step_bias,
    decay_log,
    skip_weight,
    gate_gain,
    output_projection_weight,
):
    devices = lax.axis_size("seq") * lax.axis_size("head")
    seqs = hidden.shape[0]
    spans = devices // seqs
    groups = [[d for d in range(devices) if d % seqs == r] for r in range(seqs)]
    onward = [(i, i + seqs) for i in range(devices - seqs)]
    backward = [(i + seqs, i) for i in range(devices - seqs)]
    tokens = seqs * hidden.shape[1]
    blocks = tokens // CH

    def tails_before(v):
        if seqs != 2:
            return None
        odd = [d for d in range(devices) if d % 2]
        got = [
            lax.ppermute(
                v[s : s + 1, v.shape[1] - HALO :],
                BOTH,
                [(d, d + 1 + s) for d in odd if d + 1 + s < devices],
            )
            for s in range(2)
        ]
        return got[0] + got[1]

    def with_halo(v, before):
        tails = v[:, CH - HALO :]
        if before is None:
            before = lax.ppermute(tails[-1:], BOTH, onward)
        return jnp.concatenate([before, tails[:-1]], axis=0)

    fast = paired()
    me = lax.axis_index("seq").astype(jnp.int32)[None]
    scan_part = pad_lanes(input_projection_weight[:, DI:], WIDE)
    other_part = jnp.concatenate([input_projection_weight[:, :DI], output_projection_weight], 1)
    before = tails_before(hidden)
    hidden, join_hidden = to_span(hidden)
    if fast:
        pieces, (hidden, other_part) = gather_core(
            gather_head(scan_part), (hidden, other_part)
        )
        conv_bias, *turns = tie(conv_bias, *gather_head_by_turns(other_part))
        other_mine = in_order(turns)
        w_gate, w_out = other_mine[:, :DI], other_mine[:, DI:]
        gate_got, out_got = trade(w_gate, "seq", 2), trade(w_out, "seq", 4)
    else:
        pieces = [gather_rows(scan_part)]
        others = gather_rows(other_part)
        w_gate, w_out = others[:, :DI], others[:, DI:]
    hidden = join_hidden(hidden)
    halo = with_halo(hidden, before)
    out_grad, join_out_grad = to_span(out_grad)
    copies = 16 if fast else 1

    gain_one = norm_gain[None]
    gain_two = gate_gain[None]
    taps = jnp.pad(conv_weight, ((0, 4), (0, 0)))
    offset = conv_bias[None]
    bias = pad_lanes(step_bias[None], 128)
    rate = pad_lanes(-jnp.exp(decay_log)[None], 128)
    skip = jnp.repeat(skip_weight, P_SIZE)[None]

    (
        normed, normed_halo, ext, slope, conv, cum, cumt, step, stept, arg, local, part, w_scan,
    ) = per_block(
        partial(before_scan, len(pieces)),
        [me, hidden, halo, gain_one, taps, offset, bias, rate],
        [
            ((blocks, CH, D), BF),
            ((blocks, HALO, D), BF),
            ((blocks, HALO + CH, CONV), BF),
            ((blocks, CH, CONV), BF),
            ((blocks, CH, CONV), BF),
            ((blocks, CH, 128), F32),
            ((blocks, 32, CH), F32),
            ((blocks, CH, 128), F32),
            ((blocks, 32, CH), F32),
            ((blocks, CH, 128), F32),
            ((blocks, N, DI), F32),
            ((N, STATE), BF),
            ((D, WIDE), BF),
        ],
        [
            pltpu.VMEM((HALO + CH, CONV), F32),
            pltpu.VMEM((D, WIDE), BF),
            pltpu.VMEM((N, DI), F32),
            pltpu.VMEM((8, 128), F32),
            pltpu.SemaphoreType.DMA((copies,)),
            pltpu.SemaphoreType.DMA,
        ],
        loose=pieces,
        loose_outs=1,
        micros=12, name="before_scan",
    )
    if fast:
        cumt, gate_got, out_got = tie(cumt, gate_got, out_got)
        w_gate = jnp.concatenate([w_gate, gate_got], axis=0)
        w_out = jnp.concatenate([w_out, out_got], axis=0)
        ways = (trade(w_gate, "seq", 4), trade(w_out, "seq", 2))
        ways += (trade(w_gate, "seq", 1), trade(w_out, "seq", 1))
    else:
        ways = ()
    (within,) = per_block(
        within_block, [conv, cum, cumt, stept], [((blocks, CH, DI), F32)],
        micros=5, name="within_block",
    )
    sent, within, out_grad, ways = tie(send_states(part, groups, spans), within, out_grad, ways)
    incoming, ways = return_states(sent, groups, spans, False, ways)
    if fast:
        gates = [w_gate, ways[0], ways[2], trade(ways[0], "seq", 1)]
        outs = [w_out, ways[1], ways[3], trade(ways[1], "seq", 1)]
    else:
        gates, outs = [w_gate], [w_out]
    normed_rows = normed.reshape(tokens, D)
    out_grad = join_out_grad(out_grad)
    cotangent = out_grad.reshape(tokens, D)
    gate, d_mixed_in, w_gate, w_out = pl.pallas_call(
        partial(through_others, len(gates)),
        grid=(4,),
        in_specs=[
            pl.BlockSpec(memory_space=pltpu.SMEM),
            pl.BlockSpec((tokens, D), lambda j: (0, 0)),
            pl.BlockSpec((tokens, D), lambda j: (0, 0)),
        ]
        + [pl.BlockSpec(memory_space=pl.ANY)] * (2 * len(gates)),
        out_specs=[
            pl.BlockSpec((tokens, DI // 2), lambda j: (0, jnp.minimum(j, 1))),
            pl.BlockSpec((tokens, DI // 2), lambda j: (0, jnp.maximum(j - 2, 0))),
            pl.BlockSpec(memory_space=pl.ANY),
            pl.BlockSpec(memory_space=pl.ANY),
        ],
        out_shape=[jax.ShapeDtypeStruct((tokens, DI), F32)] * 2
        + [jax.ShapeDtypeStruct((D, DI), BF)] * 2,
        scratch_shapes=[
            pltpu.VMEM((D, DI), BF),
            pltpu.VMEM((D, DI), BF),
            pltpu.SemaphoreType.DMA((2, 8 if fast else 1)),
            pltpu.SemaphoreType.DMA((2,)),
        ],
        compiler_params=PARAMS,
        cost_estimate=cost(8),
        name="through_others",
    )(me, normed_rows, cotangent, *gates, *outs)
    gate, d_mixed_in = gate.reshape(blocks, CH, DI), d_mixed_in.reshape(blocks, CH, DI)

    gate, incoming = tie(gate, incoming)
    incoming = unscaled(incoming)
    mixed_in, d_gate, d_y, dot_y, starts, local_back, part, row_sums = per_block(
        around_norm,
        [within, conv, cum, local, incoming, gate, d_mixed_in, gain_two, skip],
        [
            ((blocks, CH, DI), BF),
            ((blocks, CH, DI), BF),
            ((blocks, CH, DI), BF),
            ((blocks, CH, 128), F32),
            ((blocks, N, DI), F32),
            ((blocks, N, DI), BF),
            ((N, STATE), BF),
            ((8, CONV), F32),
        ],
        [pltpu.VMEM((N, DI), F32), pltpu.VMEM((N, DI), F32), pltpu.VMEM((8, 128), F32)],
        micros=13, name="around_norm",
    )

    mixed_rows = mixed_in.reshape(tokens, DI)
    d_gate_rows = d_gate.reshape(tokens, DI)
    other_terms = pl.pallas_call(
        other_weight_grad,
        grid=(4,),
        in_specs=[
            pl.BlockSpec(memory_space=pltpu.SMEM),
            pl.BlockSpec((tokens, D), lambda j: (0, 0)),
            pl.BlockSpec((tokens, DI // 2), lambda j: (0, jnp.minimum(j, 1))),
            pl.BlockSpec((tokens, D), lambda j: (0, 0)),
            pl.BlockSpec((tokens, DI // 2), lambda j: (0, jnp.maximum(j - 2, 0))),
        ],
        out_specs=[pl.BlockSpec(memory_space=pl.ANY)] * len(pieces),
        out_shape=[jax.ShapeDtypeStruct((D // len(pieces), 2 * DI), BF)] * len(pieces),
        scratch_shapes=[pltpu.VMEM((D, 2 * DI), BF), pltpu.SemaphoreType.DMA((copies,))],
        compiler_params=PARAMS,
        cost_estimate=cost(8),
        name="other_weight_grad",
    )(me, normed_rows, d_gate_rows, cotangent, mixed_rows)
    branch = dot(mixed_rows, w_out, (1, 1))
    mixed = (hidden.reshape(tokens, D).astype(F32) + branch).astype(BF)
    sent, other_terms, mixed, d_y = tie(
        send_states(part, groups, spans), other_terms, mixed, d_y
    )
    incoming, _ = return_states(sent, groups, spans, True)
    if fast:
        other, other_sent = fold(other_terms[0], trade(other_terms[1], "seq", 1))
    else:
        other = other_terms[0]

    dx_within, d_keys, d_queries = per_block(
        within_block_back,
        [conv, cum, cumt, step, d_y, starts],
        [((blocks, CH, DI), F32), ((blocks, CH, N), F32), ((blocks, CH, N), F32)],
        [pltpu.VMEM((CH, CH), F32)],
        micros=9, name="within_block_back",
    )
    if fast:
        got = trade_near(other_sent, False)
    d_scan, d_halo, conv_sums = per_block(
        after_scan,
        [
            conv, slope, ext, cum, step, arg, d_y, dx_within, d_keys, d_queries, dot_y, starts,
            local_back, incoming, skip, rate, taps,
        ],
        [
            ((blocks, CH, WIDE), BF),
            ((blocks, HALO, WIDE), BF),
            ((8, CONV), F32),
        ],
        [
            pltpu.VMEM((HALO + CH + 8, CONV), F32),
            pltpu.VMEM((N, DI), F32),
        ],
        reverse=True,
        micros=16, name="after_scan",
    )

    if fast:
        d_scan, got = tie(d_scan, got)
        other, other_sent = fold(other, got)
        other, other_sent = fold(other, trade_near(other_sent, True))
        other_got = trade(other_sent, "seq", 1)
    mixed, join_mixed = from_span(mixed, seqs)
    mixed, d_scan = tie(mixed, d_scan)
    if not fast:
        mixed = join_mixed(mixed)
    terms = pl.pallas_call(
        partial(scan_weight_grad, len(pieces)),
        in_specs=[pl.BlockSpec(memory_space=pltpu.SMEM)]
        + [pl.BlockSpec(memory_space=pltpu.VMEM)] * 4,
        out_specs=[pl.BlockSpec(memory_space=pl.ANY)] * len(pieces),
        out_shape=[jax.ShapeDtypeStruct((D // len(pieces), WIDE), BF)] * len(pieces),
        scratch_shapes=[pltpu.VMEM((D, WIDE), BF), pltpu.SemaphoreType.DMA((copies,))],
        compiler_params=PARAMS,
        cost_estimate=cost(6),
        name="scan_weight_grad",
    )(
        me,
        normed_rows,
        normed_halo.reshape(blocks * HALO, D),
        d_scan.reshape(tokens, WIDE),
        d_halo.reshape(blocks * HALO, WIDE),
    )

    def to_normed(go):
        d_scan_now = tie(d_scan, go)[0]
        d_normed, d_normed_halo, small = per_block(
            back_to_normed,
            [
                hidden, halo, d_gate, d_scan_now, d_halo, w_gate, w_scan, row_sums, conv_sums,
            ],
            [((blocks, CH, D), F32), ((blocks, 8, D), F32), ((16, WIDE), BF)],
            [pltpu.VMEM((8, CONV), F32)],
            micros=7, name="back_to_normed",
        )
        from_next = lax.ppermute(d_normed_halo[:1], BOTH, backward)
        return d_normed, jnp.concatenate([d_normed_halo[1:], from_next], axis=0), small

    def to_hidden(d_normed, from_next):
        return per_block(
            finish,
            [hidden, out_grad, d_normed, from_next, gain_one],
            [((blocks, CH, D), F32)],
            micros=3, name="finish",
        )[0].reshape(tokens, D)

    def grad_back(grad):
        got, join = from_span(grad, seqs)
        return join(got)

    if fast:
        scan_rows, other_rows, small, hidden_grad, mixed = tail(
            *terms, other, other_got, to_normed, to_hidden, grad_back, lambda: join_mixed(mixed)
        )
    else:
        d_normed, from_next, small = to_normed(jnp.zeros((8, 128), F32))
        other_rows = scatter_rows(other)
        scan_rows = scatter_rows(terms[0])
        small = lax.psum(whole_small(small), BOTH)
        hidden_grad = grad_back(to_hidden(d_normed, from_next))
    small = small[:, :CONV]
    in_rows = jnp.concatenate([other_rows[:, :DI], scan_rows[:, : CONV + H]], axis=1)
    return (
        mixed,
        hidden_grad,
        small[7, :D],
        in_rows,
        small[:KERNEL],
        small[4],
        small[5, DI : DI + H],
        small[5, DI + 128 : DI + 128 + H],
        small[6, :H],
        small[5, :DI],
        other_rows[:, DI:],
    )


def solution(mesh):
    rows = P(None, BOTH, None)
    weight = P(BOTH, None)
    return jax.shard_map(
        on_device,
        mesh=mesh,
        in_specs=(rows, rows, P(), weight, P(), P(), P(), P(), P(), P(), weight),
        out_specs=(rows, rows, P(), weight, P(), P(), P(), P(), P(), P(), weight),
        check_vma=False,
    )
```

```python
from functools import partial

import jax
import jax.numpy as jnp
from jax import lax
from jax.experimental import pallas as pl
from jax.experimental.pallas import tpu as pltpu
from jax.sharding import PartitionSpec as P

D = 768
H = 24
P_SIZE = 64
N = 128
KERNEL = 4
CH = 256
DI = H * P_SIZE
CONV = DI + 2 * N
STEP_AT = CONV
WIDE = CONV + 128
STATE = DI + 128
HALO = 16
EPSILON = 1e-05
BF = jnp.bfloat16
F32 = jnp.float32
BOTH = ("seq", "head")
PARAMS = pltpu.CompilerParams(vmem_limit_bytes=56 * 1024 * 1024)


def cost(micros):
    return pl.CostEstimate(
        flops=int(micros * 1.1e9), bytes_accessed=int(micros * 3e6), transcendentals=0
    )


def dot(a, b, contract=(1, 0)):
    return lax.dot_general(
        a, b, (((contract[0],), (contract[1],)), ((), ())), preferred_element_type=F32
    )


def halves(v):
    high = v.astype(BF)
    return high, (v - high.astype(F32)).astype(BF)


def head_map(rows, period=None):
    row = lax.broadcasted_iota(jnp.int32, (rows, DI), 0)
    col = lax.broadcasted_iota(jnp.int32, (rows, DI), 1)
    if period is not None:
        row = jnp.bitwise_and(row, period - 1)
    return (row == jnp.right_shift(col, 6)).astype(F32).astype(BF)


def spread_heads(v, heads):
    high, low = halves(v)
    return dot(high, heads) + dot(low, heads)


def sum_heads(v, heads):
    high, low = halves(v)
    return dot(high, heads, (1, 1)) + dot(low, heads, (1, 1))


def sigmoid(v):
    return 0.5 * jnp.tanh(0.5 * v) + 0.5


def softplus(v):
    return jnp.maximum(v, 0.0) + jnp.log1p(jnp.exp(-jnp.abs(v)))


def cumulate(v, flip):
    ones = triangle(flip).astype(F32).astype(BF)
    high, rest = halves(v)
    low = (v - high.astype(F32) - rest.astype(F32)).astype(BF)
    return dot(ones, high) + dot(ones, rest) + dot(ones, low)


def triangle(flip):
    row = lax.broadcasted_iota(jnp.int32, (CH, CH), 0)
    col = lax.broadcasted_iota(jnp.int32, (CH, CH), 1)
    return row <= col if flip else row >= col


def last_lanes(last):
    high = last.astype(BF).astype(F32)
    rest = last - high
    mid = rest.astype(BF).astype(F32)
    low = rest - mid
    return high + pltpu.roll(mid, 32, 1) + pltpu.roll(low, 64, 1)


def store_state(out, state, last):
    out[:, :DI] = state.astype(BF)
    out[:, DI:] = jnp.broadcast_to(last_lanes(last), (N, 128)).astype(BF)


def spread_row(v, heads):
    return spread_heads(jnp.broadcast_to(v, (8, 128)), heads)[0:1]


def block_copies(me, pieces, whole, sems, way, outward=False):
    copies = []
    for at, piece in enumerate(pieces):
        if len(pieces) == 1:
            pairs = [(piece, whole)]
        else:
            halved = len(pieces) == 4
            seq = jnp.bitwise_xor(me[0], at // 2 if halved else at)
            late = at % 2 if halved else 0
            core = jnp.bitwise_and(seq, 1)
            near = 2 + 2 * core
            count = (8 if way == "core" else 4) // (2 if halved else 1)
            size = piece.shape[0] // count
            pairs = []
            for k in range(count):
                if way == "core":
                    mask = (k & 1) + ((k >> 1) & 1) * near + ((k >> 2) + late) * (6 - near)
                    row = (jnp.bitwise_xor(seq, mask) * 2 + core) * size
                else:
                    first, second = (2, 4) if way == "x" else (4, 2)
                    row = jnp.bitwise_xor(seq, k * first + late * second) * size
                rows = pl.ds(pl.multiple_of(row, size), size)
                pairs.append((piece.at[pl.ds(k * size, size)], whole.at[rows]))
        for block, rows in pairs:
            pair = (rows, block) if outward else (block, rows)
            copies.append(pltpu.make_async_copy(*pair, sems.at[len(copies)]))
    return copies


def start_all(copies):
    for copy in copies:
        copy.start()


def wait_all(copies):
    for copy in copies:
        copy.wait()


def before_scan(
    count, me, hid, halo, gain, taps, offset, bias, rate, *refs
):
    pieces = refs[:count]
    (
        normed_out, normed_halo_out, ext_out, slope_out, conv_out, cum_out, cumt_out, step_out, stept_out,
        arg_out, local_out, state_out, weight_out,
        ext32, weight, total, total_last, in_sems, out_sem,
    ) = refs[count:]
    keep_weight = pltpu.make_async_copy(weight, weight_out, out_sem)

    @pl.when(pl.program_id(0) == 0)
    def _():
        copies = block_copies(me, pieces, weight, in_sems, "core")
        start_all(copies)
        wait_all(copies)
        keep_weight.start()
        total[...] = jnp.zeros_like(total)
        total_last[...] = jnp.zeros_like(total_last)

    def norm(v):
        v = v.astype(F32)
        scale = lax.rsqrt(jnp.mean(v * v, axis=-1, keepdims=True) + EPSILON)
        return (v * scale * gain[...]).astype(BF)

    rows = norm(hid[...])
    rows_halo = norm(halo[...])
    normed_out[...] = rows
    normed_halo_out[...] = rows_halo
    projected = dot(rows, weight[...])
    projected_halo = dot(rows_halo, weight[:, :CONV])
    low = projected[:, :CONV].astype(BF)
    low_halo = projected_halo.astype(BF)
    ext_out[:HALO] = low_halo
    ext_out[HALO:] = low
    ext32[:HALO] = low_halo.astype(F32)
    ext32[HALO:] = low.astype(F32)
    for at in range(0, CONV, 128):
        cols = slice(at, at + 128)
        pre = offset[:, cols] + taps[0:1, cols] * ext32[HALO - 3 : HALO - 3 + CH, cols]
        for k in range(1, KERNEL):
            pre = pre + taps[k : k + 1, cols] * ext32[HALO - 3 + k : HALO - 3 + k + CH, cols]
        sig = sigmoid(pre)
        act = pre * sig
        conv_out[:, cols] = act.astype(BF)
        slope_out[:, cols] = (sig + act * (1.0 - sig)).astype(BF)
    arg = projected[:, STEP_AT:].astype(BF).astype(F32) + bias[...]
    step = softplus(arg)
    cum = cumulate(step * rate[...], False)
    arg_out[...] = arg
    step_out[...] = step
    stept_out[...] = jnp.transpose(step)[:32]
    cum_out[...] = cum
    cumt_out[...] = jnp.transpose(cum)[:32]
    last = cum[CH - 1 : CH]
    heads = head_map(128)
    w = spread_heads(jnp.exp(last - cum) * step, heads)
    weighted = (conv_out[:, :DI].astype(F32) * w).astype(BF)
    local = dot(conv_out[:, DI : DI + N], weighted, (0, 0))
    local_out[...] = local
    total[...] = total[...] * spread_row(jnp.exp(last), heads) + local
    total_last[...] += jnp.broadcast_to(last, total_last.shape)

    @pl.when(pl.program_id(0) == pl.num_programs(0) - 1)
    def _():
        keep_weight.wait()
        store_state(state_out, total[...], total_last[0:1])


def within_block(conv, cum, cumt, stept, y_out):
    keys = conv[:, DI : DI + N]
    queries = conv[:, DI + N :]
    scores = jnp.where(triangle(False), dot(queries, keys, (1, 1)), 0.0)
    half = CH // 2
    lane = lax.broadcasted_iota(jnp.int32, (half, 128), 1) < P_SIZE
    for pair in range(H // 2):
        cols = slice(pair * 128, pair * 128 + 128)
        for top, width in ((0, half), (half, CH)):
            x = conv[:width, cols]
            parts = []
            for h in (2 * pair, 2 * pair + 1):
                spread = cum[top : top + half, h : h + 1] - cumt[h : h + 1, :width]
                decay = jnp.exp(jnp.minimum(spread, 0.0))
                mixing = scores[top : top + half, :width] * decay * stept[h : h + 1, :width]
                parts.append(dot(mixing.astype(BF), x))
            y_out[top : top + half, cols] = jnp.where(lane, parts[0], parts[1])


def state_scan(reverse, blocks, rows, parts_in, out, decay):
    heads = head_map(128, 32)
    lane = lax.broadcasted_iota(jnp.int32, (blocks * rows, 128), 1)
    last = parts_in[:, :, DI:].reshape(blocks * rows, 128)
    last = jnp.where(lane < 96, last.astype(F32), 0.0).astype(BF)
    decay[...] = jnp.exp(dot(last, heads)).reshape(blocks, rows, DI)
    carry = jnp.zeros((rows, DI), F32)
    for k in range(blocks - 1, -1, -1) if reverse else range(blocks):
        if reverse:
            out[k] = carry.astype(BF)
        else:
            top = jnp.max(jnp.abs(carry), axis=-1, keepdims=True)
            power = jnp.ceil(jnp.log2(jnp.maximum(top, 1e-30)))
            out[k, :, :DI] = carry * jnp.exp2(-power)
            out[k, :, DI:] = jnp.broadcast_to(power, (rows, 128))
        carry = decay[k] * carry + parts_in[k, :, :DI].astype(F32)


def around_norm(
    within, conv, cum, local, incoming, gate, dmi, gain, skip,
    mixed_in_out, d_gate_out, d_y_out, dot_y_out, start_out, local_back_out, state_out, sums_out,
    start, total, total_last,
):
    @pl.when(pl.program_id(0) == 0)
    def _():
        start[...] = incoming[...].astype(F32)
        total[...] = jnp.zeros_like(total)
        total_last[...] = jnp.zeros_like(total_last)
        sums_out[...] = jnp.zeros_like(sums_out)

    start_high, start_low = halves(start[...])
    start_out[...] = start[...]
    heads = head_map(128)
    x = conv[:, :DI].astype(F32)
    queries = conv[:, DI + N :]
    cum_here = cum[...]
    e_cum = spread_heads(jnp.exp(cum_here), heads)
    y_scan = within[...] + (dot(queries, start_high) + dot(queries, start_low)) * e_cum
    y = (y_scan + skip[...] * x).astype(BF).astype(F32)
    gate_here = gate[...]
    sig = sigmoid(gate_here)
    act = gate_here * sig
    gated = y * act
    scale = lax.rsqrt(jnp.mean(gated * gated, axis=-1, keepdims=True) + EPSILON)
    unit = gated * scale
    mixed_in_out[...] = (unit * gain[...]).astype(BF)
    d_mixed_in = dmi[...]
    gain_part = jnp.sum(d_mixed_in * unit, axis=0, keepdims=True)
    d_unit = d_mixed_in * gain[...]
    d_gated = scale * (d_unit - unit * jnp.mean(d_unit * unit, axis=-1, keepdims=True))
    d_y_low = (d_gated * act).astype(BF)
    d_y_out[...] = d_y_low
    d_gate_out[...] = (d_gated * y * (sig * (1.0 + gate_here * (1.0 - sig)))).astype(BF)
    d_y = d_y_low.astype(F32)
    dot_y_out[...] = sum_heads(d_y * y_scan, heads)
    skip_part = jnp.sum(d_y * x, axis=0, keepdims=True)
    sums_out[5:6, :DI] += gain_part
    sums_out[6:7, :128] += sum_heads(jnp.broadcast_to(skip_part, (8, DI)), heads)[0:1]
    scaled, scaled_low = halves(d_y * e_cum)
    local_back = dot(queries, scaled, (0, 0)) + dot(queries, scaled_low, (0, 0))
    local_back_out[...] = local_back.astype(BF)
    last = cum_here[CH - 1 : CH]
    start[...] = start[...] * spread_row(jnp.exp(last), heads) + local[...]
    total[...] += spread_row(jnp.exp(total_last[0:1]), heads) * local_back
    total_last[...] += jnp.broadcast_to(last, total_last.shape)

    @pl.when(pl.program_id(0) == pl.num_programs(0) - 1)
    def _():
        store_state(state_out, total[...], total_last[0:1])


def within_block_back(
    conv, cum, cumt, step, d_y, start, dx_out, d_keys_out, d_queries_out, scores_grad
):
    keys = conv[:, DI : DI + N]
    queries = conv[:, DI + N :]
    scores = jnp.where(triangle(True), dot(keys, queries, (1, 1)), 0.0)
    scores_grad[...] = jnp.zeros_like(scores_grad)
    half = CH // 2
    lane = lax.broadcasted_iota(jnp.int32, (half, 128), 1) < P_SIZE
    for pair in range(H // 2):
        cols = slice(pair * 128, pair * 128 + 128)
        for top, left in ((0, 0), (half, half)):
            x = conv[top : top + half, cols].astype(F32)
            dy = d_y[left:, cols]
            parts, grads = [], None
            for side, h in enumerate((2 * pair, 2 * pair + 1)):
                spread = cumt[h : h + 1, left:] - cum[top : top + half, h : h + 1]
                decay = jnp.exp(jnp.minimum(spread, 0.0)) * step[top : top + half, h : h + 1]
                mixing = (scores[top : top + half, left:] * decay).astype(BF)
                parts.append(dot(mixing, dy))
                x_one = jnp.where(lane if side == 0 else ~lane, x, 0.0).astype(BF)
                d_mixing = dot(x_one, dy, (1, 1))
                grads = d_mixing * decay if grads is None else grads + d_mixing * decay
            scores_grad[top : top + half, left:] += grads
            dx_out[top : top + half, cols] = jnp.where(lane, parts[0], parts[1])
    d_scores = jnp.where(triangle(True), scores_grad[...], 0.0)
    high, low = halves(d_scores)
    d_keys_out[...] = dot(high, queries) + dot(low, queries)
    scaled, scaled_low = halves(
        d_y[...].astype(F32) * spread_heads(jnp.exp(cum[...]), head_map(128))
    )
    start_high, start_low = halves(start[...])
    d_queries_out[...] = (
        dot(high, keys, (0, 0))
        + dot(low, keys, (0, 0))
        + dot(scaled, start_high, (1, 1))
        + dot(scaled_low, start_high, (1, 1))
        + dot(scaled, start_low, (1, 1))
    )


def after_scan(
    conv, slope, ext, cum, step, arg, d_y, dx_within, d_keys_in, d_queries, dot_y, start, local_back,
    incoming, skip, rate, taps,
    d_proj_out, d_halo_out, sums_out, d_pre, after,
):
    @pl.when(pl.program_id(0) == 0)
    def _():
        after[...] = incoming[...].astype(F32)
        sums_out[...] = jnp.zeros_like(sums_out)

    after_high = after[...].astype(BF)
    heads = head_map(128)
    x = conv[:, :DI].astype(F32)
    keys = conv[:, DI : DI + N]
    cum_here = cum[...]
    step_here = step[...]
    last = cum_here[CH - 1 : CH]
    w = spread_heads(jnp.exp(last - cum_here) * step_here, heads)
    weighted = (x * w).astype(BF)
    dx_state = dot(keys, after_high) * w
    d_keys = d_keys_in[...] + dot(weighted, after_high, (1, 1))
    dx_scan = dx_within[...] + dx_state
    sum_scan = sum_heads(x * dx_scan, heads)
    passing = jnp.sum(start[...] * after[...], axis=0, keepdims=True)
    state_part = jnp.sum(x * dx_state, axis=0, keepdims=True)
    rows = jnp.concatenate([passing, state_part, jnp.zeros((6, DI), F32)], axis=0)
    rows = sum_heads(rows, heads)
    d_last = rows[1:2] + jnp.exp(last) * rows[0:1]
    row = lax.broadcasted_iota(jnp.int32, (CH, 128), 0)
    d_cum = dot_y[...] - sum_scan + jnp.where(row == CH - 1, d_last, 0.0)
    later = cumulate(d_cum, True)
    sig = sigmoid(arg[...])
    ratio = jnp.where(step_here > 1e-30, sig / jnp.maximum(step_here, 1e-30), 1.0)
    d_arg = sum_scan * ratio + rate[...] * later * sig
    bias_part = jnp.sum(d_arg, axis=0, keepdims=True)
    decay_part = rate[...] * jnp.sum(step_here * later, axis=0, keepdims=True)

    dx = dx_scan + skip[...] * d_y[...].astype(F32)
    d_pre[:HALO] = jnp.zeros((HALO, CONV), F32)
    d_pre[HALO + CH :] = jnp.zeros((8, CONV), F32)
    for at in range(0, CONV, 128):
        cols = slice(at, at + 128)
        if at < DI:
            d_out = dx[:, cols]
        else:
            d_out = d_keys if at == DI else d_queries[...]
        d_here = d_out * slope[:, cols].astype(F32)
        d_pre[HALO : HALO + CH, cols] = d_here
        inputs = ext[:, cols].astype(F32)
        d_in, sums = None, []
        for k in range(KERNEL):
            shifted = d_pre[3 - k : 3 - k + HALO + CH, cols]
            part = taps[k : k + 1, cols] * shifted
            d_in = part if d_in is None else d_in + part
            sums.append(jnp.sum(shifted * inputs, axis=0, keepdims=True))
        sums.append(jnp.sum(d_here, axis=0, keepdims=True))
        if at < DI:
            sums.append(jnp.zeros((1, 128), F32))
        else:
            sums.append(bias_part if at == DI else decay_part)
        sums.append(jnp.zeros((2, 128), F32))
        sums_out[:, cols] += jnp.concatenate(sums, axis=0)
        d_halo_out[:, cols] = d_in[:HALO].astype(BF)
        d_proj_out[:, cols] = d_in[HALO:].astype(BF)
    d_halo_out[:, STEP_AT:] = jnp.zeros((HALO, 128), BF)
    d_proj_out[:, STEP_AT:] = d_arg.astype(BF)
    after[...] = after[...] * spread_row(jnp.exp(last), heads) + local_back[...].astype(F32)


def scan_weight_grad(count, me, rows, rows_halo, grad, grad_halo, *refs):
    outs, (total, sems) = refs[:count], refs[count:]
    copies = []
    for at, (left, width) in enumerate(((0, 1024), (1024, WIDE - 1024))):
        cols = slice(left, left + width)
        part = dot(rows[...], grad[:, cols], (0, 0))
        part = part + dot(rows_halo[...], grad_halo[:, cols], (0, 0))
        total[:, cols] = part.astype(BF)
        here = pl.ds(left, width)
        step = block_copies(
            me, [out.at[:, here] for out in outs], total.at[:, here], sems.at[at], "core",
            outward=True,
        )
        start_all(step)
        copies += step
    wait_all(copies)


def other_weight_grad(me, normed, d_gate, cotangent, mixed_in, *refs):
    outs, (total, sems) = refs[:-2], refs[-2:]
    step = pl.program_id(0)

    def keep(part):
        cols = pl.ds(pl.multiple_of(step * part.shape[1], 128), part.shape[1])
        total[:, cols] = part.astype(BF)

    @pl.when(step < 2)
    def _():
        keep(dot(normed[...], d_gate[...], (0, 0)))

    @pl.when(step >= 2)
    def _():
        keep(dot(cotangent[...], mixed_in[...], (0, 0)))

    @pl.when(step == 3)
    def _():
        copies = block_copies(me, outs, total, sems, "core", outward=True)
        start_all(copies)
        wait_all(copies)


def through_others(count, me, normed, cotangent, *refs):
    gates, outs, refs = refs[:count], refs[count : 2 * count], refs[2 * count :]
    gate_out, back_out, w_gate_out, w_out_out, w_gate, w_out, in_sems, out_sems = refs
    step = pl.program_id(0)
    gate_in = block_copies(me, gates, w_gate, in_sems.at[0], "x")
    out_in = block_copies(me, outs, w_out, in_sems.at[1], "y")
    keep_gate = pltpu.make_async_copy(w_gate, w_gate_out, out_sems.at[0])
    keep_out = pltpu.make_async_copy(w_out, w_out_out, out_sems.at[1])

    @pl.when(step == 0)
    def _():
        start_all(gate_in)
        start_all(out_in)
        wait_all(gate_in)
        keep_gate.start()

    @pl.when(step == 2)
    def _():
        wait_all(out_in)
        keep_out.start()

    cols = pl.ds(pl.multiple_of((step % 2) * (DI // 2), 128), DI // 2)

    @pl.when(step < 2)
    def _():
        gate_out[...] = dot(normed[...], w_gate[:, cols])

    @pl.when(step >= 2)
    def _():
        back_out[...] = dot(cotangent[...], w_out[:, cols])

    @pl.when(step == 3)
    def _():
        keep_gate.wait()
        keep_out.wait()


def unit_rows(v):
    v = v.astype(F32)
    scale = lax.rsqrt(jnp.mean(v * v, axis=-1, keepdims=True) + EPSILON)
    return v * scale, scale


def back_to_normed(
    hidden, halo, d_gate, d_scan, d_halo, weight_gate, weight, row_sums, conv_sums,
    out, halo_out, sums_out, total,
):
    @pl.when(pl.program_id(0) == 0)
    def _():
        total[...] = row_sums[...] + conv_sums[...]

    d_normed = dot(d_gate[...], weight_gate[...], (1, 1)) + dot(d_scan[...], weight[...], (1, 1))
    d_normed_halo = dot(d_halo[...], weight[...], (1, 1))
    out[...] = d_normed
    halo_out[...] = d_normed_halo[HALO - 8 :]
    part = jnp.sum(d_normed * unit_rows(hidden[...])[0], axis=0, keepdims=True)
    part = part + jnp.sum(d_normed_halo * unit_rows(halo[...])[0], axis=0, keepdims=True)
    total[7:8, :D] += part

    @pl.when(pl.program_id(0) == pl.num_programs(0) - 1)
    def _():
        high, low = halves(total[...])
        sums_out[:, CONV:] = jnp.zeros((16, WIDE - CONV), BF)
        sums_out[:, :CONV] = jnp.concatenate(
            [high.astype(F32), low.astype(F32)], axis=0
        ).astype(BF)


def finish(hidden, out_grad, d_normed_in, from_next, gain, grad_out):
    unit, scale = unit_rows(hidden[...])
    tail = jnp.concatenate([jnp.zeros((CH - 8, D), F32), from_next[...]], axis=0)
    d_unit = (d_normed_in[...] + tail) * gain[...]
    grad_out[...] = out_grad[...].astype(F32) + scale * (
        d_unit - unit * jnp.mean(d_unit * unit, axis=-1, keepdims=True)
    )


def tie(*values):
    return lax.optimization_barrier(values)


def after(v, other):
    one = other[tuple(slice(0, 1) for _ in other.shape)].reshape((1,) * v.ndim)
    return jnp.where(one == one, v, jnp.zeros_like(v))


def trade(v, axis, mask):
    return lax.ppermute(v, axis, [(i, i ^ mask) for i in range(lax.axis_size(axis))])


def trade_near(v, first):
    pairs = [(i, i ^ (2 if (i % 2 == 0) == first else 4)) for i in range(lax.axis_size("seq"))]
    return lax.ppermute(v, "seq", pairs)


def paired():
    seq, head = lax.axis_size("seq"), lax.axis_size("head")
    return seq == 8 and head & (head - 1) == 0 and D % (seq * 32) == 0


def half_rows(v, of):
    size = v.shape[0] // 2
    return lax.dynamic_slice_in_dim(v, of * size, size, axis=0)


def gather_head(v):
    count = lax.axis_size("head")
    return lax.all_to_all(
        jnp.concatenate([v] * count, axis=0), "head", split_axis=0, concat_axis=0, tiled=True
    )


def gather_head_by_turns(v):
    count, me = lax.axis_size("head"), lax.axis_index("head")
    parts = [v] + [
        lax.ppermute(v, "head", [(i, (i - k) % count) for i in range(count)])
        for k in range(1, count)
    ]
    return parts


def in_order(parts):
    count, me = lax.axis_size("head"), lax.axis_index("head")
    both = jnp.concatenate(list(parts) * 2, axis=0)
    size = parts[0].shape[0]
    return lax.dynamic_slice_in_dim(both, (count - me) * size, count * size, axis=0)


def gather_core(mine, later):
    core = lax.rem(lax.axis_index("seq"), 2)
    got = trade(half_rows(mine, 1 - core), "seq", 1)
    part = jnp.concatenate([half_rows(mine, core), got], axis=0)
    got, *later = tie(trade_near(part, True), *later)
    part = jnp.concatenate([part, got], axis=0)
    got = trade_near(part, False)
    return [part, got, trade(part, "seq", 1), trade(got, "seq", 1)], later


def add(a, b):
    return (a.astype(F32) + b.astype(F32)).astype(BF)


def fold(kept, got):
    size = kept.shape[0] // 2
    sent = add(kept[size:], got[size:])
    return add(kept[:size], got[:size]), sent


def whole_small(small):
    return small[..., :8, :].astype(F32) + small[..., 8:, :].astype(F32)


def add_small(a, b):
    total = whole_small(a) + whole_small(b)
    high = lax.reduce_precision(total, exponent_bits=8, mantissa_bits=7)
    return jnp.concatenate([high, total - high], axis=0).astype(BF)


def join_cores(kept, got):
    core = lax.rem(lax.axis_index("seq"), 2)
    first, second = jnp.where(core == 0, kept, got), jnp.where(core == 0, got, kept)
    return jnp.concatenate([first, second], axis=0)


def scatter_head_by_turns(part):
    count, me = lax.axis_size("head"), lax.axis_index("head")
    size = part.shape[0] // count
    total = lax.dynamic_slice_in_dim(part, me * size, size, axis=0).astype(F32)
    for k in range(1, count):
        away = lax.dynamic_slice_in_dim(part, lax.rem(me + k, count) * size, size, axis=0)
        got = lax.ppermute(away, "head", [(i, (i + k) % count) for i in range(count)])
        total = total + got.astype(F32)
    return total


def tail(kept, sent, other, other_got, work, rest, trade_rest, last):
    part, sent = fold(kept, trade(sent, "seq", 1))
    d_normed, from_next, small = work(sent)
    other = scatter_head_by_turns(join_cores(other, other_got))
    for near in (False, True):
        size = sent.shape[0]
        got = trade_near(jnp.concatenate([sent, small], axis=0), near)
        if not near:
            got, grad = tie(got, rest(d_normed, from_next))
        small = add_small(small, got[size:])
        part, sent = fold(part, got[:size])
    size = sent.shape[0]
    got = trade(jnp.concatenate([sent, small], axis=0), "seq", 1)
    small = add_small(small, got[size:])
    part = join_cores(part, got[:size])
    part, small, grad, mixed = tie(part, small, trade_rest(grad), last())
    got = lax.all_to_all(part, "head", split_axis=0, concat_axis=0, tiled=True)
    turns = in_order(gather_head_by_turns(small))
    small = jnp.sum(whole_small(turns.reshape((-1,) + small.shape)), axis=0)
    got = got.reshape(lax.axis_size("head"), -1, WIDE).astype(F32)
    return jnp.sum(got, axis=0), other, small, grad, mixed


def per_block(
    body, ins, outs, scratch=(), loose=(), loose_outs=0, reverse=False, micros=1, name=None
):
    blocks = next(v.shape[0] for v in ins if v.ndim == 3)
    free = pl.BlockSpec(memory_space=pl.ANY)

    def spec(shape):
        if len(shape) == 1:
            return pl.BlockSpec(memory_space=pltpu.SMEM)
        if len(shape) == 2:
            return pl.BlockSpec(shape, lambda s: (0, 0))
        return pl.BlockSpec(
            (None,) + tuple(shape[1:]), lambda s: (blocks - 1 - s if reverse else s, 0, 0)
        )

    return pl.pallas_call(
        body,
        grid=(blocks,),
        in_specs=[spec(v.shape) for v in ins] + [free] * len(loose),
        out_specs=[spec(shape) for shape, _ in outs[: len(outs) - loose_outs]]
        + [free] * loose_outs,
        out_shape=[jax.ShapeDtypeStruct(shape, kind) for shape, kind in outs],
        scratch_shapes=list(scratch),
        compiler_params=PARAMS,
        cost_estimate=cost(micros),
        name=name,
    )(*ins, *loose)


def send_states(part, groups, spans):
    sent = lax.all_to_all(
        part, BOTH, split_axis=0, concat_axis=0, tiled=True, axis_index_groups=groups
    )
    return sent.reshape(spans, N // spans, STATE)


def return_states(sent, groups, spans, reverse, later=()):
    rows = N // spans
    width, kind = (DI, BF) if reverse else (STATE, F32)
    if rows % 8 == 0:
        out = pl.pallas_call(
            partial(state_scan, reverse, spans, rows),
            out_shape=jax.ShapeDtypeStruct((spans, rows, width), kind),
            scratch_shapes=[pltpu.VMEM((spans, rows, DI), F32)],
            compiler_params=PARAMS,
            cost_estimate=cost(2),
            name="state_scan",
        )(sent)
    else:
        last = sent[:, :, DI:].astype(F32)
        last = last[..., :H] + last[..., 32 : 32 + H] + last[..., 64 : 64 + H]
        decay = jnp.repeat(jnp.exp(last), P_SIZE, axis=-1)

        def move(carry, at):
            return at[0] * carry + at[1], carry

        _, out = lax.scan(
            move,
            jnp.zeros((rows, DI), F32),
            (decay, sent[:, :, :DI].astype(F32)),
            reverse=reverse,
        )
        if reverse:
            out = out.astype(BF)
        else:
            top = jnp.max(jnp.abs(out), axis=-1, keepdims=True)
            power = jnp.ceil(jnp.log2(jnp.maximum(top, 1e-30)))
            out = jnp.concatenate(
                [out * jnp.exp2(-power), jnp.broadcast_to(power, out.shape[:-1] + (128,))], axis=-1
            )
    if not reverse:
        out = out.astype(jnp.float16)
    out, later = tie(out, later)
    back = lax.all_to_all(
        out.reshape(N, width), BOTH, split_axis=0, concat_axis=0, tiled=True,
        axis_index_groups=groups,
    )
    return back, later


def unscaled(v):
    v = v.astype(F32)
    return v[:, :DI] * jnp.exp2(v[:, DI : DI + 1])


def to_span(v):
    seqs, rows, width = v.shape
    if seqs == 2:
        mine = lax.rem(lax.axis_index("head"), 2)
        got = trade(lax.dynamic_index_in_dim(v, 1 - mine, keepdims=False), "head", 1)

        def join(got):
            keep = lax.dynamic_index_in_dim(v, mine, keepdims=False)
            first, second = jnp.where(mine == 0, keep, got), jnp.where(mine == 0, got, keep)
            return jnp.concatenate([first, second], axis=0).reshape(-1, CH, width)

        return got, join
    groups = [[i + j for j in range(seqs)] for i in range(0, lax.axis_size("head"), seqs)]
    v = lax.all_to_all(
        v, "head", split_axis=0, concat_axis=1, tiled=True, axis_index_groups=groups
    )
    return v, lambda got: got.reshape(-1, CH, width)


def from_span(v, seqs):
    rows = v.shape[0] // seqs
    if seqs == 2:
        mine = lax.rem(lax.axis_index("head"), 2)
        got = trade(half_rows(v, 1 - mine).astype(BF), "head", 1)

        def join(got):
            keep, got = half_rows(v, mine), got.astype(v.dtype)
            return jnp.stack([jnp.where(mine == 0, keep, got), jnp.where(mine == 0, got, keep)])

        return got, join
    groups = [[i + j for j in range(seqs)] for i in range(0, lax.axis_size("head"), seqs)]
    v = v.reshape(1, seqs * rows, v.shape[-1])
    got = lax.all_to_all(
        v, "head", split_axis=1, concat_axis=0, tiled=True, axis_index_groups=groups
    )
    return got, lambda got: got


def pad_lanes(v, width):
    return jnp.pad(v, [(0, 0)] * (v.ndim - 1) + [(0, width - v.shape[-1])])


def gather_rows(v):
    return lax.all_gather(lax.all_gather(v, "head", axis=0, tiled=True), "seq", axis=0, tiled=True)


def scatter_rows(v):
    part = lax.psum_scatter(v, "seq", scatter_dimension=0, tiled=True)
    part = lax.psum_scatter(part, "head", scatter_dimension=0, tiled=True)
    return lax.optimization_barrier(part).astype(F32)


def on_device(
    hidden,
    out_grad,
    norm_gain,
    input_projection_weight,
    conv_weight,
    conv_bias,
    step_bias,
    decay_log,
    skip_weight,
    gate_gain,
    output_projection_weight,
):
    devices = lax.axis_size("seq") * lax.axis_size("head")
    seqs = hidden.shape[0]
    spans = devices // seqs
    groups = [[d for d in range(devices) if d % seqs == r] for r in range(seqs)]
    onward = [(i, i + seqs) for i in range(devices - seqs)]
    backward = [(i + seqs, i) for i in range(devices - seqs)]
    tokens = seqs * hidden.shape[1]
    blocks = tokens // CH

    def tails_before(v):
        if seqs != 2:
            return None
        odd = [d for d in range(devices) if d % 2]
        got = [
            lax.ppermute(
                v[s : s + 1, v.shape[1] - HALO :],
                BOTH,
                [(d, d + 1 + s) for d in odd if d + 1 + s < devices],
            )
            for s in range(2)
        ]
        return got[0] + got[1]

    def with_halo(v, before):
        tails = v[:, CH - HALO :]
        if before is None:
            before = lax.ppermute(tails[-1:], BOTH, onward)
        return jnp.concatenate([before, tails[:-1]], axis=0)

    fast = paired()
    me = lax.axis_index("seq").astype(jnp.int32)[None]
    scan_part = pad_lanes(input_projection_weight[:, DI:], WIDE)
    other_part = jnp.concatenate([input_projection_weight[:, :DI], output_projection_weight], 1)
    before = tails_before(hidden)
    hidden, join_hidden = to_span(hidden)
    if fast:
        pieces, (hidden, other_part) = gather_core(
            gather_head(scan_part), (hidden, other_part)
        )
        conv_bias, *turns = tie(conv_bias, *gather_head_by_turns(other_part))
        other_mine = in_order(turns)
        w_gate, w_out = other_mine[:, :DI], other_mine[:, DI:]
        gate_got, out_got = trade(w_gate, "seq", 2), trade(w_out, "seq", 4)
    else:
        pieces = [gather_rows(scan_part)]
        others = gather_rows(other_part)
        w_gate, w_out = others[:, :DI], others[:, DI:]
    hidden = join_hidden(hidden)
    halo = with_halo(hidden, before)
    out_grad, join_out_grad = to_span(out_grad)
    copies = 16 if fast else 1
    sides = 2 if fast else 1

    gain_one = norm_gain[None]
    gain_two = gate_gain[None]
    taps = jnp.pad(conv_weight, ((0, 4), (0, 0)))
    offset = conv_bias[None]
    bias = pad_lanes(step_bias[None], 128)
    rate = pad_lanes(-jnp.exp(decay_log)[None], 128)
    skip = jnp.repeat(skip_weight, P_SIZE)[None]

    (
        normed, normed_halo, ext, slope, conv, cum, cumt, step, stept, arg, local, part, w_scan,
    ) = per_block(
        partial(before_scan, len(pieces)),
        [me, hidden, halo, gain_one, taps, offset, bias, rate],
        [
            ((blocks, CH, D), BF),
            ((blocks, HALO, D), BF),
            ((blocks, HALO + CH, CONV), BF),
            ((blocks, CH, CONV), BF),
            ((blocks, CH, CONV), BF),
            ((blocks, CH, 128), F32),
            ((blocks, 32, CH), F32),
            ((blocks, CH, 128), F32),
            ((blocks, 32, CH), F32),
            ((blocks, CH, 128), F32),
            ((blocks, N, DI), F32),
            ((N, STATE), BF),
            ((D, WIDE), BF),
        ],
        [
            pltpu.VMEM((HALO + CH, CONV), F32),
            pltpu.VMEM((D, WIDE), BF),
            pltpu.VMEM((N, DI), F32),
            pltpu.VMEM((8, 128), F32),
            pltpu.SemaphoreType.DMA((copies,)),
            pltpu.SemaphoreType.DMA,
        ],
        loose=pieces,
        loose_outs=1,
        micros=12, name="before_scan",
    )
    if fast:
        cumt, gate_got, out_got = tie(cumt, gate_got, out_got)
        w_gate = jnp.concatenate([w_gate, gate_got], axis=0)
        w_out = jnp.concatenate([w_out, out_got], axis=0)
        ways = (trade(w_gate, "seq", 4), trade(w_out, "seq", 2))
        ways += (trade(w_gate, "seq", 1), trade(w_out, "seq", 1))
    else:
        ways = ()
    (within,) = per_block(
        within_block, [conv, cum, cumt, stept], [((blocks, CH, DI), F32)],
        micros=5, name="within_block",
    )
    sent, within, out_grad, ways = tie(send_states(part, groups, spans), within, out_grad, ways)
    incoming, ways = return_states(sent, groups, spans, False, ways)
    if fast:
        gates = [w_gate, ways[0], ways[2], trade(ways[0], "seq", 1)]
        outs = [w_out, ways[1], ways[3], trade(ways[1], "seq", 1)]
    else:
        gates, outs = [w_gate], [w_out]
    normed_rows = normed.reshape(tokens, D)
    out_grad = join_out_grad(out_grad)
    cotangent = out_grad.reshape(tokens, D)
    gate, d_mixed_in, w_gate, w_out = pl.pallas_call(
        partial(through_others, len(gates)),
        grid=(4,),
        in_specs=[
            pl.BlockSpec(memory_space=pltpu.SMEM),
            pl.BlockSpec((tokens, D), lambda j: (0, 0)),
            pl.BlockSpec((tokens, D), lambda j: (0, 0)),
        ]
        + [pl.BlockSpec(memory_space=pl.ANY)] * (2 * len(gates)),
        out_specs=[
            pl.BlockSpec((tokens, DI // 2), lambda j: (0, jnp.minimum(j, 1))),
            pl.BlockSpec((tokens, DI // 2), lambda j: (0, jnp.maximum(j - 2, 0))),
            pl.BlockSpec(memory_space=pl.ANY),
            pl.BlockSpec(memory_space=pl.ANY),
        ],
        out_shape=[jax.ShapeDtypeStruct((tokens, DI), F32)] * 2
        + [jax.ShapeDtypeStruct((D, DI), BF)] * 2,
        scratch_shapes=[
            pltpu.VMEM((D, DI), BF),
            pltpu.VMEM((D, DI), BF),
            pltpu.SemaphoreType.DMA((2, 8 if fast else 1)),
            pltpu.SemaphoreType.DMA((2,)),
        ],
        compiler_params=PARAMS,
        cost_estimate=cost(8),
        name="through_others",
    )(me, normed_rows, cotangent, *gates, *outs)
    gate, d_mixed_in = gate.reshape(blocks, CH, DI), d_mixed_in.reshape(blocks, CH, DI)

    gate, incoming = tie(gate, incoming)
    incoming = unscaled(incoming)
    mixed_in, d_gate, d_y, dot_y, starts, local_back, part, row_sums = per_block(
        around_norm,
        [within, conv, cum, local, incoming, gate, d_mixed_in, gain_two, skip],
        [
            ((blocks, CH, DI), BF),
            ((blocks, CH, DI), BF),
            ((blocks, CH, DI), BF),
            ((blocks, CH, 128), F32),
            ((blocks, N, DI), F32),
            ((blocks, N, DI), BF),
            ((N, STATE), BF),
            ((8, CONV), F32),
        ],
        [pltpu.VMEM((N, DI), F32), pltpu.VMEM((N, DI), F32), pltpu.VMEM((8, 128), F32)],
        micros=13, name="around_norm",
    )

    mixed_rows = mixed_in.reshape(tokens, DI)
    d_gate_rows = d_gate.reshape(tokens, DI)
    other_terms = pl.pallas_call(
        other_weight_grad,
        grid=(4,),
        in_specs=[
            pl.BlockSpec(memory_space=pltpu.SMEM),
            pl.BlockSpec((tokens, D), lambda j: (0, 0)),
            pl.BlockSpec((tokens, DI // 2), lambda j: (0, jnp.minimum(j, 1))),
            pl.BlockSpec((tokens, D), lambda j: (0, 0)),
            pl.BlockSpec((tokens, DI // 2), lambda j: (0, jnp.maximum(j - 2, 0))),
        ],
        out_specs=[pl.BlockSpec(memory_space=pl.ANY)] * sides,
        out_shape=[jax.ShapeDtypeStruct((D // sides, 2 * DI), BF)] * sides,
        scratch_shapes=[pltpu.VMEM((D, 2 * DI), BF), pltpu.SemaphoreType.DMA((copies,))],
        compiler_params=PARAMS,
        cost_estimate=cost(8),
        name="other_weight_grad",
    )(me, normed_rows, d_gate_rows, cotangent, mixed_rows)
    branch = dot(mixed_rows, w_out, (1, 1))
    mixed = (hidden.reshape(tokens, D).astype(F32) + branch).astype(BF)
    sent, other_terms, mixed, d_y = tie(
        send_states(part, groups, spans), other_terms, mixed, d_y
    )
    incoming, _ = return_states(sent, groups, spans, True)
    if fast:
        other, other_sent = fold(other_terms[0], trade(other_terms[1], "seq", 1))
    else:
        other = other_terms[0]

    dx_within, d_keys, d_queries = per_block(
        within_block_back,
        [conv, cum, cumt, step, d_y, starts],
        [((blocks, CH, DI), F32), ((blocks, CH, N), F32), ((blocks, CH, N), F32)],
        [pltpu.VMEM((CH, CH), F32)],
        micros=9, name="within_block_back",
    )
    if fast:
        got = trade_near(other_sent, False)
    d_scan, d_halo, conv_sums = per_block(
        after_scan,
        [
            conv, slope, ext, cum, step, arg, d_y, dx_within, d_keys, d_queries, dot_y, starts,
            local_back, incoming, skip, rate, taps,
        ],
        [
            ((blocks, CH, WIDE), BF),
            ((blocks, HALO, WIDE), BF),
            ((8, CONV), F32),
        ],
        [
            pltpu.VMEM((HALO + CH + 8, CONV), F32),
            pltpu.VMEM((N, DI), F32),
        ],
        reverse=True,
        micros=16, name="after_scan",
    )

    if fast:
        d_scan, got = tie(d_scan, got)
        other, other_sent = fold(other, got)
        other, other_sent = fold(other, trade_near(other_sent, True))
        other_got = trade(other_sent, "seq", 1)
    mixed, join_mixed = from_span(mixed, seqs)
    mixed, d_scan = tie(mixed, d_scan)
    if not fast:
        mixed = join_mixed(mixed)
    terms = pl.pallas_call(
        partial(scan_weight_grad, sides),
        in_specs=[pl.BlockSpec(memory_space=pltpu.SMEM)]
        + [pl.BlockSpec(memory_space=pltpu.VMEM)] * 4,
        out_specs=[pl.BlockSpec(memory_space=pl.ANY)] * sides,
        out_shape=[jax.ShapeDtypeStruct((D // sides, WIDE), BF)] * sides,
        scratch_shapes=[pltpu.VMEM((D, WIDE), BF), pltpu.SemaphoreType.DMA((2, copies))],
        compiler_params=PARAMS,
        cost_estimate=cost(6),
        name="scan_weight_grad",
    )(
        me,
        normed_rows,
        normed_halo.reshape(blocks * HALO, D),
        d_scan.reshape(tokens, WIDE),
        d_halo.reshape(blocks * HALO, WIDE),
    )

    def to_normed(go):
        d_scan_now = tie(d_scan, go)[0]
        d_normed, d_normed_halo, small = per_block(
            back_to_normed,
            [
                hidden, halo, d_gate, d_scan_now, d_halo, w_gate, w_scan, row_sums, conv_sums,
            ],
            [((blocks, CH, D), F32), ((blocks, 8, D), F32), ((16, WIDE), BF)],
            [pltpu.VMEM((8, CONV), F32)],
            micros=7, name="back_to_normed",
        )
        from_next = lax.ppermute(d_normed_halo[:1], BOTH, backward)
        return d_normed, jnp.concatenate([d_normed_halo[1:], from_next], axis=0), small

    def to_hidden(d_normed, from_next):
        return per_block(
            finish,
            [hidden, out_grad, d_normed, from_next, gain_one],
            [((blocks, CH, D), F32)],
            micros=3, name="finish",
        )[0].reshape(tokens, D)

    def grad_back(grad):
        got, join = from_span(grad, seqs)
        return join(got)

    if fast:
        scan_rows, other_rows, small, hidden_grad, mixed = tail(
            *terms, other, other_got, to_normed, to_hidden, grad_back, lambda: join_mixed(mixed)
        )
    else:
        d_normed, from_next, small = to_normed(jnp.zeros((8, 128), F32))
        other_rows = scatter_rows(other)
        scan_rows = scatter_rows(terms[0])
        small = lax.psum(whole_small(small), BOTH)
        hidden_grad = grad_back(to_hidden(d_normed, from_next))
    small = small[:, :CONV]
    in_rows = jnp.concatenate([other_rows[:, :DI], scan_rows[:, : CONV + H]], axis=1)
    return (
        mixed,
        hidden_grad,
        small[7, :D],
        in_rows,
        small[:KERNEL],
        small[4],
        small[5, DI : DI + H],
        small[5, DI + 128 : DI + 128 + H],
        small[6, :H],
        small[5, :DI],
        other_rows[:, DI:],
    )


def solution(mesh):
    rows = P(None, BOTH, None)
    weight = P(BOTH, None)
    return jax.shard_map(
        on_device,
        mesh=mesh,
        in_specs=(rows, rows, P(), weight, P(), P(), P(), P(), P(), P(), weight),
        out_specs=(rows, rows, P(), weight, P(), P(), P(), P(), P(), P(), weight),
        check_vma=False,
    )
```

```python
from functools import partial

import jax
import jax.numpy as jnp
from jax import lax
from jax.experimental import pallas as pl
from jax.experimental.pallas import tpu as pltpu
from jax.sharding import PartitionSpec as P

D = 768
H = 24
P_SIZE = 64
N = 128
KERNEL = 4
CH = 256
DI = H * P_SIZE
CONV = DI + 2 * N
STEP_AT = CONV
WIDE = CONV + 128
STATE = DI + 128
HALO = 16
EPSILON = 1e-05
BF = jnp.bfloat16
F32 = jnp.float32
BOTH = ("seq", "head")
PARAMS = pltpu.CompilerParams(vmem_limit_bytes=56 * 1024 * 1024)


def cost(micros):
    return pl.CostEstimate(
        flops=int(micros * 1.1e9), bytes_accessed=int(micros * 3e6), transcendentals=0
    )


def dot(a, b, contract=(1, 0)):
    return lax.dot_general(
        a, b, (((contract[0],), (contract[1],)), ((), ())), preferred_element_type=F32
    )


def halves(v):
    high = v.astype(BF)
    return high, (v - high.astype(F32)).astype(BF)


def head_map(rows, period=None):
    row = lax.broadcasted_iota(jnp.int32, (rows, DI), 0)
    col = lax.broadcasted_iota(jnp.int32, (rows, DI), 1)
    if period is not None:
        row = jnp.bitwise_and(row, period - 1)
    return (row == jnp.right_shift(col, 6)).astype(F32).astype(BF)


def spread_heads(v, heads):
    high, low = halves(v)
    return dot(high, heads) + dot(low, heads)


def sum_heads(v, heads):
    high, low = halves(v)
    return dot(high, heads, (1, 1)) + dot(low, heads, (1, 1))


def sigmoid(v):
    return 0.5 * jnp.tanh(0.5 * v) + 0.5


def softplus(v):
    return jnp.maximum(v, 0.0) + jnp.log1p(jnp.exp(-jnp.abs(v)))


def cumulate(v, flip):
    ones = triangle(flip).astype(F32).astype(BF)
    high, rest = halves(v)
    low = (v - high.astype(F32) - rest.astype(F32)).astype(BF)
    return dot(ones, high) + dot(ones, rest) + dot(ones, low)


def triangle(flip):
    row = lax.broadcasted_iota(jnp.int32, (CH, CH), 0)
    col = lax.broadcasted_iota(jnp.int32, (CH, CH), 1)
    return row <= col if flip else row >= col


def last_lanes(last):
    high = last.astype(BF).astype(F32)
    rest = last - high
    mid = rest.astype(BF).astype(F32)
    low = rest - mid
    return high + pltpu.roll(mid, 32, 1) + pltpu.roll(low, 64, 1)


def store_state(out, state, last):
    out[:, :DI] = state.astype(BF)
    out[:, DI:] = jnp.broadcast_to(last_lanes(last), (N, 128)).astype(BF)


def spread_row(v, heads):
    return spread_heads(jnp.broadcast_to(v, (8, 128)), heads)[0:1]


def block_copies(me, pieces, whole, sems, way, outward=False):
    copies = []
    for at, piece in enumerate(pieces):
        if len(pieces) == 1:
            pairs = [(piece, whole)]
        else:
            halved = len(pieces) == 4
            seq = jnp.bitwise_xor(me[0], at // 2 if halved else at)
            late = at % 2 if halved else 0
            core = jnp.bitwise_and(seq, 1)
            near = 2 + 2 * core
            count = (8 if way == "core" else 4) // (2 if halved else 1)
            size = piece.shape[0] // count
            pairs = []
            for k in range(count):
                if way == "core":
                    mask = (k & 1) + ((k >> 1) & 1) * near + ((k >> 2) + late) * (6 - near)
                    row = (jnp.bitwise_xor(seq, mask) * 2 + core) * size
                else:
                    first, second = (2, 4) if way == "x" else (4, 2)
                    row = jnp.bitwise_xor(seq, k * first + late * second) * size
                rows = pl.ds(pl.multiple_of(row, size), size)
                pairs.append((piece.at[pl.ds(k * size, size)], whole.at[rows]))
        for block, rows in pairs:
            pair = (rows, block) if outward else (block, rows)
            copies.append(pltpu.make_async_copy(*pair, sems.at[len(copies)]))
    return copies


def start_all(copies):
    for copy in copies:
        copy.start()


def wait_all(copies):
    for copy in copies:
        copy.wait()


def before_scan(
    count, me, hid, halo, gain, taps, offset, bias, rate, *refs
):
    pieces = refs[:count]
    (
        normed_out, normed_halo_out, ext_out, slope_out, conv_out, cum_out, cumt_out, step_out, stept_out,
        arg_out, local_out, state_out, weight_out,
        ext32, weight, total, total_last, in_sems, out_sem,
    ) = refs[count:]
    keep_weight = pltpu.make_async_copy(weight, weight_out, out_sem)

    @pl.when(pl.program_id(0) == 0)
    def _():
        copies = block_copies(me, pieces, weight, in_sems, "core")
        start_all(copies)
        wait_all(copies)
        keep_weight.start()
        total[...] = jnp.zeros_like(total)
        total_last[...] = jnp.zeros_like(total_last)

    def norm(v):
        v = v.astype(F32)
        scale = lax.rsqrt(jnp.mean(v * v, axis=-1, keepdims=True) + EPSILON)
        return (v * scale * gain[...]).astype(BF)

    rows = norm(hid[...])
    rows_halo = norm(halo[...])
    normed_out[...] = rows
    normed_halo_out[...] = rows_halo
    projected = dot(rows, weight[...])
    projected_halo = dot(rows_halo, weight[:, :CONV])
    low = projected[:, :CONV].astype(BF)
    low_halo = projected_halo.astype(BF)
    ext_out[:HALO] = low_halo
    ext_out[HALO:] = low
    ext32[:HALO] = low_halo.astype(F32)
    ext32[HALO:] = low.astype(F32)
    for at in range(0, CONV, 128):
        cols = slice(at, at + 128)
        pre = offset[:, cols] + taps[0:1, cols] * ext32[HALO - 3 : HALO - 3 + CH, cols]
        for k in range(1, KERNEL):
            pre = pre + taps[k : k + 1, cols] * ext32[HALO - 3 + k : HALO - 3 + k + CH, cols]
        sig = sigmoid(pre)
        act = pre * sig
        conv_out[:, cols] = act.astype(BF)
        slope_out[:, cols] = (sig + act * (1.0 - sig)).astype(BF)
    arg = projected[:, STEP_AT:].astype(BF).astype(F32) + bias[...]
    step = softplus(arg)
    cum = cumulate(step * rate[...], False)
    arg_out[...] = arg
    step_out[...] = step
    stept_out[...] = jnp.transpose(step)[:32]
    cum_out[...] = cum
    cumt_out[...] = jnp.transpose(cum)[:32]
    last = cum[CH - 1 : CH]
    heads = head_map(128)
    w = spread_heads(jnp.exp(last - cum) * step, heads)
    weighted = (conv_out[:, :DI].astype(F32) * w).astype(BF)
    local = dot(conv_out[:, DI : DI + N], weighted, (0, 0))
    local_out[...] = local.astype(BF)
    total[...] = total[...] * spread_row(jnp.exp(last), heads) + local
    total_last[...] += jnp.broadcast_to(last, total_last.shape)

    @pl.when(pl.program_id(0) == pl.num_programs(0) - 1)
    def _():
        keep_weight.wait()
        store_state(state_out, total[...], total_last[0:1])


def within_block(conv, cum, cumt, stept, y_out):
    keys = conv[:, DI : DI + N]
    queries = conv[:, DI + N :]
    scores = jnp.where(triangle(False), dot(queries, keys, (1, 1)), 0.0)
    half = CH // 2
    lane = lax.broadcasted_iota(jnp.int32, (half, 128), 1) < P_SIZE
    for pair in range(H // 2):
        cols = slice(pair * 128, pair * 128 + 128)
        for top, width in ((0, half), (half, CH)):
            x = conv[:width, cols]
            parts = []
            for h in (2 * pair, 2 * pair + 1):
                spread = cum[top : top + half, h : h + 1] - cumt[h : h + 1, :width]
                decay = jnp.exp(jnp.minimum(spread, 0.0))
                mixing = scores[top : top + half, :width] * decay * stept[h : h + 1, :width]
                parts.append(dot(mixing.astype(BF), x))
            y_out[top : top + half, cols] = jnp.where(lane, parts[0], parts[1])


def state_scan(reverse, blocks, rows, parts_in, out, decay):
    heads = head_map(128, 32)
    lane = lax.broadcasted_iota(jnp.int32, (blocks * rows, 128), 1)
    last = parts_in[:, :, DI:].reshape(blocks * rows, 128)
    last = jnp.where(lane < 96, last.astype(F32), 0.0).astype(BF)
    decay[...] = jnp.exp(dot(last, heads)).reshape(blocks, rows, DI)
    carry = jnp.zeros((rows, DI), F32)
    for k in range(blocks - 1, -1, -1) if reverse else range(blocks):
        if reverse:
            out[k] = carry.astype(BF)
        else:
            top = jnp.max(jnp.abs(carry), axis=-1, keepdims=True)
            power = jnp.ceil(jnp.log2(jnp.maximum(top, 1e-30)))
            out[k, :, :DI] = carry * jnp.exp2(-power)
            out[k, :, DI:] = jnp.broadcast_to(power, (rows, 128))
        carry = decay[k] * carry + parts_in[k, :, :DI].astype(F32)


def around_norm(
    within, conv, cum, local, incoming, gate, dmi, gain, skip,
    mixed_in_out, d_gate_out, d_y_out, dot_y_out, start_out, local_back_out, state_out, sums_out,
    start, total, total_last,
):
    @pl.when(pl.program_id(0) == 0)
    def _():
        start[...] = incoming[...].astype(F32)
        total[...] = jnp.zeros_like(total)
        total_last[...] = jnp.zeros_like(total_last)
        sums_out[...] = jnp.zeros_like(sums_out)

    start_high, start_low = halves(start[...])
    start_out[...] = start[...]
    heads = head_map(128)
    x = conv[:, :DI].astype(F32)
    queries = conv[:, DI + N :]
    cum_here = cum[...]
    e_cum = spread_heads(jnp.exp(cum_here), heads)
    y_scan = within[...] + (dot(queries, start_high) + dot(queries, start_low)) * e_cum
    y = (y_scan + skip[...] * x).astype(BF).astype(F32)
    gate_here = gate[...]
    sig = sigmoid(gate_here)
    act = gate_here * sig
    gated = y * act
    scale = lax.rsqrt(jnp.mean(gated * gated, axis=-1, keepdims=True) + EPSILON)
    unit = gated * scale
    mixed_in_out[...] = (unit * gain[...]).astype(BF)
    d_mixed_in = dmi[...]
    gain_part = jnp.sum(d_mixed_in * unit, axis=0, keepdims=True)
    d_unit = d_mixed_in * gain[...]
    d_gated = scale * (d_unit - unit * jnp.mean(d_unit * unit, axis=-1, keepdims=True))
    d_y_low = (d_gated * act).astype(BF)
    d_y_out[...] = d_y_low
    d_gate_out[...] = (d_gated * y * (sig * (1.0 + gate_here * (1.0 - sig)))).astype(BF)
    d_y = d_y_low.astype(F32)
    dot_y_out[...] = sum_heads(d_y * y_scan, heads)
    skip_part = jnp.sum(d_y * x, axis=0, keepdims=True)
    sums_out[5:6, :DI] += gain_part
    sums_out[6:7, :128] += sum_heads(jnp.broadcast_to(skip_part, (8, DI)), heads)[0:1]
    scaled, scaled_low = halves(d_y * e_cum)
    local_back = dot(queries, scaled, (0, 0)) + dot(queries, scaled_low, (0, 0))
    local_back_out[...] = local_back.astype(BF)
    last = cum_here[CH - 1 : CH]
    start[...] = start[...] * spread_row(jnp.exp(last), heads) + local[...].astype(F32)
    total[...] += spread_row(jnp.exp(total_last[0:1]), heads) * local_back
    total_last[...] += jnp.broadcast_to(last, total_last.shape)

    @pl.when(pl.program_id(0) == pl.num_programs(0) - 1)
    def _():
        store_state(state_out, total[...], total_last[0:1])


def within_block_back(
    conv, cum, cumt, step, d_y, start, dx_out, d_keys_out, d_queries_out, scores_grad
):
    keys = conv[:, DI : DI + N]
    queries = conv[:, DI + N :]
    scores = jnp.where(triangle(True), dot(keys, queries, (1, 1)), 0.0)
    scores_grad[...] = jnp.zeros_like(scores_grad)
    half = CH // 2
    lane = lax.broadcasted_iota(jnp.int32, (half, 128), 1) < P_SIZE
    for pair in range(H // 2):
        cols = slice(pair * 128, pair * 128 + 128)
        for top, left in ((0, 0), (half, half)):
            x = conv[top : top + half, cols].astype(F32)
            dy = d_y[left:, cols]
            parts, grads = [], None
            for side, h in enumerate((2 * pair, 2 * pair + 1)):
                spread = cumt[h : h + 1, left:] - cum[top : top + half, h : h + 1]
                decay = jnp.exp(jnp.minimum(spread, 0.0)) * step[top : top + half, h : h + 1]
                mixing = (scores[top : top + half, left:] * decay).astype(BF)
                parts.append(dot(mixing, dy))
                x_one = jnp.where(lane if side == 0 else ~lane, x, 0.0).astype(BF)
                d_mixing = dot(x_one, dy, (1, 1))
                grads = d_mixing * decay if grads is None else grads + d_mixing * decay
            scores_grad[top : top + half, left:] += grads
            dx_out[top : top + half, cols] = jnp.where(lane, parts[0], parts[1])
    d_scores = jnp.where(triangle(True), scores_grad[...], 0.0)
    high, low = halves(d_scores)
    d_keys_out[...] = dot(high, queries) + dot(low, queries)
    scaled, scaled_low = halves(
        d_y[...].astype(F32) * spread_heads(jnp.exp(cum[...]), head_map(128))
    )
    start_high, start_low = halves(start[...])
    d_queries_out[...] = (
        dot(high, keys, (0, 0))
        + dot(low, keys, (0, 0))
        + dot(scaled, start_high, (1, 1))
        + dot(scaled_low, start_high, (1, 1))
        + dot(scaled, start_low, (1, 1))
    )


def after_scan(
    conv, slope, ext, cum, step, arg, d_y, dx_within, d_keys_in, d_queries, dot_y, start, local_back,
    incoming, skip, rate, taps,
    d_proj_out, d_halo_out, sums_out, d_pre, after,
):
    @pl.when(pl.program_id(0) == 0)
    def _():
        after[...] = incoming[...].astype(F32)
        sums_out[...] = jnp.zeros_like(sums_out)

    after_high = after[...].astype(BF)
    heads = head_map(128)
    x = conv[:, :DI].astype(F32)
    keys = conv[:, DI : DI + N]
    cum_here = cum[...]
    step_here = step[...]
    last = cum_here[CH - 1 : CH]
    w = spread_heads(jnp.exp(last - cum_here) * step_here, heads)
    weighted = (x * w).astype(BF)
    dx_state = dot(keys, after_high) * w
    d_keys = d_keys_in[...] + dot(weighted, after_high, (1, 1))
    dx_scan = dx_within[...] + dx_state
    sum_scan = sum_heads(x * dx_scan, heads)
    passing = jnp.sum(start[...] * after[...], axis=0, keepdims=True)
    state_part = jnp.sum(x * dx_state, axis=0, keepdims=True)
    rows = jnp.concatenate([passing, state_part, jnp.zeros((6, DI), F32)], axis=0)
    rows = sum_heads(rows, heads)
    d_last = rows[1:2] + jnp.exp(last) * rows[0:1]
    row = lax.broadcasted_iota(jnp.int32, (CH, 128), 0)
    d_cum = dot_y[...] - sum_scan + jnp.where(row == CH - 1, d_last, 0.0)
    later = cumulate(d_cum, True)
    sig = sigmoid(arg[...])
    ratio = jnp.where(step_here > 1e-30, sig / jnp.maximum(step_here, 1e-30), 1.0)
    d_arg = sum_scan * ratio + rate[...] * later * sig
    bias_part = jnp.sum(d_arg, axis=0, keepdims=True)
    decay_part = rate[...] * jnp.sum(step_here * later, axis=0, keepdims=True)

    dx = dx_scan + skip[...] * d_y[...].astype(F32)
    d_pre[:HALO] = jnp.zeros((HALO, CONV), F32)
    d_pre[HALO + CH :] = jnp.zeros((8, CONV), F32)
    for at in range(0, CONV, 128):
        cols = slice(at, at + 128)
        if at < DI:
            d_out = dx[:, cols]
        else:
            d_out = d_keys if at == DI else d_queries[...]
        d_here = d_out * slope[:, cols].astype(F32)
        d_pre[HALO : HALO + CH, cols] = d_here
        inputs = ext[:, cols].astype(F32)
        d_in, sums = None, []
        for k in range(KERNEL):
            shifted = d_pre[3 - k : 3 - k + HALO + CH, cols]
            part = taps[k : k + 1, cols] * shifted
            d_in = part if d_in is None else d_in + part
            sums.append(jnp.sum(shifted * inputs, axis=0, keepdims=True))
        sums.append(jnp.sum(d_here, axis=0, keepdims=True))
        if at < DI:
            sums.append(jnp.zeros((1, 128), F32))
        else:
            sums.append(bias_part if at == DI else decay_part)
        sums.append(jnp.zeros((2, 128), F32))
        sums_out[:, cols] += jnp.concatenate(sums, axis=0)
        d_halo_out[:, cols] = d_in[:HALO].astype(BF)
        d_proj_out[:, cols] = d_in[HALO:].astype(BF)
    d_halo_out[:, STEP_AT:] = jnp.zeros((HALO, 128), BF)
    d_proj_out[:, STEP_AT:] = d_arg.astype(BF)
    after[...] = after[...] * spread_row(jnp.exp(last), heads) + local_back[...].astype(F32)


def scan_weight_grad(count, me, rows, rows_halo, grad, grad_halo, *refs):
    outs, (total, sems) = refs[:count], refs[count:]
    copies = []
    for at, (left, width) in enumerate(((0, 1024), (1024, WIDE - 1024))):
        cols = slice(left, left + width)
        part = dot(rows[...], grad[:, cols], (0, 0))
        part = part + dot(rows_halo[...], grad_halo[:, cols], (0, 0))
        total[:, cols] = part.astype(BF)
        here = pl.ds(left, width)
        step = block_copies(
            me, [out.at[:, here] for out in outs], total.at[:, here], sems.at[at], "core",
            outward=True,
        )
        start_all(step)
        copies += step
    wait_all(copies)


def other_weight_grad(me, normed, d_gate, cotangent, mixed_in, *refs):
    outs, (total, sems) = refs[:-2], refs[-2:]
    step = pl.program_id(0)

    def keep(part):
        cols = pl.ds(pl.multiple_of(step * part.shape[1], 128), part.shape[1])
        total[:, cols] = part.astype(BF)

    @pl.when(step < 2)
    def _():
        keep(dot(normed[...], d_gate[...], (0, 0)))

    @pl.when(step >= 2)
    def _():
        keep(dot(cotangent[...], mixed_in[...], (0, 0)))

    @pl.when(step == 3)
    def _():
        copies = block_copies(me, outs, total, sems, "core", outward=True)
        start_all(copies)
        wait_all(copies)


def through_others(count, me, normed, cotangent, *refs):
    gates, outs, refs = refs[:count], refs[count : 2 * count], refs[2 * count :]
    gate_out, back_out, w_gate_out, w_out_out, w_gate, w_out, in_sems, out_sems = refs
    step = pl.program_id(0)
    gate_in = block_copies(me, gates, w_gate, in_sems.at[0], "x")
    out_in = block_copies(me, outs, w_out, in_sems.at[1], "y")
    keep_gate = pltpu.make_async_copy(w_gate, w_gate_out, out_sems.at[0])
    keep_out = pltpu.make_async_copy(w_out, w_out_out, out_sems.at[1])

    @pl.when(step == 0)
    def _():
        start_all(gate_in)
        start_all(out_in)
        wait_all(gate_in)
        keep_gate.start()

    @pl.when(step == 2)
    def _():
        wait_all(out_in)
        keep_out.start()

    cols = pl.ds(pl.multiple_of((step % 2) * (DI // 2), 128), DI // 2)

    @pl.when(step < 2)
    def _():
        gate_out[...] = dot(normed[...], w_gate[:, cols])

    @pl.when(step >= 2)
    def _():
        back_out[...] = dot(cotangent[...], w_out[:, cols])

    @pl.when(step == 3)
    def _():
        keep_gate.wait()
        keep_out.wait()


def unit_rows(v):
    v = v.astype(F32)
    scale = lax.rsqrt(jnp.mean(v * v, axis=-1, keepdims=True) + EPSILON)
    return v * scale, scale


def back_to_normed(
    hidden, halo, d_gate, d_scan, d_halo, weight_gate, weight, row_sums, conv_sums,
    out, halo_out, sums_out, total,
):
    @pl.when(pl.program_id(0) == 0)
    def _():
        total[...] = row_sums[...] + conv_sums[...]

    d_normed = dot(d_gate[...], weight_gate[...], (1, 1)) + dot(d_scan[...], weight[...], (1, 1))
    d_normed_halo = dot(d_halo[...], weight[...], (1, 1))
    out[...] = d_normed
    halo_out[...] = d_normed_halo[HALO - 8 :]
    part = jnp.sum(d_normed * unit_rows(hidden[...])[0], axis=0, keepdims=True)
    part = part + jnp.sum(d_normed_halo * unit_rows(halo[...])[0], axis=0, keepdims=True)
    total[7:8, :D] += part

    @pl.when(pl.program_id(0) == pl.num_programs(0) - 1)
    def _():
        high, low = halves(total[...])
        sums_out[:, CONV:] = jnp.zeros((16, WIDE - CONV), BF)
        sums_out[:, :CONV] = jnp.concatenate(
            [high.astype(F32), low.astype(F32)], axis=0
        ).astype(BF)


def finish(hidden, out_grad, d_normed_in, from_next, gain, grad_out):
    unit, scale = unit_rows(hidden[...])
    tail = jnp.concatenate([jnp.zeros((CH - 8, D), F32), from_next[...]], axis=0)
    d_unit = (d_normed_in[...] + tail) * gain[...]
    grad_out[...] = out_grad[...].astype(F32) + scale * (
        d_unit - unit * jnp.mean(d_unit * unit, axis=-1, keepdims=True)
    )


def tie(*values):
    return lax.optimization_barrier(values)


def after(v, other):
    one = other[tuple(slice(0, 1) for _ in other.shape)].reshape((1,) * v.ndim)
    return jnp.where(one == one, v, jnp.zeros_like(v))


def trade(v, axis, mask):
    return lax.ppermute(v, axis, [(i, i ^ mask) for i in range(lax.axis_size(axis))])


def trade_near(v, first):
    pairs = [(i, i ^ (2 if (i % 2 == 0) == first else 4)) for i in range(lax.axis_size("seq"))]
    return lax.ppermute(v, "seq", pairs)


def paired():
    seq, head = lax.axis_size("seq"), lax.axis_size("head")
    return seq == 8 and head & (head - 1) == 0 and D % (seq * 32) == 0


def half_rows(v, of):
    size = v.shape[0] // 2
    return lax.dynamic_slice_in_dim(v, of * size, size, axis=0)


def gather_head(v):
    count = lax.axis_size("head")
    return lax.all_to_all(
        jnp.concatenate([v] * count, axis=0), "head", split_axis=0, concat_axis=0, tiled=True
    )


def gather_head_by_turns(v):
    count, me = lax.axis_size("head"), lax.axis_index("head")
    parts = [v] + [
        lax.ppermute(v, "head", [(i, (i - k) % count) for i in range(count)])
        for k in range(1, count)
    ]
    return parts


def in_order(parts):
    count, me = lax.axis_size("head"), lax.axis_index("head")
    both = jnp.concatenate(list(parts) * 2, axis=0)
    size = parts[0].shape[0]
    return lax.dynamic_slice_in_dim(both, (count - me) * size, count * size, axis=0)


def gather_core(mine, later):
    core = lax.rem(lax.axis_index("seq"), 2)
    got = trade(half_rows(mine, 1 - core), "seq", 1)
    part = jnp.concatenate([half_rows(mine, core), got], axis=0)
    got, *later = tie(trade_near(part, True), *later)
    part = jnp.concatenate([part, got], axis=0)
    got = trade_near(part, False)
    return [part, got, trade(part, "seq", 1), trade(got, "seq", 1)], later


def add(a, b):
    return (a.astype(F32) + b.astype(F32)).astype(BF)


def fold(kept, got):
    size = kept.shape[0] // 2
    sent = add(kept[size:], got[size:])
    return add(kept[:size], got[:size]), sent


def whole_small(small):
    return small[..., :8, :].astype(F32) + small[..., 8:, :].astype(F32)


def add_small(a, b):
    total = whole_small(a) + whole_small(b)
    high = lax.reduce_precision(total, exponent_bits=8, mantissa_bits=7)
    return jnp.concatenate([high, total - high], axis=0).astype(BF)


def join_cores(kept, got):
    core = lax.rem(lax.axis_index("seq"), 2)
    first, second = jnp.where(core == 0, kept, got), jnp.where(core == 0, got, kept)
    return jnp.concatenate([first, second], axis=0)


def scatter_head_by_turns(part):
    count, me = lax.axis_size("head"), lax.axis_index("head")
    size = part.shape[0] // count
    total = lax.dynamic_slice_in_dim(part, me * size, size, axis=0).astype(F32)
    for k in range(1, count):
        away = lax.dynamic_slice_in_dim(part, lax.rem(me + k, count) * size, size, axis=0)
        got = lax.ppermute(away, "head", [(i, (i + k) % count) for i in range(count)])
        total = total + got.astype(F32)
    return total


def tail(kept, sent, other, other_got, work, rest, trade_rest, last):
    part, sent = fold(kept, trade(sent, "seq", 1))
    d_normed, from_next, small = work(sent)
    other = scatter_head_by_turns(join_cores(other, other_got))
    for near in (False, True):
        size = sent.shape[0]
        got = trade_near(jnp.concatenate([sent, small], axis=0), near)
        if not near:
            got, grad = tie(got, rest(d_normed, from_next))
        small = add_small(small, got[size:])
        part, sent = fold(part, got[:size])
    size = sent.shape[0]
    got = trade(jnp.concatenate([sent, small], axis=0), "seq", 1)
    small = add_small(small, got[size:])
    part = join_cores(part, got[:size])
    part, small, grad, mixed = tie(part, small, trade_rest(grad), last())
    got = lax.all_to_all(part, "head", split_axis=0, concat_axis=0, tiled=True)
    turns = in_order(gather_head_by_turns(small))
    small = jnp.sum(whole_small(turns.reshape((-1,) + small.shape)), axis=0)
    got = got.reshape(lax.axis_size("head"), -1, WIDE).astype(F32)
    return jnp.sum(got, axis=0), other, small, grad, mixed


def per_block(
    body, ins, outs, scratch=(), loose=(), loose_outs=0, reverse=False, micros=1, name=None
):
    blocks = next(v.shape[0] for v in ins if v.ndim == 3)
    free = pl.BlockSpec(memory_space=pl.ANY)

    def spec(shape):
        if len(shape) == 1:
            return pl.BlockSpec(memory_space=pltpu.SMEM)
        if len(shape) == 2:
            return pl.BlockSpec(shape, lambda s: (0, 0))
        return pl.BlockSpec(
            (None,) + tuple(shape[1:]), lambda s: (blocks - 1 - s if reverse else s, 0, 0)
        )

    return pl.pallas_call(
        body,
        grid=(blocks,),
        in_specs=[spec(v.shape) for v in ins] + [free] * len(loose),
        out_specs=[spec(shape) for shape, _ in outs[: len(outs) - loose_outs]]
        + [free] * loose_outs,
        out_shape=[jax.ShapeDtypeStruct(shape, kind) for shape, kind in outs],
        scratch_shapes=list(scratch),
        compiler_params=PARAMS,
        cost_estimate=cost(micros),
        name=name,
    )(*ins, *loose)


def send_states(part, groups, spans):
    sent = lax.all_to_all(
        part, BOTH, split_axis=0, concat_axis=0, tiled=True, axis_index_groups=groups
    )
    return sent.reshape(spans, N // spans, STATE)


def return_states(sent, groups, spans, reverse, later=()):
    rows = N // spans
    width, kind = (DI, BF) if reverse else (STATE, F32)
    if rows % 8 == 0:
        out = pl.pallas_call(
            partial(state_scan, reverse, spans, rows),
            out_shape=jax.ShapeDtypeStruct((spans, rows, width), kind),
            scratch_shapes=[pltpu.VMEM((spans, rows, DI), F32)],
            compiler_params=PARAMS,
            cost_estimate=cost(2),
            name="state_scan",
        )(sent)
    else:
        last = sent[:, :, DI:].astype(F32)
        last = last[..., :H] + last[..., 32 : 32 + H] + last[..., 64 : 64 + H]
        decay = jnp.repeat(jnp.exp(last), P_SIZE, axis=-1)

        def move(carry, at):
            return at[0] * carry + at[1], carry

        _, out = lax.scan(
            move,
            jnp.zeros((rows, DI), F32),
            (decay, sent[:, :, :DI].astype(F32)),
            reverse=reverse,
        )
        if reverse:
            out = out.astype(BF)
        else:
            top = jnp.max(jnp.abs(out), axis=-1, keepdims=True)
            power = jnp.ceil(jnp.log2(jnp.maximum(top, 1e-30)))
            out = jnp.concatenate(
                [out * jnp.exp2(-power), jnp.broadcast_to(power, out.shape[:-1] + (128,))], axis=-1
            )
    if not reverse:
        out = out.astype(jnp.float16)
    out, later = tie(out, later)
    back = lax.all_to_all(
        out.reshape(N, width), BOTH, split_axis=0, concat_axis=0, tiled=True,
        axis_index_groups=groups,
    )
    return back, later


def unscaled(v):
    v = v.astype(F32)
    return v[:, :DI] * jnp.exp2(v[:, DI : DI + 1])


def to_span(v):
    seqs, rows, width = v.shape
    if seqs == 2:
        mine = lax.rem(lax.axis_index("head"), 2)
        got = trade(lax.dynamic_index_in_dim(v, 1 - mine, keepdims=False), "head", 1)

        def join(got):
            keep = lax.dynamic_index_in_dim(v, mine, keepdims=False)
            first, second = jnp.where(mine == 0, keep, got), jnp.where(mine == 0, got, keep)
            return jnp.concatenate([first, second], axis=0).reshape(-1, CH, width)

        return got, join
    groups = [[i + j for j in range(seqs)] for i in range(0, lax.axis_size("head"), seqs)]
    v = lax.all_to_all(
        v, "head", split_axis=0, concat_axis=1, tiled=True, axis_index_groups=groups
    )
    return v, lambda got: got.reshape(-1, CH, width)


def from_span(v, seqs):
    rows = v.shape[0] // seqs
    if seqs == 2:
        mine = lax.rem(lax.axis_index("head"), 2)
        got = trade(half_rows(v, 1 - mine).astype(BF), "head", 1)

        def join(got):
            keep, got = half_rows(v, mine), got.astype(v.dtype)
            return jnp.stack([jnp.where(mine == 0, keep, got), jnp.where(mine == 0, got, keep)])

        return got, join
    groups = [[i + j for j in range(seqs)] for i in range(0, lax.axis_size("head"), seqs)]
    v = v.reshape(1, seqs * rows, v.shape[-1])
    got = lax.all_to_all(
        v, "head", split_axis=1, concat_axis=0, tiled=True, axis_index_groups=groups
    )
    return got, lambda got: got


def pad_lanes(v, width):
    return jnp.pad(v, [(0, 0)] * (v.ndim - 1) + [(0, width - v.shape[-1])])


def gather_rows(v):
    return lax.all_gather(lax.all_gather(v, "head", axis=0, tiled=True), "seq", axis=0, tiled=True)


def scatter_rows(v):
    part = lax.psum_scatter(v, "seq", scatter_dimension=0, tiled=True)
    part = lax.psum_scatter(part, "head", scatter_dimension=0, tiled=True)
    return lax.optimization_barrier(part).astype(F32)


def on_device(
    hidden,
    out_grad,
    norm_gain,
    input_projection_weight,
    conv_weight,
    conv_bias,
    step_bias,
    decay_log,
    skip_weight,
    gate_gain,
    output_projection_weight,
):
    devices = lax.axis_size("seq") * lax.axis_size("head")
    seqs = hidden.shape[0]
    spans = devices // seqs
    groups = [[d for d in range(devices) if d % seqs == r] for r in range(seqs)]
    onward = [(i, i + seqs) for i in range(devices - seqs)]
    backward = [(i + seqs, i) for i in range(devices - seqs)]
    tokens = seqs * hidden.shape[1]
    blocks = tokens // CH

    def tails_before(v):
        if seqs != 2:
            return None
        odd = [d for d in range(devices) if d % 2]
        got = [
            lax.ppermute(
                v[s : s + 1, v.shape[1] - HALO :],
                BOTH,
                [(d, d + 1 + s) for d in odd if d + 1 + s < devices],
            )
            for s in range(2)
        ]
        return got[0] + got[1]

    def with_halo(v, before):
        tails = v[:, CH - HALO :]
        if before is None:
            before = lax.ppermute(tails[-1:], BOTH, onward)
        return jnp.concatenate([before, tails[:-1]], axis=0)

    fast = paired()
    me = lax.axis_index("seq").astype(jnp.int32)[None]
    scan_part = pad_lanes(input_projection_weight[:, DI:], WIDE)
    other_part = jnp.concatenate([input_projection_weight[:, :DI], output_projection_weight], 1)
    before = tails_before(hidden)
    hidden, join_hidden = to_span(hidden)
    if fast:
        pieces, (hidden, other_part) = gather_core(
            gather_head(scan_part), (hidden, other_part)
        )
        conv_bias, *turns = tie(conv_bias, *gather_head_by_turns(other_part))
        other_mine = in_order(turns)
        w_gate, w_out = other_mine[:, :DI], other_mine[:, DI:]
        gate_got, out_got = trade(w_gate, "seq", 2), trade(w_out, "seq", 4)
    else:
        pieces = [gather_rows(scan_part)]
        others = gather_rows(other_part)
        w_gate, w_out = others[:, :DI], others[:, DI:]
    hidden = join_hidden(hidden)
    halo = with_halo(hidden, before)
    out_grad, join_out_grad = to_span(out_grad)
    copies = 16 if fast else 1
    sides = 2 if fast else 1

    gain_one = norm_gain[None]
    gain_two = gate_gain[None]
    taps = jnp.pad(conv_weight, ((0, 4), (0, 0)))
    offset = conv_bias[None]
    bias = pad_lanes(step_bias[None], 128)
    rate = pad_lanes(-jnp.exp(decay_log)[None], 128)
    skip = jnp.repeat(skip_weight, P_SIZE)[None]

    (
        normed, normed_halo, ext, slope, conv, cum, cumt, step, stept, arg, local, part, w_scan,
    ) = per_block(
        partial(before_scan, len(pieces)),
        [me, hidden, halo, gain_one, taps, offset, bias, rate],
        [
            ((blocks, CH, D), BF),
            ((blocks, HALO, D), BF),
            ((blocks, HALO + CH, CONV), BF),
            ((blocks, CH, CONV), BF),
            ((blocks, CH, CONV), BF),
            ((blocks, CH, 128), F32),
            ((blocks, 32, CH), F32),
            ((blocks, CH, 128), F32),
            ((blocks, 32, CH), F32),
            ((blocks, CH, 128), F32),
            ((blocks, N, DI), BF),
            ((N, STATE), BF),
            ((D, WIDE), BF),
        ],
        [
            pltpu.VMEM((HALO + CH, CONV), F32),
            pltpu.VMEM((D, WIDE), BF),
            pltpu.VMEM((N, DI), F32),
            pltpu.VMEM((8, 128), F32),
            pltpu.SemaphoreType.DMA((copies,)),
            pltpu.SemaphoreType.DMA,
        ],
        loose=pieces,
        loose_outs=1,
        micros=12, name="before_scan",
    )
    if fast:
        cumt, gate_got, out_got = tie(cumt, gate_got, out_got)
        w_gate = jnp.concatenate([w_gate, gate_got], axis=0)
        w_out = jnp.concatenate([w_out, out_got], axis=0)
        ways = (trade(w_gate, "seq", 4), trade(w_out, "seq", 2))
        ways += (trade(w_gate, "seq", 1), trade(w_out, "seq", 1))
    else:
        ways = ()
    (within,) = per_block(
        within_block, [conv, cum, cumt, stept], [((blocks, CH, DI), F32)],
        micros=5, name="within_block",
    )
    sent, within, out_grad, ways = tie(send_states(part, groups, spans), within, out_grad, ways)
    incoming, ways = return_states(sent, groups, spans, False, ways)
    if fast:
        gates = [w_gate, ways[0], ways[2], trade(ways[0], "seq", 1)]
        outs = [w_out, ways[1], ways[3], trade(ways[1], "seq", 1)]
    else:
        gates, outs = [w_gate], [w_out]
    normed_rows = normed.reshape(tokens, D)
    out_grad = join_out_grad(out_grad)
    cotangent = out_grad.reshape(tokens, D)
    gate, d_mixed_in, w_gate, w_out = pl.pallas_call(
        partial(through_others, len(gates)),
        grid=(4,),
        in_specs=[
            pl.BlockSpec(memory_space=pltpu.SMEM),
            pl.BlockSpec((tokens, D), lambda j: (0, 0)),
            pl.BlockSpec((tokens, D), lambda j: (0, 0)),
        ]
        + [pl.BlockSpec(memory_space=pl.ANY)] * (2 * len(gates)),
        out_specs=[
            pl.BlockSpec((tokens, DI // 2), lambda j: (0, jnp.minimum(j, 1))),
            pl.BlockSpec((tokens, DI // 2), lambda j: (0, jnp.maximum(j - 2, 0))),
            pl.BlockSpec(memory_space=pl.ANY),
            pl.BlockSpec(memory_space=pl.ANY),
        ],
        out_shape=[jax.ShapeDtypeStruct((tokens, DI), F32)] * 2
        + [jax.ShapeDtypeStruct((D, DI), BF)] * 2,
        scratch_shapes=[
            pltpu.VMEM((D, DI), BF),
            pltpu.VMEM((D, DI), BF),
            pltpu.SemaphoreType.DMA((2, 8 if fast else 1)),
            pltpu.SemaphoreType.DMA((2,)),
        ],
        compiler_params=PARAMS,
        cost_estimate=cost(8),
        name="through_others",
    )(me, normed_rows, cotangent, *gates, *outs)
    gate, d_mixed_in = gate.reshape(blocks, CH, DI), d_mixed_in.reshape(blocks, CH, DI)

    gate, incoming = tie(gate, incoming)
    incoming = unscaled(incoming)
    mixed_in, d_gate, d_y, dot_y, starts, local_back, part, row_sums = per_block(
        around_norm,
        [within, conv, cum, local, incoming, gate, d_mixed_in, gain_two, skip],
        [
            ((blocks, CH, DI), BF),
            ((blocks, CH, DI), BF),
            ((blocks, CH, DI), BF),
            ((blocks, CH, 128), F32),
            ((blocks, N, DI), F32),
            ((blocks, N, DI), BF),
            ((N, STATE), BF),
            ((8, CONV), F32),
        ],
        [pltpu.VMEM((N, DI), F32), pltpu.VMEM((N, DI), F32), pltpu.VMEM((8, 128), F32)],
        micros=13, name="around_norm",
    )

    mixed_rows = mixed_in.reshape(tokens, DI)
    d_gate_rows = d_gate.reshape(tokens, DI)
    other_terms = pl.pallas_call(
        other_weight_grad,
        grid=(4,),
        in_specs=[
            pl.BlockSpec(memory_space=pltpu.SMEM),
            pl.BlockSpec((tokens, D), lambda j: (0, 0)),
            pl.BlockSpec((tokens, DI // 2), lambda j: (0, jnp.minimum(j, 1))),
            pl.BlockSpec((tokens, D), lambda j: (0, 0)),
            pl.BlockSpec((tokens, DI // 2), lambda j: (0, jnp.maximum(j - 2, 0))),
        ],
        out_specs=[pl.BlockSpec(memory_space=pl.ANY)] * sides,
        out_shape=[jax.ShapeDtypeStruct((D // sides, 2 * DI), BF)] * sides,
        scratch_shapes=[pltpu.VMEM((D, 2 * DI), BF), pltpu.SemaphoreType.DMA((copies,))],
        compiler_params=PARAMS,
        cost_estimate=cost(8),
        name="other_weight_grad",
    )(me, normed_rows, d_gate_rows, cotangent, mixed_rows)
    branch = dot(mixed_rows, w_out, (1, 1))
    mixed = (hidden.reshape(tokens, D).astype(F32) + branch).astype(BF)
    sent, other_terms, mixed, d_y = tie(
        send_states(part, groups, spans), other_terms, mixed, d_y
    )
    incoming, _ = return_states(sent, groups, spans, True)
    if fast:
        other, other_sent = fold(other_terms[0], trade(other_terms[1], "seq", 1))
    else:
        other = other_terms[0]

    dx_within, d_keys, d_queries = per_block(
        within_block_back,
        [conv, cum, cumt, step, d_y, starts],
        [((blocks, CH, DI), F32), ((blocks, CH, N), F32), ((blocks, CH, N), F32)],
        [pltpu.VMEM((CH, CH), F32)],
        micros=9, name="within_block_back",
    )
    if fast:
        got = trade_near(other_sent, False)
    d_scan, d_halo, conv_sums = per_block(
        after_scan,
        [
            conv, slope, ext, cum, step, arg, d_y, dx_within, d_keys, d_queries, dot_y, starts,
            local_back, incoming, skip, rate, taps,
        ],
        [
            ((blocks, CH, WIDE), BF),
            ((blocks, HALO, WIDE), BF),
            ((8, CONV), F32),
        ],
        [
            pltpu.VMEM((HALO + CH + 8, CONV), F32),
            pltpu.VMEM((N, DI), F32),
        ],
        reverse=True,
        micros=16, name="after_scan",
    )

    if fast:
        d_scan, got = tie(d_scan, got)
        other, other_sent = fold(other, got)
        other, other_sent = fold(other, trade_near(other_sent, True))
        other_got = trade(other_sent, "seq", 1)
    mixed, join_mixed = from_span(mixed, seqs)
    mixed, d_scan = tie(mixed, d_scan)
    if not fast:
        mixed = join_mixed(mixed)
    terms = pl.pallas_call(
        partial(scan_weight_grad, sides),
        in_specs=[pl.BlockSpec(memory_space=pltpu.SMEM)]
        + [pl.BlockSpec(memory_space=pltpu.VMEM)] * 4,
        out_specs=[pl.BlockSpec(memory_space=pl.ANY)] * sides,
        out_shape=[jax.ShapeDtypeStruct((D // sides, WIDE), BF)] * sides,
        scratch_shapes=[pltpu.VMEM((D, WIDE), BF), pltpu.SemaphoreType.DMA((2, copies))],
        compiler_params=PARAMS,
        cost_estimate=cost(6),
        name="scan_weight_grad",
    )(
        me,
        normed_rows,
        normed_halo.reshape(blocks * HALO, D),
        d_scan.reshape(tokens, WIDE),
        d_halo.reshape(blocks * HALO, WIDE),
    )

    def to_normed(go):
        d_scan_now = tie(d_scan, go)[0]
        d_normed, d_normed_halo, small = per_block(
            back_to_normed,
            [
                hidden, halo, d_gate, d_scan_now, d_halo, w_gate, w_scan, row_sums, conv_sums,
            ],
            [((blocks, CH, D), F32), ((blocks, 8, D), F32), ((16, WIDE), BF)],
            [pltpu.VMEM((8, CONV), F32)],
            micros=7, name="back_to_normed",
        )
        from_next = lax.ppermute(d_normed_halo[:1], BOTH, backward)
        return d_normed, jnp.concatenate([d_normed_halo[1:], from_next], axis=0), small

    def to_hidden(d_normed, from_next):
        return per_block(
            finish,
            [hidden, out_grad, d_normed, from_next, gain_one],
            [((blocks, CH, D), F32)],
            micros=3, name="finish",
        )[0].reshape(tokens, D)

    def grad_back(grad):
        got, join = from_span(grad, seqs)
        return join(got)

    if fast:
        scan_rows, other_rows, small, hidden_grad, mixed = tail(
            *terms, other, other_got, to_normed, to_hidden, grad_back, lambda: join_mixed(mixed)
        )
    else:
        d_normed, from_next, small = to_normed(jnp.zeros((8, 128), F32))
        other_rows = scatter_rows(other)
        scan_rows = scatter_rows(terms[0])
        small = lax.psum(whole_small(small), BOTH)
        hidden_grad = grad_back(to_hidden(d_normed, from_next))
    small = small[:, :CONV]
    in_rows = jnp.concatenate([other_rows[:, :DI], scan_rows[:, : CONV + H]], axis=1)
    return (
        mixed,
        hidden_grad,
        small[7, :D],
        in_rows,
        small[:KERNEL],
        small[4],
        small[5, DI : DI + H],
        small[5, DI + 128 : DI + 128 + H],
        small[6, :H],
        small[5, :DI],
        other_rows[:, DI:],
    )


def solution(mesh):
    rows = P(None, BOTH, None)
    weight = P(BOTH, None)
    return jax.shard_map(
        on_device,
        mesh=mesh,
        in_specs=(rows, rows, P(), weight, P(), P(), P(), P(), P(), P(), weight),
        out_specs=(rows, rows, P(), weight, P(), P(), P(), P(), P(), P(), weight),
        check_vma=False,
    )
```
